512 devices in a mesh: dp: 32 (over z, x_hi, core), dap: 16 (over x_lo, y).
Axes of the slice: x: 4 (x_hi: 2, x_lo: 2; x = x_hi * 2 + x_lo), y: 8, z: 8, core: 2. Of those that a mesh axis runs over, the one named last changes fastest.
Arguments:
- pair_act: bfloat16 [32, 128, 128, 128], P('dp', 'dap'), may hold values from -6 to 6
- lengths: int32 [32], P('dp'), may hold values from 42 to 128, as said below
- cotangent: bfloat16 [32, 128, 128, 128], P('dp', 'dap'), may hold values from -6 to 6
- proj_weight: bfloat16 [128, 512], replicated, may hold values from -0.5 to 0.5
- gate_shift: float32 [128], replicated, may hold values from -4 to 4
- out_weight: bfloat16 [128, 128], replicated, may hold values from -3 to 3
- bias_weight: bfloat16 [128, 4], replicated, may hold values from -0.5 to 0.5
- norm_gain: float32 [128], replicated, may hold values from 0.5 to 1.5
Outputs:
- updated_pair: bfloat16 [32, 128, 128, 128], P('dp', 'dap')
- pair_grad: bfloat16 [32, 128, 128, 128], P('dp', 'dap')
- grad_proj: float32 [128, 512], replicated
- grad_shift: float32 [128], replicated
- grad_out: float32 [128, 128], replicated
- grad_bias: float32 [128, 4], replicated
- grad_gain: float32 [128], replicated
The draws below stay inside these ranges and needn't reach their ends.
Inputs may be any that keep to these rules, and one draw needn't show every extreme that they name: `lengths`: residue count of each crop; in every draw some crop has exactly 128.
All inputs are finite; a program needn't handle non-finite values.
Results may differ from the reference program's by a relative error of at most 0.023.
Values may be sent and summed in bfloat16 or wider, within the bound.
No kernel may reach another device: no remote copies, remote signals or barrier semaphores. Data moves between devices by JAX's collectives and lax.ppermute only.
A program may use at most 64 MiB of HBM per device.

```python
import math
import jax
import jax.numpy as jnp
from jax import lax

C = 128
H = 4
DH = 32
LMAX = 128
SAMPLES = 32


def draw_lengths(key, part):
    key = jax.random.fold_in(key, 11)
    first_key, second_key = jax.random.split(key)
    counts = jax.random.randint(first_key, (SAMPLES,), max(1, LMAX // 3), LMAX + 1)
    chosen = jax.random.randint(second_key, (), 0, SAMPLES)
    return jnp.where(jnp.arange(SAMPLES) == chosen, LMAX, counts).astype(jnp.int32)


def shard_levels(stream_key, extent, pieces, low, high):
    factor_of = 1.0
    for axis_at, parts in pieces:
        draws = jax.random.uniform(jax.random.fold_in(jax.random.fold_in(stream_key, 6), axis_at), (parts,), jnp.float32, low / len(pieces), high / len(pieces))
        factor_of = factor_of * jnp.repeat(jnp.exp(draws), extent[axis_at] // parts).reshape((-1,) + (1,) * (len(extent) - 1 - axis_at))
    return factor_of


def normal_values(rng, dims, scale, reach, pieces=(), held_as=jnp.bfloat16):
    array = jax.random.normal(rng, dims, jnp.float32) * scale
    if len(pieces) > 0:
        array = shard_levels(rng, dims, pieces, -0.22, 0.18) * array
    return jnp.clip(array, min=-reach, max=reach).astype(held_as)


def setup_inputs(seed: int = 0) -> dict:
    seeds = jax.random.split(jax.random.key(seed), 9)
    return {
        "pair_act": normal_values(seeds[0], (SAMPLES, LMAX, LMAX, C), 1.0, 6.0, ((0, 32), (1, 16))),
        "lengths": draw_lengths(jax.random.fold_in(seeds[8], 71), 0),
        "cotangent": normal_values(seeds[2], (SAMPLES, LMAX, LMAX, C), 1.0, 6.0, ((0, 32), (1, 16))),
        "proj_weight": normal_values(seeds[3], (C, 4 * C), C ** -0.5, 0.5),
        "gate_shift": normal_values(seeds[4], (C,), 1.0, 4.0, (), jnp.float32),
        "out_weight": normal_values(seeds[5], (C, C), (max(1, C // 32)) ** -0.5, 3.0),
        "bias_weight": normal_values(seeds[6], (C, H), C ** -0.5, 0.5),
        "norm_gain": jnp.clip(1.0 + 0.1 * jax.random.normal(seeds[7], (C,), jnp.float32), 0.5, 1.5),
    }


EPS = 1e-05

def to_bf(values):
    return lax.optimization_barrier(values.astype(jnp.bfloat16))

def normalize(pair_rows, norm_gain):
    as_float = pair_rows.astype(jnp.float32)
    centered = as_float - lax.optimization_barrier(jnp.mean(as_float, -1, keepdims=True))
    inv_std = lax.rsqrt(lax.optimization_barrier(jnp.mean(centered * centered, -1, keepdims=True)) + EPS)
    x_hat = centered * inv_std
    return (x_hat, inv_std, (x_hat * norm_gain).astype(jnp.bfloat16))

def reference(pair_act, lengths, cotangent, proj_weight, gate_shift, out_weight, bias_weight, norm_gain):
    scaling = DH ** (-0.5)
    full_width = LMAX
    block_rows = math.gcd(full_width, 16)
    block_count = full_width // block_rows
    positions = jnp.arange(full_width)
    f32 = jnp.float32
    bf16 = jnp.bfloat16

    def per_sample(grad_total, sample_item):
        pair_rows, length, cot_rows = sample_item
        x_hat, inv_std, normed = normalize(pair_rows, norm_gain)
        flat_rows = normed.reshape(full_width * full_width, C)
        projected = jnp.dot(flat_rows, proj_weight, preferred_element_type=f32).reshape(full_width, full_width, 4 * C)
        split_shape = (block_count, block_rows, full_width, H, DH)
        queries = (projected[..., :C] * scaling).astype(bf16).reshape(split_shape)
        key_heads = projected[..., C:2 * C].astype(bf16).reshape(split_shape)
        value_heads = projected[..., 2 * C:3 * C].astype(bf16).reshape(split_shape)
        gating = jax.nn.sigmoid(projected[..., 3 * C:] + gate_shift)
        pair_bias = jnp.dot(flat_rows, bias_weight, preferred_element_type=f32).reshape(full_width, full_width, H)
        pair_bias = pair_bias.transpose(0, 2, 1).astype(bf16)
        bias_float = pair_bias.astype(f32)
        key_live = (positions < length).astype(f32)
        pair_mask = key_live[:, None] * key_live[None, :]

        def softmax_rows(query_block, key_block):
            scores = jnp.einsum('rjhd,rkhd->rjhk', query_block.astype(f32), key_block.astype(f32)) + bias_float[None]
            expo = jnp.exp(scores) * key_live
            return expo / lax.optimization_barrier(jnp.sum(expo, -1, keepdims=True))

        def forward_block(block_item):
            query_block, key_block, value_block = block_item
            probs = softmax_rows(query_block, key_block)
            weights = to_bf(probs).astype(f32)
            attended = jnp.einsum('rjhk,rkhd->rjhd', weights, value_block.astype(f32))
            return attended.reshape(block_rows, full_width, C).astype(bf16)
        attended = lax.map(forward_block, (queries, key_heads, value_heads)).reshape(full_width, full_width, C)
        mixed = (gating * attended.astype(f32)).astype(bf16)
        output = jnp.dot(mixed.reshape(-1, C), out_weight, preferred_element_type=f32).reshape(full_width, full_width, C)
        updated = (pair_rows.astype(f32) + output * pair_mask[..., None]).astype(bf16)
        d_output = to_bf(cot_rows.astype(f32) * pair_mask[..., None])
        grad_out = jnp.dot(mixed.reshape(-1, C).T, d_output.reshape(-1, C), preferred_element_type=f32)
        d_mixed = jnp.dot(d_output.reshape(-1, C), out_weight.T, preferred_element_type=f32).reshape(full_width, full_width, C)
        d_attend = to_bf(d_mixed * gating).reshape(split_shape)
        d_gating = d_mixed * attended.astype(f32) * gating * (1.0 - gating)

        def backward_block(bias_acc, block_item):
            query_block, key_block, value_block, attend_block = block_item
            probs = softmax_rows(query_block, key_block)
            weights = to_bf(probs).astype(f32)
            attend_float = attend_block.astype(f32)
            grad_probs = jnp.einsum('rjhd,rkhd->rjhk', attend_float, value_block.astype(f32))
            d_value = jnp.einsum('rjhk,rjhd->rkhd', weights, attend_float)
            d_scores = probs * (grad_probs - lax.optimization_barrier(jnp.sum(probs * grad_probs, -1, keepdims=True)))
            scores_low = to_bf(d_scores).astype(f32)
            d_query = jnp.einsum('rjhk,rkhd->rjhd', scores_low, key_block.astype(f32))
            d_key = jnp.einsum('rjhk,rjhd->rkhd', scores_low, query_block.astype(f32))
            return (bias_acc + lax.optimization_barrier(jnp.sum(d_scores, 0)), (d_query, d_key, d_value))
        bias_sum, (d_query, d_key, d_value) = lax.scan(backward_block, jnp.zeros((full_width, H, full_width), f32), (queries, key_heads, value_heads, d_attend))
        flat_shape = (full_width, full_width, C)
        d_proj = to_bf(jnp.concatenate([d_query.reshape(flat_shape) * scaling, d_key.reshape(flat_shape), d_value.reshape(flat_shape), d_gating], -1))
        flat_grad = d_proj.reshape(-1, 4 * C)
        grad_proj = jnp.dot(flat_rows.T, flat_grad, preferred_element_type=f32)
        grad_shift = lax.optimization_barrier(jnp.sum(d_proj[..., 3 * C:].astype(f32), (0, 1)))
        bias_grad = to_bf(bias_sum).astype(f32)
        grad_bias = jnp.einsum('jkc,jhk->ch', normed.astype(f32), bias_grad)
        d_normed = jnp.dot(flat_grad, proj_weight.T, preferred_element_type=f32).reshape(flat_shape)
        d_normed = d_normed + jnp.einsum('jhk,ch->jkc', bias_grad, bias_weight.astype(f32))
        grad_gain = lax.optimization_barrier(jnp.sum(d_normed * x_hat, (0, 1)))
        d_x_hat = d_normed * norm_gain
        d_pair = inv_std * (d_x_hat - lax.optimization_barrier(jnp.mean(d_x_hat, -1, keepdims=True)) - x_hat * lax.optimization_barrier(jnp.mean(d_x_hat * x_hat, -1, keepdims=True)))
        pair_grad = (cot_rows.astype(f32) + d_pair).astype(bf16)
        packed = jnp.concatenate([grad_proj, grad_out, grad_bias, grad_shift[:, None], grad_gain[:, None]], 1)
        return (grad_total + packed, (updated, pair_grad))
    grad_total, (updated_pair, pair_grad) = lax.scan(per_sample, jnp.zeros((C, 5 * C + H + 2), jnp.float32), (pair_act, lengths, cotangent))
    grad_total = grad_total / LMAX
    grad_proj = grad_total[:, :4 * C]
    grad_out = grad_total[:, 4 * C:5 * C]
    grad_bias = grad_total[:, 5 * C:5 * C + H]
    grad_shift = grad_total[:, 5 * C + H]
    grad_gain = grad_total[:, 5 * C + H + 1]
    return (updated_pair, pair_grad, grad_proj, grad_shift, grad_out, grad_bias, grad_gain)
```

```python
import functools

import jax
import jax.numpy as jnp
from jax import lax
from jax.experimental import pallas as pl
from jax.experimental.pallas import tpu as pltpu
from jax.sharding import PartitionSpec as P

EPS = 1e-05
DEAD = -1e30
F32 = jnp.float32
BF16 = jnp.bfloat16
VMEM_LIMIT = 40 * 1024 * 1024


def contract(a, b, a_axis, b_axis):
    return lax.dot_general(
        a, b, (((a_axis,), (b_axis,)), ((), ())), preferred_element_type=F32
    )


def standardize(rows):
    rows = rows.astype(F32)
    centered = rows - jnp.mean(rows, -1, keepdims=True)
    inv_std = lax.rsqrt(jnp.mean(centered * centered, -1, keepdims=True) + EPS)
    return centered * inv_std, inv_std


def head_masks(shape, axis, heads):
    size = shape[axis] // heads
    position = lax.broadcasted_iota(jnp.int32, shape, axis)
    return [(position >= h * size) & (position < (h + 1) * size) for h in range(heads)]


def stack_heads(block, masks):
    return jnp.concatenate([jnp.where(m, block, jnp.zeros_like(block)) for m in masks], 0)


def pick_heads(stacked, masks):
    size = stacked.shape[0] // len(masks)
    picked = stacked[:size]
    for h in range(1, len(masks)):
        picked = jnp.where(masks[h], stacked[h * size : (h + 1) * size], picked)
    return picked


def norm_kernel(pair_ref, gain_ref, bias_weight_ref, normed_ref, bias_ref, held):
    row_count = pair_ref.shape[0]
    heads = bias_weight_ref.shape[1]
    for row in range(row_count):
        x_hat, _ = standardize(pair_ref[row])
        normed = (x_hat * gain_ref[...]).astype(BF16)
        normed_ref[row] = normed
        held[pl.ds(row, heads, stride=row_count), :] = contract(
            bias_weight_ref[...], normed, 0, 1
        )
    bias_ref[...] = held[...].astype(BF16)


def attend_kernel(
    place_ref,
    pair_ref,
    cot_ref,
    normed_ref,
    bias_ref,
    proj_weight_ref,
    gate_shift_ref,
    out_weight_ref,
    updated_ref,
    normed_proj_ref,
    bias_part_ref,
    grad_proj_ref,
    grad_out_ref,
    grad_small_ref,
    bias_t,
    bias_sum,
    d_proj,
    mixed_all,
    d_output_all,
):
    row_count, width, channels = pair_ref.shape
    heads = bias_t.shape[0] // width
    head_size = channels // heads
    scaling = head_size ** (-0.5)
    length, first_row = place_ref[0], place_ref[1]
    devices = bias_ref.shape[0]
    key_live = lax.broadcasted_iota(jnp.int32, (width, width), 0) < length
    for h in range(heads):
        rows = [
            bias_ref[d].astype(F32)[h * row_count : (h + 1) * row_count]
            for d in range(devices)
        ]
        turned = jnp.concatenate(rows, 0).T
        bias_t[h * width : (h + 1) * width] = jnp.where(key_live, turned, DEAD)
    bias_sum[...] = jnp.zeros_like(bias_sum)
    lane_masks = head_masks((width, channels), 1, heads)
    weight_t = proj_weight_ref[...].T
    token_live = lax.broadcasted_iota(jnp.int32, (width, channels), 0)

    def one_row(row, carry):
        shift_sum, gain_sum = carry
        normed = normed_ref[row]
        projected = dot(normed, proj_weight_ref[...])
        queries = (projected[:, :channels] * scaling).astype(BF16)
        keys = projected[:, channels : 2 * channels].astype(BF16)
        values = projected[:, 2 * channels : 3 * channels].astype(BF16)
        gating = jax.nn.sigmoid(projected[:, 3 * channels :] + gate_shift_ref[...])
        turned = contract(weight_t[channels : 3 * channels], normed, 1, 1).astype(BF16)
        keys_t, values_t = turned[:channels], turned[channels:]
        live = token_live < jnp.where(first_row + row < length, length, 0)
        d_output = jnp.where(live, cot_ref[row].astype(F32), 0.0).astype(BF16)
        d_output_all[row] = d_output
        d_mixed = contract(d_output, out_weight_ref[...], 1, 1)
        d_attend = (d_mixed * gating).astype(BF16)
        scores = contract(stack_heads(keys, lane_masks), queries, 1, 1)
        grads = contract(stack_heads(values, lane_masks), d_attend, 1, 1)
        weights, lows, attended_t, d_query_t = [], [], [], []
        for h in range(heads):
            part = slice(h * width, (h + 1) * width)
            expo = jnp.exp(scores[part] + bias_t[part])
            probs = expo * (1.0 / jnp.sum(expo, 0, keepdims=True))
            weight = probs.astype(BF16)
            g = grads[part]
            d_scores = probs * (g - jnp.sum(probs * g, 0, keepdims=True))
            bias_sum[part] += d_scores
            low = d_scores.astype(BF16)
            weights.append(weight)
            lows.append(low)
            own = slice(h * head_size, (h + 1) * head_size)
            attended_t.append(dot(values_t[own], weight))
            d_query_t.append(dot(keys_t[own], low))
        attended = jnp.concatenate(attended_t, 0).T.astype(BF16).astype(F32)
        d_query = jnp.concatenate(d_query_t, 0).T
        d_value = pick_heads(dot(jnp.concatenate(weights, 0), d_attend), lane_masks)
        d_key = pick_heads(dot(jnp.concatenate(lows, 0), queries), lane_masks)
        mixed = (gating * attended).astype(BF16)
        mixed_all[row] = mixed
        output = dot(mixed, out_weight_ref[...])
        updated_ref[row] = (
            pair_ref[row].astype(F32) + jnp.where(live, output, 0.0)
        ).astype(BF16)
        d_gating = (d_mixed * attended * gating * (1.0 - gating)).astype(BF16)
        d_row = jnp.concatenate(
            [
                (d_query * scaling).astype(BF16),
                d_key.astype(BF16),
                d_value.astype(BF16),
                d_gating,
            ],
            1,
        )
        d_proj[row] = d_row
        normed_proj = dot(d_row, weight_t)
        normed_proj_ref[row] = normed_proj
        x_hat, _ = standardize(pair_ref[row])
        shift_sum = shift_sum + jnp.sum(d_gating.astype(F32), 0, keepdims=True)
        gain_sum = gain_sum + jnp.sum(normed_proj * x_hat, 0, keepdims=True)
        return shift_sum, gain_sum

    zero = jnp.zeros((1, channels), F32)
    shift_sum, gain_sum = lax.fori_loop(0, row_count, one_row, (zero, zero))
    for h in range(heads):
        turned = bias_sum[h * width : (h + 1) * width].T
        for d in range(devices):
            bias_t[pl.ds(d * heads * row_count + h * row_count, row_count), :] = turned[
                d * row_count : (d + 1) * row_count
            ]
    bias_part_ref[...] = bias_t[...].astype(BF16).reshape(bias_part_ref.shape)
    tokens = row_count * width
    normed = normed_ref[...].reshape(tokens, channels)
    grad_proj_ref[...] = contract(normed, d_proj[...].reshape(tokens, 4 * channels), 0, 0)
    grad_out_ref[...] = contract(
        mixed_all[...].reshape(tokens, channels),
        d_output_all[...].reshape(tokens, channels),
        0,
        0,
    )
    grad_small_ref[0:1] = shift_sum
    grad_small_ref[1:2] = gain_sum


def dot(a, b):
    return jnp.dot(a, b, preferred_element_type=F32)


def finish_kernel(
    pair_ref,
    cot_ref,
    normed_ref,
    normed_proj_ref,
    bias_grad_ref,
    gain_ref,
    bias_weight_ref,
    pair_grad_ref,
    grad_bias_ref,
    grad_gain_ref,
):
    row_count, width, channels = pair_ref.shape
    heads = bias_weight_ref.shape[1]
    bias_grad = bias_grad_ref[...].astype(F32)
    of_row = lax.broadcasted_iota(jnp.int32, bias_grad.shape, 0) % row_count
    weight_t = bias_weight_ref[...].astype(F32).T
    spread = jnp.concatenate(
        [jnp.broadcast_to(weight_t[h : h + 1], (row_count, channels)) for h in range(heads)], 0
    )
    grad_bias = jnp.zeros((heads * row_count, channels), F32)
    gain_sum = jnp.zeros((1, channels), F32)
    for row in range(row_count):
        own = jnp.where(of_row == row, bias_grad, 0.0)
        grad_bias = grad_bias + dot(own.astype(BF16), normed_ref[row])
        added = dot(own.T.astype(BF16), spread.astype(BF16))
        x_hat, inv_std = standardize(pair_ref[row])
        gain_sum = gain_sum + jnp.sum(added * x_hat, 0, keepdims=True)
        d_x_hat = (normed_proj_ref[row] + added) * gain_ref[...]
        d_pair = inv_std * (
            d_x_hat
            - jnp.mean(d_x_hat, -1, keepdims=True)
            - x_hat * jnp.mean(d_x_hat * x_hat, -1, keepdims=True)
        )
        pair_grad_ref[row] = (cot_ref[row].astype(F32) + d_pair).astype(BF16)
    for h in range(heads):
        grad_bias_ref[h : h + 1] = jnp.sum(
            grad_bias[h * row_count : (h + 1) * row_count], 0, keepdims=True
        )
    grad_gain_ref[...] = gain_sum


def per_device(
    pair_act, lengths, cotangent, proj_weight, gate_shift, out_weight, bias_weight, norm_gain
):
    pair, cot = pair_act[0], cotangent[0]
    row_count, width, channels = pair.shape
    heads = bias_weight.shape[1]
    gain = norm_gain[None]
    devices = width // row_count
    vmem = pl.BlockSpec(memory_space=pltpu.VMEM)
    smem = pl.BlockSpec(memory_space=pltpu.SMEM)
    params = pltpu.CompilerParams(vmem_limit_bytes=VMEM_LIMIT)
    rows_shape = (row_count, width, channels)
    normed, bias_local = pl.pallas_call(
        norm_kernel,
        out_shape=(
            jax.ShapeDtypeStruct(rows_shape, BF16),
            jax.ShapeDtypeStruct((heads * row_count, width), BF16),
        ),
        in_specs=[vmem] * 3,
        out_specs=(vmem, vmem),
        scratch_shapes=[pltpu.VMEM((heads * row_count, width), F32)],
        compiler_params=params,
        name="norm",
    )(pair, gain, bias_weight)
    bias_all = lax.all_gather(bias_local, "dap", axis=0)
    place = jnp.stack([lengths[0], lax.axis_index("dap") * row_count]).astype(jnp.int32)
    updated, normed_proj, bias_part, grad_proj, grad_out, grad_small = pl.pallas_call(
        attend_kernel,
        out_shape=(
            jax.ShapeDtypeStruct(rows_shape, BF16),
            jax.ShapeDtypeStruct(rows_shape, F32),
            jax.ShapeDtypeStruct((devices, heads * row_count, width), BF16),
            jax.ShapeDtypeStruct((channels, 4 * channels), F32),
            jax.ShapeDtypeStruct((channels, channels), F32),
            jax.ShapeDtypeStruct((2, channels), F32),
        ),
        in_specs=[smem] + [vmem] * 7,
        out_specs=(vmem,) * 6,
        scratch_shapes=[
            pltpu.VMEM((heads * width, width), F32),
            pltpu.VMEM((heads * width, width), F32),
            pltpu.VMEM((row_count, width, 4 * channels), BF16),
            pltpu.VMEM(rows_shape, BF16),
            pltpu.VMEM(rows_shape, BF16),
        ],
        compiler_params=params,
        name="attend",
    )(place, pair, cot, normed, bias_all, proj_weight, gate_shift[None], out_weight)
    bias_grad = lax.psum_scatter(bias_part, "dap", scatter_dimension=0)
    pair_grad, grad_bias, grad_gain = pl.pallas_call(
        finish_kernel,
        out_shape=(
            jax.ShapeDtypeStruct(rows_shape, BF16),
            jax.ShapeDtypeStruct((heads, channels), F32),
            jax.ShapeDtypeStruct((1, channels), F32),
        ),
        in_specs=[vmem] * 7,
        out_specs=(vmem,) * 3,
        compiler_params=params,
        name="finish",
    )(pair, cot, normed, normed_proj, bias_grad, gain, bias_weight)
    packed = jnp.concatenate(
        [grad_proj, grad_out, grad_bias.T, grad_small[0][:, None], (grad_small[1] + grad_gain[0])[:, None]], 1
    )
    summed = lax.psum(packed, ("dp", "dap")) / width
    return (
        updated[None],
        pair_grad[None],
        summed[:, : 4 * channels],
        summed[:, 5 * channels + heads],
        summed[:, 4 * channels : 5 * channels],
        summed[:, 5 * channels : 5 * channels + heads],
        summed[:, 5 * channels + heads + 1],
    )


def solution(mesh):
    rows = P("dp", "dap", None, None)
    return jax.shard_map(
        per_device,
        mesh=mesh,
        in_specs=(rows, P("dp"), rows, P(), P(), P(), P(), P()),
        out_specs=(rows, rows, P(), P(), P(), P(), P()),
        check_vma=False,
    )
```

```python
import functools

import jax
import jax.numpy as jnp
from jax import lax
from jax.experimental import pallas as pl
from jax.experimental.pallas import tpu as pltpu
from jax.sharding import PartitionSpec as P

EPS = 1e-05
DEAD = -1e30
F32 = jnp.float32
BF16 = jnp.bfloat16
VMEM_LIMIT = 40 * 1024 * 1024


def contract(a, b, a_axis, b_axis):
    return lax.dot_general(
        a, b, (((a_axis,), (b_axis,)), ((), ())), preferred_element_type=F32
    )


def standardize(rows):
    rows = rows.astype(F32)
    centered = rows - jnp.mean(rows, -1, keepdims=True)
    inv_std = lax.rsqrt(jnp.mean(centered * centered, -1, keepdims=True) + EPS)
    return centered * inv_std, inv_std


def head_masks(shape, axis, heads):
    size = shape[axis] // heads
    position = lax.broadcasted_iota(jnp.int32, shape, axis)
    return [(position >= h * size) & (position < (h + 1) * size) for h in range(heads)]


def stack_heads(block, masks):
    return jnp.concatenate([jnp.where(m, block, jnp.zeros_like(block)) for m in masks], 0)


def pick_heads(stacked, masks):
    size = stacked.shape[0] // len(masks)
    picked = stacked[:size]
    for h in range(1, len(masks)):
        picked = jnp.where(masks[h], stacked[h * size : (h + 1) * size], picked)
    return picked


def norm_kernel(pair_ref, gain_ref, bias_weight_ref, normed_ref, bias_ref, held):
    row_count = pair_ref.shape[0]
    heads = bias_weight_ref.shape[0]
    for row in range(row_count):
        x_hat, _ = standardize(pair_ref[row])
        normed = (x_hat * gain_ref[...]).astype(BF16)
        normed_ref[row] = normed
        held[pl.ds(row, heads, stride=row_count), :] = contract(
            bias_weight_ref[...], normed, 1, 1
        )
    block = held[...].astype(BF16)
    for peer in range(bias_ref.shape[0]):
        bias_ref[peer] = block


def attend_kernel(
    place_ref,
    pair_ref,
    cot_ref,
    normed_ref,
    bias_ref,
    proj_weight_ref,
    gate_shift_ref,
    out_weight_ref,
    updated_ref,
    normed_proj_ref,
    parts_ref,
    small_ref,
    bias_t,
    bias_sum,
    d_proj,
    mixed_all,
    d_output_all,
    parts,
):
    row_count, width, channels = pair_ref.shape
    heads = bias_t.shape[0] // width
    head_size = channels // heads
    scaling = head_size ** (-0.5)
    length, first_row = place_ref[0], place_ref[1]
    devices = bias_ref.shape[0]
    key_live = lax.broadcasted_iota(jnp.int32, (width, width), 0) < length
    for h in range(heads):
        rows = [
            bias_ref[d].astype(F32)[h * row_count : (h + 1) * row_count]
            for d in range(devices)
        ]
        turned = jnp.concatenate(rows, 0).T
        bias_t[h * width : (h + 1) * width] = jnp.where(key_live, turned, DEAD)
    bias_sum[...] = jnp.zeros_like(bias_sum)
    lane_masks = head_masks((width, channels), 1, heads)
    weight_t = proj_weight_ref[...].T
    token_live = lax.broadcasted_iota(jnp.int32, (width, channels), 0)

    def one_row(row, carry):
        shift_sum, gain_sum = carry
        normed = normed_ref[row]
        projected = dot(normed, proj_weight_ref[...])
        queries = (projected[:, :channels] * scaling).astype(BF16)
        keys = projected[:, channels : 2 * channels].astype(BF16)
        values = projected[:, 2 * channels : 3 * channels].astype(BF16)
        gating = jax.nn.sigmoid(projected[:, 3 * channels :] + gate_shift_ref[...])
        turned = contract(weight_t[channels : 3 * channels], normed, 1, 1).astype(BF16)
        keys_t, values_t = turned[:channels], turned[channels:]
        live = token_live < jnp.where(first_row + row < length, length, 0)
        d_output = jnp.where(live, cot_ref[row].astype(F32), 0.0).astype(BF16)
        d_output_all[row] = d_output
        d_mixed = contract(d_output, out_weight_ref[...], 1, 1)
        d_attend = (d_mixed * gating).astype(BF16)
        scores = contract(stack_heads(keys, lane_masks), queries, 1, 1)
        grads = contract(stack_heads(values, lane_masks), d_attend, 1, 1)
        weights, lows, attended_t, d_query_t = [], [], [], []
        for h in range(heads):
            part = slice(h * width, (h + 1) * width)
            expo = jnp.exp(scores[part] + bias_t[part])
            probs = expo * (1.0 / jnp.sum(expo, 0, keepdims=True))
            weight = probs.astype(BF16)
            g = grads[part]
            d_scores = probs * (g - jnp.sum(probs * g, 0, keepdims=True))
            bias_sum[part] += d_scores
            low = d_scores.astype(BF16)
            weights.append(weight)
            lows.append(low)
            own = slice(h * head_size, (h + 1) * head_size)
            attended_t.append(dot(values_t[own], weight))
            d_query_t.append(dot(keys_t[own], low))
        attended = jnp.concatenate(attended_t, 0).T.astype(BF16).astype(F32)
        d_query = jnp.concatenate(d_query_t, 0).T
        d_value = pick_heads(dot(jnp.concatenate(weights, 0), d_attend), lane_masks)
        d_key = pick_heads(dot(jnp.concatenate(lows, 0), queries), lane_masks)
        mixed = (gating * attended).astype(BF16)
        mixed_all[row] = mixed
        output = dot(mixed, out_weight_ref[...])
        updated_ref[row] = (
            pair_ref[row].astype(F32) + jnp.where(live, output, 0.0)
        ).astype(BF16)
        d_gating = (d_mixed * attended * gating * (1.0 - gating)).astype(BF16)
        d_row = jnp.concatenate(
            [
                (d_query * scaling).astype(BF16),
                d_key.astype(BF16),
                d_value.astype(BF16),
                d_gating,
            ],
            1,
        )
        d_proj[row] = d_row
        normed_proj = dot(d_row, weight_t)
        normed_proj_ref[row] = normed_proj
        x_hat, _ = standardize(pair_ref[row])
        shift_sum = shift_sum + jnp.sum(d_gating.astype(F32), 0, keepdims=True)
        gain_sum = gain_sum + jnp.sum(normed_proj * x_hat, 0, keepdims=True)
        return shift_sum, gain_sum

    zero = jnp.zeros((1, channels), F32)
    shift_sum, gain_sum = lax.fori_loop(0, row_count, one_row, (zero, zero))
    shared = heads * row_count
    for h in range(heads):
        turned = bias_sum[h * width : (h + 1) * width].T
        for d in range(devices):
            parts[d, h * row_count : (h + 1) * row_count] = turned[
                d * row_count : (d + 1) * row_count
            ]
    tokens = row_count * width
    normed = normed_ref[...].reshape(tokens, channels)
    grad_proj = contract(normed, d_proj[...].reshape(tokens, 4 * channels), 0, 0)
    grad_out = contract(
        mixed_all[...].reshape(tokens, channels),
        d_output_all[...].reshape(tokens, channels),
        0,
        0,
    )
    pieces = [grad_proj[:, i * channels : (i + 1) * channels] for i in range(4)] + [grad_out]
    for d in range(devices):
        for i, piece in enumerate(pieces):
            start = shared + i * row_count
            parts[d, start : start + row_count] = piece[d * row_count : (d + 1) * row_count]
    unused = shared + len(pieces) * row_count
    parts[:, unused:] = jnp.zeros((devices, parts.shape[1] - unused, width), F32)
    parts_ref[...] = parts[...].astype(BF16)
    small_ref[0:1] = gain_sum
    small_ref[1:2] = shift_sum


def dot(a, b):
    return jnp.dot(a, b, preferred_element_type=F32)


def finish_kernel(
    pair_ref,
    cot_ref,
    normed_ref,
    normed_proj_ref,
    parts_ref,
    small_ref,
    gain_ref,
    bias_weight_ref,
    pair_grad_ref,
    sums_ref,
    held,
):
    row_count, width, channels = pair_ref.shape
    heads = bias_weight_ref.shape[0]
    shared = heads * row_count
    total = parts_ref[0].astype(F32)
    for d in range(1, parts_ref.shape[0]):
        total = total + parts_ref[d].astype(F32)
    bias_grad = total[:shared].astype(BF16).astype(F32)
    of_row = lax.broadcasted_iota(jnp.int32, bias_grad.shape, 0) % row_count
    weight_t = bias_weight_ref[...].astype(F32)
    spread = jnp.concatenate(
        [jnp.broadcast_to(weight_t[h : h + 1], (row_count, channels)) for h in range(heads)], 0
    ).astype(BF16)
    grad_bias = jnp.zeros((shared, channels), F32)
    gain_sum = small_ref[0:1]
    for row in range(row_count):
        own = jnp.where(of_row == row, bias_grad, 0.0)
        grad_bias = grad_bias + dot(own.astype(BF16), normed_ref[row])
        added = dot(own.T.astype(BF16), spread)
        x_hat, inv_std = standardize(pair_ref[row])
        gain_sum = gain_sum + jnp.sum(added * x_hat, 0, keepdims=True)
        d_x_hat = (normed_proj_ref[row] + added) * gain_ref[...]
        d_pair = inv_std * (
            d_x_hat
            - jnp.mean(d_x_hat, -1, keepdims=True)
            - x_hat * jnp.mean(d_x_hat * x_hat, -1, keepdims=True)
        )
        pair_grad_ref[row] = (cot_ref[row].astype(F32) + d_pair).astype(BF16)
    grads = 5 * row_count
    held[:grads] = total[shared : shared + grads]
    held[grads:] = jnp.zeros((held.shape[0] - grads, channels), F32)
    for h in range(heads):
        held[grads + h : grads + h + 1] = jnp.sum(
            grad_bias[h * row_count : (h + 1) * row_count], 0, keepdims=True
        )
    held[grads + heads : grads + heads + 1] = gain_sum
    held[grads + heads + 1 : grads + heads + 2] = small_ref[1:2]
    block = held[...].astype(BF16)
    for peer in range(sums_ref.shape[0]):
        sums_ref[peer] = block


def sum_kernel(sums_ref, out_ref):
    total = sums_ref[0].astype(F32)
    for d in range(1, sums_ref.shape[0]):
        total = total + sums_ref[d].astype(F32)
    block = total.astype(BF16)
    for peer in range(out_ref.shape[0]):
        out_ref[peer] = block


def assemble_kernel(
    heads, scale, blocks_ref, grad_proj_ref, grad_shift_ref, grad_out_ref, grad_bias_ref, grad_gain_ref
):
    devices = blocks_ref.shape[0]
    channels = grad_out_ref.shape[0]
    row_count = channels // devices
    grads = 5 * row_count
    small = None
    for d in range(devices):
        block = blocks_ref[d].astype(F32) * scale
        own = slice(d * row_count, (d + 1) * row_count)
        for i in range(4):
            grad_proj_ref[own, i * channels : (i + 1) * channels] = block[
                i * row_count : (i + 1) * row_count
            ]
        grad_out_ref[own] = block[4 * row_count : grads]
        small = block[grads:] if small is None else small + block[grads:]
    grad_bias_ref[...] = small[:heads]
    grad_gain_ref[...] = small[heads : heads + 1]
    grad_shift_ref[...] = small[heads + 1 : heads + 2]


def per_device(
    pair_act, lengths, cotangent, proj_weight, gate_shift, out_weight, bias_weight, norm_gain
):
    pair, cot = pair_act[0], cotangent[0]
    row_count, width, channels = pair.shape
    heads = bias_weight.shape[1]
    gain, bias_weight_t = norm_gain[None], bias_weight.T
    devices, samples = lax.axis_size("dap"), lax.axis_size("dp")
    shared = heads * row_count
    chunk = -(-(5 * row_count + heads + 2) // 16) * 16
    vmem = pl.BlockSpec(memory_space=pltpu.VMEM)
    smem = pl.BlockSpec(memory_space=pltpu.SMEM)
    params = pltpu.CompilerParams(vmem_limit_bytes=VMEM_LIMIT)
    rows_shape = (row_count, width, channels)

    def exchange(blocks, axis):
        return lax.all_to_all(blocks, axis, 0, 0, tiled=True)

    normed, bias_copies = pl.pallas_call(
        norm_kernel,
        out_shape=(
            jax.ShapeDtypeStruct(rows_shape, BF16),
            jax.ShapeDtypeStruct((devices, shared, width), BF16),
        ),
        in_specs=[vmem] * 3,
        out_specs=(vmem, vmem),
        scratch_shapes=[pltpu.VMEM((shared, width), F32)],
        compiler_params=params,
        name="norm",
    )(pair, gain, bias_weight_t)
    bias_all = exchange(bias_copies, "dap")
    place = jnp.stack([lengths[0], lax.axis_index("dap") * row_count]).astype(jnp.int32)
    updated, normed_proj, parts, small = pl.pallas_call(
        attend_kernel,
        out_shape=(
            jax.ShapeDtypeStruct(rows_shape, BF16),
            jax.ShapeDtypeStruct(rows_shape, F32),
            jax.ShapeDtypeStruct((devices, shared + chunk, width), BF16),
            jax.ShapeDtypeStruct((2, channels), F32),
        ),
        in_specs=[smem] + [vmem] * 7,
        out_specs=(vmem,) * 4,
        scratch_shapes=[
            pltpu.VMEM((heads * width, width), F32),
            pltpu.VMEM((heads * width, width), F32),
            pltpu.VMEM((row_count, width, 4 * channels), BF16),
            pltpu.VMEM(rows_shape, BF16),
            pltpu.VMEM(rows_shape, BF16),
            pltpu.VMEM((devices, shared + chunk, width), F32),
        ],
        compiler_params=params,
        name="attend",
    )(place, pair, cot, normed, bias_all, proj_weight, gate_shift[None], out_weight)
    parts = exchange(parts, "dap")
    pair_grad, sums = pl.pallas_call(
        finish_kernel,
        out_shape=(
            jax.ShapeDtypeStruct(rows_shape, BF16),
            jax.ShapeDtypeStruct((samples, chunk, channels), BF16),
        ),
        in_specs=[vmem] * 8,
        out_specs=(vmem,) * 2,
        scratch_shapes=[pltpu.VMEM((chunk, channels), F32)],
        compiler_params=params,
        name="finish",
    )(pair, cot, normed, normed_proj, parts, small, gain, bias_weight_t)
    sums = exchange(sums, "dp")
    blocks = pl.pallas_call(
        sum_kernel,
        out_shape=jax.ShapeDtypeStruct((devices, chunk, channels), BF16),
        in_specs=[vmem],
        out_specs=vmem,
        compiler_params=params,
        name="sum",
    )(sums)
    blocks = exchange(blocks, "dap")
    grad_proj, grad_shift, grad_out, grad_bias, grad_gain = pl.pallas_call(
        functools.partial(assemble_kernel, heads, 1.0 / width),
        out_shape=(
            jax.ShapeDtypeStruct((channels, 4 * channels), F32),
            jax.ShapeDtypeStruct((1, channels), F32),
            jax.ShapeDtypeStruct((channels, channels), F32),
            jax.ShapeDtypeStruct((heads, channels), F32),
            jax.ShapeDtypeStruct((1, channels), F32),
        ),
        in_specs=[vmem],
        out_specs=(vmem,) * 5,
        compiler_params=params,
        name="assemble",
    )(blocks)
    return (
        updated[None],
        pair_grad[None],
        grad_proj,
        grad_shift[0],
        grad_out,
        grad_bias.T,
        grad_gain[0],
    )


def solution(mesh):
    rows = P("dp", "dap", None, None)
    return jax.shard_map(
        per_device,
        mesh=mesh,
        in_specs=(rows, P("dp"), rows, P(), P(), P(), P(), P()),
        out_specs=(rows, rows, P(), P(), P(), P(), P()),
        check_vma=False,
    )
```

```python
import functools

import jax
import jax.numpy as jnp
from jax import lax
from jax.experimental import pallas as pl
from jax.experimental.pallas import tpu as pltpu
from jax.sharding import PartitionSpec as P

EPS = 1e-05
DEAD = -1e30
F32 = jnp.float32
BF16 = jnp.bfloat16
VMEM_LIMIT = 40 * 1024 * 1024
UNROLL_PROJECT = 4
UNROLL_ATTEND = 4


def contract(a, b, a_axis, b_axis):
    return lax.dot_general(
        a, b, (((a_axis,), (b_axis,)), ((), ())), preferred_element_type=F32
    )


def standardize(rows):
    rows = rows.astype(F32)
    centered = rows - jnp.mean(rows, -1, keepdims=True)
    inv_std = lax.rsqrt(jnp.mean(centered * centered, -1, keepdims=True) + EPS)
    return centered * inv_std, inv_std


def head_masks(shape, axis, heads):
    size = shape[axis] // heads
    position = lax.broadcasted_iota(jnp.int32, shape, axis)
    return [(position >= h * size) & (position < (h + 1) * size) for h in range(heads)]


def stack_heads(block, masks):
    return jnp.concatenate([jnp.where(m, block, jnp.zeros_like(block)) for m in masks], 0)


def pick_heads(stacked, masks):
    size = stacked.shape[0] // len(masks)
    picked = stacked[:size]
    for h in range(1, len(masks)):
        picked = jnp.where(masks[h], stacked[h * size : (h + 1) * size], picked)
    return picked


def norm_kernel(pair_ref, gain_ref, bias_weight_ref, normed_ref, bias_ref, held):
    row_count = pair_ref.shape[0]
    heads = bias_weight_ref.shape[0]
    for row in range(row_count):
        x_hat, _ = standardize(pair_ref[row])
        normed = (x_hat * gain_ref[...]).astype(BF16)
        normed_ref[row] = normed
        held[pl.ds(row, heads, stride=row_count), :] = contract(
            bias_weight_ref[...], normed, 1, 1
        )
    block = held[...].astype(BF16)
    for peer in range(bias_ref.shape[0]):
        bias_ref[peer] = block


def dot(a, b):
    return jnp.dot(a, b, preferred_element_type=F32)


def project_kernel(
    place_ref,
    cot_ref,
    normed_ref,
    proj_weight_ref,
    gate_shift_ref,
    out_weight_ref,
    queries_ref,
    turned_ref,
    gating_ref,
    d_output_ref,
    d_mixed_ref,
    d_attend_ref,
    scores_ref,
    grads_ref,
):
    row_count, width, channels = cot_ref.shape
    heads = scores_ref.shape[1] // width
    scaling = (channels // heads) ** (-0.5)
    length, first_row = place_ref[0], place_ref[1]
    lane_masks = head_masks((width, channels), 1, heads)
    weight_t = proj_weight_ref[:, channels : 3 * channels].T
    token = lax.broadcasted_iota(jnp.int32, (width, channels), 0)

    def one_row(row, carry):
        normed = normed_ref[row]
        projected = dot(normed, proj_weight_ref[...])
        queries = (projected[:, :channels] * scaling).astype(BF16)
        keys = projected[:, channels : 2 * channels].astype(BF16)
        values = projected[:, 2 * channels : 3 * channels].astype(BF16)
        gating = jax.nn.sigmoid(projected[:, 3 * channels :] + gate_shift_ref[...])
        live = token < jnp.where(first_row + row < length, length, 0)
        d_output = jnp.where(live, cot_ref[row].astype(F32), 0.0).astype(BF16)
        d_mixed = contract(d_output, out_weight_ref[...], 1, 1)
        d_attend = (d_mixed * gating).astype(BF16)
        queries_ref[row] = queries
        turned_ref[row] = contract(weight_t, normed, 1, 1).astype(BF16)
        gating_ref[row] = gating
        d_output_ref[row] = d_output
        d_mixed_ref[row] = d_mixed
        d_attend_ref[row] = d_attend
        scores_ref[row] = contract(stack_heads(keys, lane_masks), queries, 1, 1)
        grads_ref[row] = contract(stack_heads(values, lane_masks), d_attend, 1, 1)
        return carry

    lax.fori_loop(0, row_count, one_row, 0, unroll=UNROLL_PROJECT)


def attend_kernel(
    place_ref,
    bias_ref,
    normed_ref,
    queries_ref,
    turned_ref,
    gating_ref,
    d_output_ref,
    d_mixed_ref,
    d_attend_ref,
    scores_ref,
    grads_ref,
    parts_ref,
    mixed_ref,
    d_proj_ref,
    shift_ref,
    bias_t,
    bias_sum,
    parts,
):
    row_count, width, channels = normed_ref.shape
    heads = bias_t.shape[0] // width
    head_size = channels // heads
    scaling = head_size ** (-0.5)
    length = place_ref[0]
    devices = bias_ref.shape[0]
    key_live = lax.broadcasted_iota(jnp.int32, (width, width), 0) < length
    for h in range(heads):
        rows = [
            bias_ref[d].astype(F32)[h * row_count : (h + 1) * row_count]
            for d in range(devices)
        ]
        turned = jnp.concatenate(rows, 0).T
        bias_t[h * width : (h + 1) * width] = jnp.where(key_live, turned, DEAD)
    bias_sum[...] = jnp.zeros_like(bias_sum)
    lane_masks = head_masks((width, channels), 1, heads)

    def one_row(row, shift_sum):
        weights, lows, attended_t, d_query_t = [], [], [], []
        for h in range(heads):
            part = slice(h * width, (h + 1) * width)
            own = slice(h * head_size, (h + 1) * head_size)
            expo = jnp.exp(scores_ref[row, part] + bias_t[part])
            probs = expo * (1.0 / jnp.sum(expo, 0, keepdims=True))
            weight = probs.astype(BF16)
            g = grads_ref[row, part]
            d_scores = probs * (g - jnp.sum(probs * g, 0, keepdims=True))
            bias_sum[part] += d_scores
            low = d_scores.astype(BF16)
            weights.append(weight)
            lows.append(low)
            attended_t.append(
                dot(turned_ref[row, channels + own.start : channels + own.stop], weight)
            )
            d_query_t.append(dot(turned_ref[row, own], low))
        attended = jnp.concatenate(attended_t, 0).T.astype(BF16).astype(F32)
        d_query = jnp.concatenate(d_query_t, 0).T
        d_value = pick_heads(dot(jnp.concatenate(weights, 0), d_attend_ref[row]), lane_masks)
        d_key = pick_heads(dot(jnp.concatenate(lows, 0), queries_ref[row]), lane_masks)
        gating = gating_ref[row]
        mixed = gating * attended
        mixed_ref[row] = mixed.astype(BF16)
        d_gating = (d_mixed_ref[row] * mixed * (1.0 - gating)).astype(BF16)
        d_proj_ref[row, :, :channels] = (d_query * scaling).astype(BF16)
        d_proj_ref[row, :, channels : 2 * channels] = d_key.astype(BF16)
        d_proj_ref[row, :, 2 * channels : 3 * channels] = d_value.astype(BF16)
        d_proj_ref[row, :, 3 * channels :] = d_gating
        return shift_sum + jnp.sum(d_gating.astype(F32), 0, keepdims=True)

    zero = jnp.zeros((1, channels), F32)
    shift_ref[...] = lax.fori_loop(0, row_count, one_row, zero, unroll=UNROLL_ATTEND)
    shared = heads * row_count
    for h in range(heads):
        turned = bias_sum[h * width : (h + 1) * width].T
        for d in range(devices):
            parts[d, h * row_count : (h + 1) * row_count] = turned[
                d * row_count : (d + 1) * row_count
            ]
    tokens = row_count * width
    normed = normed_ref[...].reshape(tokens, channels)
    grad_proj = contract(normed, d_proj_ref[...].reshape(tokens, 4 * channels), 0, 0)
    grad_out = contract(
        mixed_ref[...].reshape(tokens, channels),
        d_output_ref[...].reshape(tokens, channels),
        0,
        0,
    )
    pieces = [grad_proj[:, i * channels : (i + 1) * channels] for i in range(4)] + [grad_out]
    for d in range(devices):
        for i, piece in enumerate(pieces):
            start = shared + i * row_count
            parts[d, start : start + row_count] = piece[d * row_count : (d + 1) * row_count]
    unused = shared + len(pieces) * row_count
    parts[:, unused:] = jnp.zeros((devices, parts.shape[1] - unused, width), F32)
    parts_ref[...] = parts[...].astype(BF16)


def update_kernel(
    place_ref,
    pair_ref,
    mixed_ref,
    d_proj_ref,
    proj_weight_ref,
    out_weight_ref,
    updated_ref,
    normed_proj_ref,
    gain_ref,
):
    row_count, width, channels = pair_ref.shape
    length, first_row = place_ref[0], place_ref[1]
    token = lax.broadcasted_iota(jnp.int32, (width, channels), 0)
    gain_sum = jnp.zeros((1, channels), F32)
    for row in range(row_count):
        live = token < jnp.where(first_row + row < length, length, 0)
        output = dot(mixed_ref[row], out_weight_ref[...])
        updated_ref[row] = (
            pair_ref[row].astype(F32) + jnp.where(live, output, 0.0)
        ).astype(BF16)
        normed_proj = contract(d_proj_ref[row], proj_weight_ref[...], 1, 1)
        normed_proj_ref[row] = normed_proj
        x_hat, _ = standardize(pair_ref[row])
        gain_sum = gain_sum + jnp.sum(normed_proj * x_hat, 0, keepdims=True)
    gain_ref[...] = gain_sum


def bias_kernel(
    parts_ref,
    normed_ref,
    gain_sum_ref,
    shift_ref,
    gain_ref,
    bias_weight_ref,
    bias_grad_ref,
    sums_ref,
    held,
):
    row_count, width, channels = normed_ref.shape
    heads = bias_weight_ref.shape[0]
    shared = heads * row_count
    total = parts_ref[0].astype(F32)
    for d in range(1, parts_ref.shape[0]):
        total = total + parts_ref[d].astype(F32)
    bias_grad = total[:shared].astype(BF16)
    bias_grad_ref[...] = bias_grad
    bias_grad = bias_grad.astype(F32)
    of_row = lax.broadcasted_iota(jnp.int32, bias_grad.shape, 0) % row_count
    grad_bias = jnp.zeros((shared, channels), F32)
    for row in range(row_count):
        own = jnp.where(of_row == row, bias_grad, 0.0).astype(BF16)
        grad_bias = grad_bias + dot(own, normed_ref[row])
    grads = 5 * row_count
    held[:grads] = total[shared : shared + grads]
    held[grads:] = jnp.zeros((held.shape[0] - grads, channels), F32)
    weight = bias_weight_ref[...].astype(F32)
    added = jnp.zeros((1, channels), F32)
    for h in range(heads):
        summed = jnp.sum(grad_bias[h * row_count : (h + 1) * row_count], 0, keepdims=True)
        held[grads + h : grads + h + 1] = summed
        added = added + summed * weight[h : h + 1]
    held[grads + heads : grads + heads + 1] = gain_sum_ref[...] + added / gain_ref[...]
    held[grads + heads + 1 : grads + heads + 2] = shift_ref[...]
    block = held[...].astype(BF16)
    for peer in range(sums_ref.shape[0]):
        sums_ref[peer] = block


def finish_kernel(
    pair_ref,
    cot_ref,
    normed_proj_ref,
    bias_grad_ref,
    gain_ref,
    bias_weight_ref,
    pair_grad_ref,
):
    row_count, width, channels = pair_ref.shape
    heads = bias_weight_ref.shape[0]
    bias_grad = bias_grad_ref[...].astype(F32)
    of_row = lax.broadcasted_iota(jnp.int32, bias_grad.shape, 0) % row_count
    weight = bias_weight_ref[...].astype(F32)
    spread = jnp.concatenate(
        [jnp.broadcast_to(weight[h : h + 1], (row_count, channels)) for h in range(heads)], 0
    ).astype(BF16)
    for row in range(row_count):
        own = jnp.where(of_row == row, bias_grad, 0.0)
        added = dot(own.T.astype(BF16), spread)
        x_hat, inv_std = standardize(pair_ref[row])
        d_x_hat = (normed_proj_ref[row] + added) * gain_ref[...]
        d_pair = inv_std * (
            d_x_hat
            - jnp.mean(d_x_hat, -1, keepdims=True)
            - x_hat * jnp.mean(d_x_hat * x_hat, -1, keepdims=True)
        )
        pair_grad_ref[row] = (cot_ref[row].astype(F32) + d_pair).astype(BF16)


def sum_kernel(sums_ref, out_ref):
    total = sums_ref[0].astype(F32)
    for d in range(1, sums_ref.shape[0]):
        total = total + sums_ref[d].astype(F32)
    block = total.astype(BF16)
    for peer in range(out_ref.shape[0]):
        out_ref[peer] = block


def assemble_kernel(
    heads, scale, blocks_ref, grad_proj_ref, grad_shift_ref, grad_out_ref, grad_bias_ref, grad_gain_ref
):
    devices = blocks_ref.shape[0]
    channels = grad_out_ref.shape[0]
    row_count = channels // devices
    grads = 5 * row_count
    small = None
    for d in range(devices):
        block = blocks_ref[d].astype(F32) * scale
        own = slice(d * row_count, (d + 1) * row_count)
        for i in range(4):
            grad_proj_ref[own, i * channels : (i + 1) * channels] = block[
                i * row_count : (i + 1) * row_count
            ]
        grad_out_ref[own] = block[4 * row_count : grads]
        small = block[grads:] if small is None else small + block[grads:]
    grad_bias_ref[...] = small[:heads]
    grad_gain_ref[...] = small[heads : heads + 1]
    grad_shift_ref[...] = small[heads + 1 : heads + 2]


def per_device(
    pair_act, lengths, cotangent, proj_weight, gate_shift, out_weight, bias_weight, norm_gain
):
    pair, cot = pair_act[0], cotangent[0]
    row_count, width, channels = pair.shape
    heads = bias_weight.shape[1]
    gain, bias_weight_t = norm_gain[None], bias_weight.T
    devices, samples = lax.axis_size("dap"), lax.axis_size("dp")
    shared = heads * row_count
    chunk = -(-(5 * row_count + heads + 2) // 16) * 16
    vmem = pl.BlockSpec(memory_space=pltpu.VMEM)
    smem = pl.BlockSpec(memory_space=pltpu.SMEM)
    rows_shape = (row_count, width, channels)
    heads_shape = (row_count, heads * width, width)
    line = ((1, channels), F32)

    def call(kernel, name, args, outs, scratch=(), placed=False, flops=0, moved=0):
        return pl.pallas_call(
            kernel,
            out_shape=tuple(jax.ShapeDtypeStruct(shape, dtype) for shape, dtype in outs),
            in_specs=[smem] * placed + [vmem] * (len(args) - placed),
            out_specs=(vmem,) * len(outs),
            scratch_shapes=[pltpu.VMEM(shape, dtype) for shape, dtype in scratch],
            compiler_params=pltpu.CompilerParams(vmem_limit_bytes=VMEM_LIMIT),
            cost_estimate=pl.CostEstimate(flops=flops, bytes_accessed=moved, transcendentals=0),
            name=name,
        )(*args)

    def exchange(blocks, axis):
        return lax.all_to_all(blocks, axis, 0, 0, tiled=True)

    normed, bias_copies = call(
        norm_kernel,
        "norm",
        (pair, gain, bias_weight_t),
        [(rows_shape, BF16), ((devices, shared, width), BF16)],
        [((shared, width), F32)],
    )
    bias_all = exchange(bias_copies, "dap")
    place = jnp.stack([lengths[0], lax.axis_index("dap") * row_count]).astype(jnp.int32)
    projected = call(
        project_kernel,
        "project",
        (place, cot, normed, proj_weight, gate_shift[None], out_weight),
        [
            (rows_shape, BF16),
            ((row_count, 2 * channels, width), BF16),
            (rows_shape, F32),
            (rows_shape, BF16),
            (rows_shape, F32),
            (rows_shape, BF16),
            (heads_shape, F32),
            (heads_shape, F32),
        ],
        placed=True,
        flops=3 * 10**9,
        moved=10**7,
    )
    parts, mixed, d_proj, shift = call(
        attend_kernel,
        "attend",
        (place, bias_all, normed, *projected),
        [
            ((devices, shared + chunk, width), BF16),
            (rows_shape, BF16),
            ((row_count, width, 4 * channels), BF16),
            line,
        ],
        [
            ((heads * width, width), F32),
            ((heads * width, width), F32),
            ((devices, shared + chunk, width), F32),
        ],
        placed=True,
    )
    parts = exchange(parts, "dap")
    updated, normed_proj, gain_sum = call(
        update_kernel,
        "update",
        (place, pair, mixed, d_proj, proj_weight, out_weight),
        [(rows_shape, BF16), (rows_shape, F32), line],
        placed=True,
        flops=2 * 10**9,
        moved=6 * 10**6,
    )
    bias_grad, sums = call(
        bias_kernel,
        "bias_grad",
        (parts, normed, gain_sum, shift, gain, bias_weight_t),
        [((shared, width), BF16), ((samples, chunk, channels), BF16)],
        [((chunk, channels), F32)],
    )
    sums = exchange(sums, "dp")
    (pair_grad,) = call(
        finish_kernel,
        "finish",
        (pair, cot, normed_proj, bias_grad, gain, bias_weight_t),
        [(rows_shape, BF16)],
        flops=2 * 10**9,
        moved=6 * 10**6,
    )
    (blocks,) = call(sum_kernel, "sum", (sums,), [((devices, chunk, channels), BF16)])
    blocks = exchange(blocks, "dap")
    grad_proj, grad_shift, grad_out, grad_bias, grad_gain = call(
        functools.partial(assemble_kernel, heads, 1.0 / width),
        "assemble",
        (blocks,),
        [
            ((channels, 4 * channels), F32),
            line,
            ((channels, channels), F32),
            ((heads, channels), F32),
            line,
        ],
    )
    return (
        updated[None],
        pair_grad[None],
        grad_proj,
        grad_shift[0],
        grad_out,
        grad_bias.T,
        grad_gain[0],
    )


def solution(mesh):
    rows = P("dp", "dap", None, None)
    return jax.shard_map(
        per_device,
        mesh=mesh,
        in_specs=(rows, P("dp"), rows, P(), P(), P(), P(), P()),
        out_specs=(rows, rows, P(), P(), P(), P(), P()),
        check_vma=False,
    )
```

```python
import functools

import jax
import jax.numpy as jnp
from jax import lax
from jax.experimental import pallas as pl
from jax.experimental.pallas import tpu as pltpu
from jax.sharding import PartitionSpec as P

EPS = 1e-05
DEAD = -1e30
F32 = jnp.float32
BF16 = jnp.bfloat16
VMEM_LIMIT = 16 * 1024 * 1024
UNROLL_PROJECT = 4
UNROLL_ATTEND = 4


def contract(a, b, a_axis, b_axis):
    return lax.dot_general(
        a, b, (((a_axis,), (b_axis,)), ((), ())), preferred_element_type=F32
    )


def standardize(rows):
    rows = rows.astype(F32)
    centered = rows - jnp.mean(rows, -1, keepdims=True)
    inv_std = lax.rsqrt(jnp.mean(centered * centered, -1, keepdims=True) + EPS)
    return centered * inv_std, inv_std


def head_masks(shape, axis, heads):
    size = shape[axis] // heads
    position = lax.broadcasted_iota(jnp.int32, shape, axis)
    return [(position >= h * size) & (position < (h + 1) * size) for h in range(heads)]


def stack_heads(block, masks):
    return jnp.concatenate([jnp.where(m, block, jnp.zeros_like(block)) for m in masks], 0)


def pick_heads(stacked, masks):
    size = stacked.shape[0] // len(masks)
    picked = stacked[:size]
    for h in range(1, len(masks)):
        picked = jnp.where(masks[h], stacked[h * size : (h + 1) * size], picked)
    return picked


def norm_kernel(pair_ref, gain_ref, bias_weight_ref, normed_ref, bias_ref, held):
    row_count = pair_ref.shape[0]
    heads = bias_weight_ref.shape[0]
    for row in range(row_count):
        x_hat, _ = standardize(pair_ref[row])
        normed = (x_hat * gain_ref[...]).astype(BF16)
        normed_ref[row] = normed
        held[pl.ds(row, heads, stride=row_count), :] = contract(
            bias_weight_ref[...], normed, 1, 1
        )
    block = held[...].astype(BF16)
    for peer in range(bias_ref.shape[0]):
        bias_ref[peer] = block


def dot(a, b):
    return jnp.dot(a, b, preferred_element_type=F32)


def project_kernel(
    place_ref,
    cot_ref,
    normed_ref,
    proj_weight_ref,
    gate_shift_ref,
    out_weight_ref,
    bias_weight_ref,
    narrow_ref,
    wide_ref,
):
    row_count, width, channels = cot_ref.shape
    heads = bias_weight_ref.shape[0]
    scaling = (channels // heads) ** (-0.5)
    length, first_row = place_ref[0], place_ref[1]
    weight_t = proj_weight_ref[:, channels : 3 * channels].T
    token = lax.broadcasted_iota(jnp.int32, (width, channels), 0)

    def one_row(row, carry):
        normed = normed_ref[row]
        projected = dot(normed, proj_weight_ref[...])
        queries = (projected[:, :channels] * scaling).astype(BF16)
        keys = projected[:, channels : 2 * channels].astype(BF16)
        values = projected[:, 2 * channels : 3 * channels].astype(BF16)
        gating = jax.nn.sigmoid(projected[:, 3 * channels :] + gate_shift_ref[...])
        live = token < jnp.where(first_row + row < length, length, 0)
        d_output = jnp.where(live, cot_ref[row].astype(F32), 0.0).astype(BF16)
        d_mixed = contract(d_output, out_weight_ref[...], 1, 1)
        d_attend = (d_mixed * gating).astype(BF16)
        for n, block in enumerate((queries, d_attend, d_output, keys, values)):
            narrow_ref[row, n * width : (n + 1) * width] = block
        narrow_ref[row, 5 * width :] = contract(weight_t, normed, 1, 1).astype(BF16)
        wide_ref[row, :width] = gating
        wide_ref[row, width:] = d_mixed
        return carry

    lax.fori_loop(0, row_count, one_row, 0, unroll=UNROLL_PROJECT)


def attend_kernel(
    place_ref,
    bias_ref,
    normed_ref,
    narrow_ref,
    wide_ref,
    proj_weight_ref,
    parts_ref,
    mixed_ref,
    normed_proj_ref,
    shift_ref,
    bias_t,
    bias_sum,
    parts,
    d_proj,
    weight_t,
):
    row_count, width, channels = normed_ref.shape
    heads = bias_t.shape[0] // width
    head_size = channels // heads
    scaling = head_size ** (-0.5)
    length = place_ref[0]
    devices = bias_ref.shape[0]
    key_live = lax.broadcasted_iota(jnp.int32, (width, width), 0) < length
    for h in range(heads):
        rows = [
            bias_ref[d].astype(F32)[h * row_count : (h + 1) * row_count]
            for d in range(devices)
        ]
        turned = jnp.concatenate(rows, 0).T
        bias_t[h * width : (h + 1) * width] = jnp.where(key_live, turned, DEAD)
    bias_sum[...] = jnp.zeros_like(bias_sum)
    lane_masks = head_masks((width, channels), 1, heads)
    weight_t[...] = proj_weight_ref[...].T

    def one_row(row, shift_sum):
        weights, lows, attended_t, d_query_t = [], [], [], []
        queries, d_attend, _, keys, values = (
            narrow_ref[row, n * width : (n + 1) * width] for n in range(5)
        )
        turned = narrow_ref.at[row, 5 * width :]
        scores = contract(stack_heads(keys, lane_masks), queries, 1, 1)
        grads = contract(stack_heads(values, lane_masks), d_attend, 1, 1)
        for h in range(heads):
            part = slice(h * width, (h + 1) * width)
            own = slice(h * head_size, (h + 1) * head_size)
            expo = jnp.exp(scores[part] + bias_t[part])
            probs = expo * (1.0 / jnp.sum(expo, 0, keepdims=True))
            weight = probs.astype(BF16)
            g = grads[part]
            d_scores = probs * (g - jnp.sum(probs * g, 0, keepdims=True))
            bias_sum[part] += d_scores
            low = d_scores.astype(BF16)
            weights.append(weight)
            lows.append(low)
            attended_t.append(dot(turned[channels + own.start : channels + own.stop], weight))
            d_query_t.append(dot(turned[own], low))
        attended = jnp.concatenate(attended_t, 0).T.astype(BF16).astype(F32)
        d_query = jnp.concatenate(d_query_t, 0).T
        d_value = pick_heads(dot(jnp.concatenate(weights, 0), d_attend), lane_masks)
        d_key = pick_heads(dot(jnp.concatenate(lows, 0), queries), lane_masks)
        gating = wide_ref[row, :width]
        mixed = gating * attended
        mixed_ref[row] = mixed.astype(BF16)
        d_gating = (wide_ref[row, width:] * mixed * (1.0 - gating)).astype(BF16)
        d_row = jnp.concatenate(
            [
                (d_query * scaling).astype(BF16),
                d_key.astype(BF16),
                d_value.astype(BF16),
                d_gating,
            ],
            1,
        )
        d_proj[row] = d_row
        normed_proj_ref[row] = dot(d_row, weight_t[...])
        return shift_sum + jnp.sum(d_gating.astype(F32), 0, keepdims=True)

    zero = jnp.zeros((1, channels), F32)
    shift_ref[...] = lax.fori_loop(0, row_count, one_row, zero, unroll=UNROLL_ATTEND)
    shared = heads * row_count
    for h in range(heads):
        turned = bias_sum[h * width : (h + 1) * width].T
        for d in range(devices):
            parts[d, h * row_count : (h + 1) * row_count] = turned[
                d * row_count : (d + 1) * row_count
            ]
    tokens = row_count * width
    normed = normed_ref[...].reshape(tokens, channels)
    grad_proj = contract(normed, d_proj[...].reshape(tokens, 4 * channels), 0, 0)
    grad_out = contract(
        mixed_ref[...].reshape(tokens, channels),
        narrow_ref[:, 2 * width : 3 * width].reshape(tokens, channels),
        0,
        0,
    )
    pieces = [grad_proj[:, i * channels : (i + 1) * channels] for i in range(4)] + [grad_out]
    for d in range(devices):
        for i, piece in enumerate(pieces):
            start = shared + i * row_count
            parts[d, start : start + row_count] = piece[d * row_count : (d + 1) * row_count]
    unused = shared + len(pieces) * row_count
    parts[:, unused:] = jnp.zeros((devices, parts.shape[1] - unused, width), F32)
    parts_ref[...] = parts[...].astype(BF16)


def bias_kernel(
    parts_ref, normed_ref, shift_ref, mixed_ref, normed_proj_ref, bias_grad_ref, sums_ref, held
):
    del mixed_ref, normed_proj_ref
    row_count, width, channels = normed_ref.shape
    shared = bias_grad_ref.shape[0]
    heads = shared // row_count
    total = parts_ref[0].astype(F32)
    for d in range(1, parts_ref.shape[0]):
        total = total + parts_ref[d].astype(F32)
    bias_grad = total[:shared].astype(BF16)
    bias_grad_ref[...] = bias_grad
    bias_grad = bias_grad.astype(F32)
    of_row = lax.broadcasted_iota(jnp.int32, bias_grad.shape, 0) % row_count
    grad_bias = jnp.zeros((shared, channels), F32)
    for row in range(row_count):
        own = jnp.where(of_row == row, bias_grad, 0.0).astype(BF16)
        grad_bias = grad_bias + dot(own, normed_ref[row])
    grads = 5 * row_count
    held[:grads] = total[shared : shared + grads]
    held[grads:] = jnp.zeros((held.shape[0] - grads, channels), F32)
    for h in range(heads):
        held[grads + h : grads + h + 1] = jnp.sum(
            grad_bias[h * row_count : (h + 1) * row_count], 0, keepdims=True
        )
    held[grads + heads : grads + heads + 1] = shift_ref[...]
    block = held[...].astype(BF16)
    for peer in range(sums_ref.shape[0]):
        sums_ref[peer] = block


def finish_kernel(
    place_ref,
    pair_ref,
    cot_ref,
    mixed_ref,
    normed_proj_ref,
    bias_grad_ref,
    gain_ref,
    bias_weight_ref,
    out_weight_ref,
    updated_ref,
    pair_grad_ref,
):
    row_count, width, channels = pair_ref.shape
    heads = bias_weight_ref.shape[0]
    length, first_row = place_ref[0], place_ref[1]
    token = lax.broadcasted_iota(jnp.int32, (width, channels), 0)
    bias_grad = bias_grad_ref[...].astype(F32)
    of_row = lax.broadcasted_iota(jnp.int32, bias_grad.shape, 0) % row_count
    weight = bias_weight_ref[...].astype(F32)
    spread = jnp.concatenate(
        [jnp.broadcast_to(weight[h : h + 1], (row_count, channels)) for h in range(heads)], 0
    ).astype(BF16)
    for row in range(row_count):
        live = token < jnp.where(first_row + row < length, length, 0)
        output = dot(mixed_ref[row], out_weight_ref[...])
        updated_ref[row] = (
            pair_ref[row].astype(F32) + jnp.where(live, output, 0.0)
        ).astype(BF16)
        own = jnp.where(of_row == row, bias_grad, 0.0)
        added = dot(own.T.astype(BF16), spread)
        x_hat, inv_std = standardize(pair_ref[row])
        d_x_hat = (normed_proj_ref[row] + added) * gain_ref[...]
        d_pair = inv_std * (
            d_x_hat
            - jnp.mean(d_x_hat, -1, keepdims=True)
            - x_hat * jnp.mean(d_x_hat * x_hat, -1, keepdims=True)
        )
        pair_grad_ref[row] = (cot_ref[row].astype(F32) + d_pair).astype(BF16)


def sum_kernel(sums_ref, out_ref):
    total = sums_ref[0].astype(F32)
    for d in range(1, sums_ref.shape[0]):
        total = total + sums_ref[d].astype(F32)
    block = total.astype(BF16)
    for peer in range(out_ref.shape[0]):
        out_ref[peer] = block


def assemble_kernel(
    scale,
    blocks_ref,
    proj_weight_ref,
    bias_weight_ref,
    gain_ref,
    grad_proj_ref,
    grad_shift_ref,
    grad_out_ref,
    grad_bias_ref,
    grad_gain_ref,
):
    devices = blocks_ref.shape[0]
    channels = grad_out_ref.shape[0]
    heads = grad_bias_ref.shape[0]
    row_count = channels // devices
    grads = 5 * row_count
    small = None
    by_channel = []
    for d in range(devices):
        block = blocks_ref[d].astype(F32) * scale
        own = slice(d * row_count, (d + 1) * row_count)
        by_lane = None
        for i in range(4):
            columns = slice(i * channels, (i + 1) * channels)
            piece = block[i * row_count : (i + 1) * row_count]
            grad_proj_ref[own, columns] = piece
            term = piece * proj_weight_ref[own, columns].astype(F32)
            by_lane = term if by_lane is None else by_lane + term
        by_channel.append(by_lane)
        grad_out_ref[own] = block[4 * row_count : grads]
        small = block[grads:] if small is None else small + block[grads:]
    grad_bias_ref[...] = small[:heads]
    grad_shift_ref[...] = small[heads : heads + 1]
    gain_sum = jnp.sum(jnp.concatenate(by_channel, 0).T, 0, keepdims=True)
    gain_sum = gain_sum + jnp.sum(
        small[:heads] * bias_weight_ref[...].astype(F32), 0, keepdims=True
    )
    grad_gain_ref[...] = gain_sum / gain_ref[...]


def per_device(
    pair_act, lengths, cotangent, proj_weight, gate_shift, out_weight, bias_weight, norm_gain
):
    pair, cot = pair_act[0], cotangent[0]
    row_count, width, channels = pair.shape
    heads = bias_weight.shape[1]
    gain, bias_weight_t = norm_gain[None], bias_weight.T
    devices, samples = lax.axis_size("dap"), lax.axis_size("dp")
    shared = heads * row_count
    chunk = -(-(5 * row_count + heads + 1) // 16) * 16
    vmem = pl.BlockSpec(memory_space=pltpu.VMEM)
    smem = pl.BlockSpec(memory_space=pltpu.SMEM)
    rows_shape = (row_count, width, channels)
    line = ((1, channels), F32)

    def call(kernel, name, args, outs, scratch=(), placed=False, flops=0, moved=0):
        return pl.pallas_call(
            kernel,
            out_shape=tuple(jax.ShapeDtypeStruct(shape, dtype) for shape, dtype in outs),
            in_specs=[smem] * placed + [vmem] * (len(args) - placed),
            out_specs=(vmem,) * len(outs),
            scratch_shapes=[pltpu.VMEM(shape, dtype) for shape, dtype in scratch],
            compiler_params=pltpu.CompilerParams(vmem_limit_bytes=VMEM_LIMIT),
            cost_estimate=pl.CostEstimate(flops=flops, bytes_accessed=moved, transcendentals=0),
            name=name,
        )(*args)

    def exchange(blocks, axis):
        return lax.all_to_all(blocks, axis, 0, 0, tiled=True)

    normed, bias_copies = call(
        norm_kernel,
        "norm",
        (pair, gain, bias_weight_t),
        [(rows_shape, BF16), ((devices, shared, width), BF16)],
        [((shared, width), F32)],
    )
    bias_all = exchange(bias_copies, "dap")
    place = jnp.stack([lengths[0], lax.axis_index("dap") * row_count]).astype(jnp.int32)
    narrow, wide = call(
        project_kernel,
        "project",
        (place, cot, normed, proj_weight, gate_shift[None], out_weight, bias_weight_t),
        [
            ((row_count, 5 * width + 2 * channels, width), BF16),
            ((row_count, 2 * width, channels), F32),
        ],
        placed=True,
        flops=3 * 10**9,
        moved=10**7,
    )
    parts, mixed, normed_proj, shift = call(
        attend_kernel,
        "attend",
        (place, bias_all, normed, narrow, wide, proj_weight),
        [
            ((devices, shared + chunk, width), BF16),
            (rows_shape, BF16),
            (rows_shape, F32),
            line,
        ],
        [
            ((heads * width, width), F32),
            ((heads * width, width), F32),
            ((devices, shared + chunk, width), F32),
            ((row_count, width, 4 * channels), BF16),
            ((4 * channels, channels), BF16),
        ],
        placed=True,
    )
    parts = exchange(parts, "dap")
    bias_grad, sums = call(
        bias_kernel,
        "bias_grad",
        (parts, normed, shift, mixed, normed_proj),
        [((shared, width), BF16), ((samples, chunk, channels), BF16)],
        [((chunk, channels), F32)],
    )
    sums = exchange(sums, "dp")
    updated, pair_grad = call(
        finish_kernel,
        "finish",
        (place, pair, cot, mixed, normed_proj, bias_grad, gain, bias_weight_t, out_weight),
        [(rows_shape, BF16), (rows_shape, BF16)],
        placed=True,
        flops=2 * 10**9,
        moved=6 * 10**6,
    )
    sums, pair_grad, updated = lax.optimization_barrier((sums, pair_grad, updated))
    (blocks,) = call(sum_kernel, "sum", (sums,), [((devices, chunk, channels), BF16)])
    blocks = exchange(blocks, "dap")
    grad_proj, grad_shift, grad_out, grad_bias, grad_gain = call(
        functools.partial(assemble_kernel, 1.0 / width),
        "assemble",
        (blocks, proj_weight, bias_weight_t, gain),
        [
            ((channels, 4 * channels), F32),
            line,
            ((channels, channels), F32),
            ((heads, channels), F32),
            line,
        ],
    )
    return (
        updated[None],
        pair_grad[None],
        grad_proj,
        grad_shift[0],
        grad_out,
        grad_bias.T,
        grad_gain[0],
    )


def solution(mesh):
    rows = P("dp", "dap", None, None)
    return jax.shard_map(
        per_device,
        mesh=mesh,
        in_specs=(rows, P("dp"), rows, P(), P(), P(), P(), P()),
        out_specs=(rows, rows, P(), P(), P(), P(), P()),
        check_vma=False,
    )
```

```python
import functools

import jax
import jax.numpy as jnp
from jax import lax
from jax.experimental import pallas as pl
from jax.experimental.pallas import tpu as pltpu
from jax.sharding import PartitionSpec as P

EPS = 1e-05
DEAD = -1e30
F32 = jnp.float32
BF16 = jnp.bfloat16
VMEM_LIMIT = 16 * 1024 * 1024
UNROLL_PROJECT = 4
UNROLL_ATTEND = 4


def dot(a, b):
    return jnp.dot(a, b, preferred_element_type=F32)


def contract(a, b, a_axis, b_axis):
    return lax.dot_general(
        a, b, (((a_axis,), (b_axis,)), ((), ())), preferred_element_type=F32
    )


def standardize(rows):
    rows = rows.astype(F32)
    centered = rows - jnp.mean(rows, -1, keepdims=True)
    inv_std = lax.rsqrt(jnp.mean(centered * centered, -1, keepdims=True) + EPS)
    return centered * inv_std, inv_std


def head_masks(shape, axis, heads):
    size = shape[axis] // heads
    position = lax.broadcasted_iota(jnp.int32, shape, axis)
    return [(position >= h * size) & (position < (h + 1) * size) for h in range(heads)]


def stack_heads(block, masks):
    return jnp.concatenate([jnp.where(m, block, jnp.zeros_like(block)) for m in masks], 0)


def pick_heads(stacked, masks):
    size = stacked.shape[0] // len(masks)
    picked = stacked[:size]
    for h in range(1, len(masks)):
        picked = jnp.where(masks[h], stacked[h * size : (h + 1) * size], picked)
    return picked


def begin_all(sources, targets, sems):
    copies = [
        pltpu.make_async_copy(source, target, sems.at[n])
        for n, (source, target) in enumerate(zip(sources, targets, strict=True))
    ]
    for copy in copies:
        copy.start()
    return copies


def norm_kernel(
    pair_hbm,
    gain_hbm,
    bias_weight_hbm,
    proj_weight_hbm,
    gate_shift_hbm,
    normed_ref,
    bias_ref,
    proj_weight_ref,
    gate_shift_ref,
    pair,
    gain,
    bias_weight,
    held,
    sems,
):
    row_count = pair.shape[0]
    heads = bias_weight.shape[0]
    copies = begin_all(
        (gain_hbm, bias_weight_hbm, pair_hbm, proj_weight_hbm, gate_shift_hbm),
        (gain, bias_weight, pair, proj_weight_ref, gate_shift_ref),
        sems,
    )
    for copy in copies[:3]:
        copy.wait()
    for row in range(row_count):
        x_hat, _ = standardize(pair[row])
        normed = (x_hat * gain[...]).astype(BF16)
        normed_ref[row] = normed
        held[pl.ds(row, heads, stride=row_count), :] = contract(bias_weight[...], normed, 1, 1)
    block = held[...].astype(BF16)
    for peer in range(bias_ref.shape[0]):
        bias_ref[peer] = block
    for copy in copies[3:]:
        copy.wait()


def project_kernel(
    heads,
    place_ref,
    normed_ref,
    proj_weight_ref,
    gate_shift_ref,
    cot_hbm,
    out_weight_hbm,
    narrow_ref,
    wide_ref,
    cot,
    out_weight,
    sems,
):
    row_count, width, channels = cot.shape
    scaling = (channels // heads) ** (-0.5)
    copies = begin_all((cot_hbm, out_weight_hbm), (cot, out_weight), sems)
    length, first_row = place_ref[0], place_ref[1]
    weight_t = proj_weight_ref[...].T
    share = weight_t.shape[0] // row_count
    for row in range(row_count):
        narrow_ref[row, 5 * width + 2 * channels :] = weight_t[row * share : (row + 1) * share]
    weight_t = weight_t[channels : 3 * channels]
    token = lax.broadcasted_iota(jnp.int32, (width, channels), 0)

    def place(row, n, block):
        narrow_ref[row, n * width : (n + 1) * width] = block.astype(BF16)

    def forward(row, carry):
        normed = normed_ref[row]
        projected = dot(normed, proj_weight_ref[...])
        place(row, 0, projected[:, :channels] * scaling)
        place(row, 3, projected[:, channels : 2 * channels])
        place(row, 4, projected[:, 2 * channels : 3 * channels])
        wide_ref[row, :width] = jax.nn.sigmoid(projected[:, 3 * channels :] + gate_shift_ref[...])
        narrow_ref[row, 5 * width : 5 * width + 2 * channels] = contract(
            weight_t, normed, 1, 1
        ).astype(BF16)
        return carry

    def backward(row, carry):
        live = token < jnp.where(first_row + row < length, length, 0)
        d_output = jnp.where(live, cot[row].astype(F32), 0.0).astype(BF16)
        d_mixed = contract(d_output, out_weight[...], 1, 1)
        place(row, 1, d_mixed * wide_ref[row, :width])
        place(row, 2, d_output)
        wide_ref[row, width:] = d_mixed
        return carry

    lax.fori_loop(0, row_count, forward, 0, unroll=UNROLL_PROJECT)
    for copy in copies:
        copy.wait()
    lax.fori_loop(0, row_count, backward, 0, unroll=UNROLL_PROJECT)


def attend_kernel(
    place_ref,
    bias_ref,
    normed_ref,
    narrow_ref,
    wide_ref,
    parts_ref,
    mixed_ref,
    normed_proj_ref,
    shift_ref,
    bias_t,
    bias_sum,
    parts,
    d_proj,
    weight_t,
):
    row_count, width, channels = normed_ref.shape
    heads = bias_t.shape[0] // width
    head_size = channels // heads
    scaling = head_size ** (-0.5)
    length = place_ref[0]
    devices = bias_ref.shape[0]
    key_live = lax.broadcasted_iota(jnp.int32, (width, width), 0) < length
    for h in range(heads):
        rows = [
            bias_ref[d].astype(F32)[h * row_count : (h + 1) * row_count]
            for d in range(devices)
        ]
        turned = jnp.concatenate(rows, 0).T
        bias_t[h * width : (h + 1) * width] = jnp.where(key_live, turned, DEAD)
    bias_sum[...] = jnp.zeros_like(bias_sum)
    lane_masks = head_masks((width, channels), 1, heads)
    share = weight_t.shape[0] // row_count
    for row in range(row_count):
        weight_t[row * share : (row + 1) * share] = narrow_ref[row, 5 * width + 2 * channels :]

    def one_row(row, shift_sum):
        weights, lows, attended_t, d_query_t = [], [], [], []
        queries, d_attend, _, keys, values = (
            narrow_ref[row, n * width : (n + 1) * width] for n in range(5)
        )
        turned = narrow_ref.at[row, 5 * width :]
        scores = contract(stack_heads(keys, lane_masks), queries, 1, 1)
        grads = contract(stack_heads(values, lane_masks), d_attend, 1, 1)
        for h in range(heads):
            part = slice(h * width, (h + 1) * width)
            own = slice(h * head_size, (h + 1) * head_size)
            expo = jnp.exp(scores[part] + bias_t[part])
            probs = expo * (1.0 / jnp.sum(expo, 0, keepdims=True))
            weight = probs.astype(BF16)
            g = grads[part]
            d_scores = probs * (g - jnp.sum(probs * g, 0, keepdims=True))
            bias_sum[part] += d_scores
            low = d_scores.astype(BF16)
            weights.append(weight)
            lows.append(low)
            attended_t.append(dot(turned[channels + own.start : channels + own.stop], weight))
            d_query_t.append(dot(turned[own], low))
        attended = jnp.concatenate(attended_t, 0).T.astype(BF16).astype(F32)
        d_query = jnp.concatenate(d_query_t, 0).T
        d_value = pick_heads(dot(jnp.concatenate(weights, 0), d_attend), lane_masks)
        d_key = pick_heads(dot(jnp.concatenate(lows, 0), queries), lane_masks)
        gating = wide_ref[row, :width]
        mixed = gating * attended
        mixed_ref[row] = mixed.astype(BF16)
        d_gating = (wide_ref[row, width:] * mixed * (1.0 - gating)).astype(BF16)
        d_row = jnp.concatenate(
            [
                (d_query * scaling).astype(BF16),
                d_key.astype(BF16),
                d_value.astype(BF16),
                d_gating,
            ],
            1,
        )
        d_proj[row] = d_row
        normed_proj_ref[row] = dot(d_row, weight_t[...])
        return shift_sum + jnp.sum(d_gating.astype(F32), 0, keepdims=True)

    zero = jnp.zeros((1, channels), F32)
    shift_ref[...] = lax.fori_loop(0, row_count, one_row, zero, unroll=UNROLL_ATTEND)
    shared = heads * row_count
    for h in range(heads):
        turned = bias_sum[h * width : (h + 1) * width].T
        for d in range(devices):
            parts[d, h * row_count : (h + 1) * row_count] = turned[
                d * row_count : (d + 1) * row_count
            ]
    tokens = row_count * width
    normed = normed_ref[...].reshape(tokens, channels)
    grad_proj = contract(normed, d_proj[...].reshape(tokens, 4 * channels), 0, 0)
    grad_out = contract(
        mixed_ref[...].reshape(tokens, channels),
        narrow_ref[:, 2 * width : 3 * width].reshape(tokens, channels),
        0,
        0,
    )
    pieces = [grad_proj[:, i * channels : (i + 1) * channels] for i in range(4)] + [grad_out]
    for d in range(devices):
        for i, piece in enumerate(pieces):
            start = shared + i * row_count
            parts[d, start : start + row_count] = piece[d * row_count : (d + 1) * row_count]
    unused = shared + len(pieces) * row_count
    parts[:, unused:] = jnp.zeros((devices, parts.shape[1] - unused, width), F32)
    parts_ref[...] = parts[...].astype(BF16)


def bias_kernel(
    parts_ref, normed_ref, shift_ref, mixed_ref, normed_proj_ref, bias_grad_ref, sums_ref, held
):
    del mixed_ref, normed_proj_ref
    row_count, width, channels = normed_ref.shape
    shared = bias_grad_ref.shape[0]
    heads = shared // row_count
    total = parts_ref[0].astype(F32)
    for d in range(1, parts_ref.shape[0]):
        total = total + parts_ref[d].astype(F32)
    bias_grad = total[:shared].astype(BF16)
    bias_grad_ref[...] = bias_grad
    bias_grad = bias_grad.astype(F32)
    of_row = lax.broadcasted_iota(jnp.int32, bias_grad.shape, 0) % row_count
    grad_bias = jnp.zeros((shared, channels), F32)
    for row in range(row_count):
        own = jnp.where(of_row == row, bias_grad, 0.0).astype(BF16)
        grad_bias = grad_bias + dot(own, normed_ref[row])
    grads = 5 * row_count
    held[:grads] = total[shared : shared + grads]
    held[grads:] = jnp.zeros((held.shape[0] - grads, channels), F32)
    for h in range(heads):
        held[grads + h : grads + h + 1] = jnp.sum(
            grad_bias[h * row_count : (h + 1) * row_count], 0, keepdims=True
        )
    held[grads + heads : grads + heads + 1] = shift_ref[...]
    block = held[...].astype(BF16)
    for peer in range(sums_ref.shape[0]):
        sums_ref[peer] = block


def finish_kernel(
    place_ref,
    mixed_ref,
    normed_proj_ref,
    bias_grad_ref,
    pair_hbm,
    cot_hbm,
    gain_hbm,
    bias_weight_hbm,
    out_weight_hbm,
    updated_ref,
    pair_grad_ref,
    pair_ref,
    cot_ref,
    gain_ref,
    bias_weight_ref,
    out_weight_ref,
    sems,
):
    copies = begin_all(
        (pair_hbm, cot_hbm, gain_hbm, bias_weight_hbm, out_weight_hbm),
        (pair_ref, cot_ref, gain_ref, bias_weight_ref, out_weight_ref),
        sems,
    )
    row_count, width, channels = pair_ref.shape
    heads = bias_weight_ref.shape[0]
    length, first_row = place_ref[0], place_ref[1]
    token = lax.broadcasted_iota(jnp.int32, (width, channels), 0)
    bias_grad = bias_grad_ref[...].astype(F32)
    of_row = lax.broadcasted_iota(jnp.int32, bias_grad.shape, 0) % row_count
    for copy in copies:
        copy.wait()
    weight = bias_weight_ref[...].astype(F32)
    spread = jnp.concatenate(
        [jnp.broadcast_to(weight[h : h + 1], (row_count, channels)) for h in range(heads)], 0
    ).astype(BF16)
    for row in range(row_count):
        live = token < jnp.where(first_row + row < length, length, 0)
        output = dot(mixed_ref[row], out_weight_ref[...])
        updated_ref[row] = (
            pair_ref[row].astype(F32) + jnp.where(live, output, 0.0)
        ).astype(BF16)
        own = jnp.where(of_row == row, bias_grad, 0.0)
        added = dot(own.T.astype(BF16), spread)
        x_hat, inv_std = standardize(pair_ref[row])
        d_x_hat = (normed_proj_ref[row] + added) * gain_ref[...]
        d_pair = inv_std * (
            d_x_hat
            - jnp.mean(d_x_hat, -1, keepdims=True)
            - x_hat * jnp.mean(d_x_hat * x_hat, -1, keepdims=True)
        )
        pair_grad_ref[row] = (cot_ref[row].astype(F32) + d_pair).astype(BF16)


def sum_kernel(sums_ref, out_ref):
    total = sums_ref[0].astype(F32)
    for d in range(1, sums_ref.shape[0]):
        total = total + sums_ref[d].astype(F32)
    block = total.astype(BF16)
    for peer in range(out_ref.shape[0]):
        out_ref[peer] = block


def assemble_kernel(
    scale,
    blocks_ref,
    proj_weight_ref,
    bias_weight_ref,
    gain_ref,
    grad_proj_ref,
    grad_shift_ref,
    grad_out_ref,
    grad_bias_ref,
    grad_gain_ref,
):
    devices = blocks_ref.shape[0]
    channels = grad_out_ref.shape[0]
    heads = grad_bias_ref.shape[0]
    row_count = channels // devices
    grads = 5 * row_count
    small = None
    by_channel = []
    for d in range(devices):
        block = blocks_ref[d].astype(F32) * scale
        own = slice(d * row_count, (d + 1) * row_count)
        by_lane = None
        for i in range(4):
            columns = slice(i * channels, (i + 1) * channels)
            piece = block[i * row_count : (i + 1) * row_count]
            grad_proj_ref[own, columns] = piece
            term = piece * proj_weight_ref[own, columns].astype(F32)
            by_lane = term if by_lane is None else by_lane + term
        by_channel.append(by_lane)
        grad_out_ref[own] = block[4 * row_count : grads]
        small = block[grads:] if small is None else small + block[grads:]
    grad_bias_ref[...] = small[:heads]
    grad_shift_ref[...] = small[heads : heads + 1]
    gain_sum = jnp.sum(jnp.concatenate(by_channel, 0).T, 0, keepdims=True)
    gain_sum = gain_sum + jnp.sum(
        small[:heads] * bias_weight_ref[...].astype(F32), 0, keepdims=True
    )
    grad_gain_ref[...] = gain_sum / gain_ref[...]


def per_device(
    pair_act, lengths, cotangent, proj_weight, gate_shift, out_weight, bias_weight, norm_gain
):
    pair, cot = pair_act[0], cotangent[0]
    row_count, width, channels = pair.shape
    heads = bias_weight.shape[1]
    gain, bias_weight_t = norm_gain[None], bias_weight.T
    devices, samples = lax.axis_size("dap"), lax.axis_size("dp")
    shared = heads * row_count
    chunk = -(-(5 * row_count + heads + 1) // 16) * 16
    vmem = pl.BlockSpec(memory_space=pltpu.VMEM)
    smem = pl.BlockSpec(memory_space=pltpu.SMEM)
    hbm = pl.BlockSpec(memory_space=pltpu.MemorySpace.HBM)
    rows_shape = (row_count, width, channels)
    line = ((1, channels), F32)

    def away(array):
        return pltpu.with_memory_space_constraint(array, pltpu.MemorySpace.HBM)

    def call(kernel, name, args, outs, scratch=(), placed=False, near=0, sems=0, flops=0, moved=0):
        return pl.pallas_call(
            kernel,
            out_shape=tuple(jax.ShapeDtypeStruct(shape, dtype) for shape, dtype in outs),
            in_specs=[smem] * placed + [vmem] * near + [hbm] * (len(args) - placed - near),
            out_specs=(vmem,) * len(outs),
            scratch_shapes=[pltpu.VMEM(shape, dtype) for shape, dtype in scratch]
            + [pltpu.SemaphoreType.DMA((sems,))] * bool(sems),
            compiler_params=pltpu.CompilerParams(vmem_limit_bytes=VMEM_LIMIT),
            cost_estimate=pl.CostEstimate(flops=flops, bytes_accessed=moved, transcendentals=0),
            name=name,
        )(*args[: placed + near], *(away(a) for a in args[placed + near :]))

    def exchange(blocks, axis):
        return lax.all_to_all(blocks, axis, 0, 0, tiled=True)

    inputs = (pair, gain, bias_weight_t, proj_weight, gate_shift[None])
    normed, bias_copies, near_proj, near_shift = call(
        norm_kernel,
        "norm",
        inputs,
        [
            (rows_shape, BF16),
            ((devices, shared, width), BF16),
            *((a.shape, a.dtype) for a in inputs[3:]),
        ],
        [
            (rows_shape, BF16),
            line,
            (bias_weight_t.shape, BF16),
            ((shared, width), F32),
        ],
        sems=len(inputs),
    )
    bias_all = exchange(bias_copies, "dap")
    place = jnp.stack([lengths[0], lax.axis_index("dap") * row_count]).astype(jnp.int32)
    narrow, wide = call(
        functools.partial(project_kernel, heads),
        "project",
        (place, normed, near_proj, near_shift, cot, out_weight),
        [
            ((row_count, 5 * width + 2 * channels + 4 * channels // row_count, width), BF16),
            ((row_count, 2 * width, channels), F32),
        ],
        [(rows_shape, BF16), (out_weight.shape, BF16)],
        placed=True,
        near=3,
        sems=2,
        flops=3 * 10**9,
        moved=10**7,
    )
    parts, mixed, normed_proj, shift = call(
        attend_kernel,
        "attend",
        (place, bias_all, normed, narrow, wide),
        [
            ((devices, shared + chunk, width), BF16),
            (rows_shape, BF16),
            (rows_shape, F32),
            line,
        ],
        [
            ((heads * width, width), F32),
            ((heads * width, width), F32),
            ((devices, shared + chunk, width), F32),
            ((row_count, width, 4 * channels), BF16),
            ((4 * channels, channels), BF16),
        ],
        placed=True,
        near=4,
    )
    parts = exchange(parts, "dap")
    bias_grad, sums = call(
        bias_kernel,
        "bias_grad",
        (parts, normed, shift, mixed, normed_proj),
        [((shared, width), BF16), ((samples, chunk, channels), BF16)],
        [((chunk, channels), F32)],
        near=5,
    )
    sums = exchange(sums, "dp")
    updated, pair_grad = call(
        finish_kernel,
        "finish",
        (place, mixed, normed_proj, bias_grad, pair, cot, gain, bias_weight_t, out_weight),
        [(rows_shape, BF16), (rows_shape, BF16)],
        [
            (rows_shape, BF16),
            (rows_shape, BF16),
            line,
            (bias_weight_t.shape, BF16),
            (out_weight.shape, BF16),
        ],
        placed=True,
        near=3,
        sems=5,
        flops=2 * 10**9,
        moved=6 * 10**6,
    )
    sums, pair_grad, updated = lax.optimization_barrier((sums, pair_grad, updated))
    (blocks,) = call(
        sum_kernel, "sum", (sums,), [((devices, chunk, channels), BF16)], near=1
    )
    blocks = exchange(blocks, "dap")
    grad_proj, grad_shift, grad_out, grad_bias, grad_gain = call(
        functools.partial(assemble_kernel, 1.0 / width),
        "assemble",
        (blocks, proj_weight, bias_weight_t, gain),
        [
            ((channels, 4 * channels), F32),
            line,
            ((channels, channels), F32),
            ((heads, channels), F32),
            line,
        ],
        near=4,
    )
    return (
        updated[None],
        pair_grad[None],
        grad_proj,
        grad_shift[0],
        grad_out,
        grad_bias.T,
        grad_gain[0],
    )


def solution(mesh):
    rows = P("dp", "dap", None, None)
    return jax.shard_map(
        per_device,
        mesh=mesh,
        in_specs=(rows, P("dp"), rows, P(), P(), P(), P(), P()),
        out_specs=(rows, rows, P(), P(), P(), P(), P()),
        check_vma=False,
    )
```

```python
import functools

import jax
import jax.numpy as jnp
from jax import lax
from jax.experimental import pallas as pl
from jax.experimental.pallas import tpu as pltpu
from jax.sharding import PartitionSpec as P

EPS = 1e-05
DEAD = -1e30
F32 = jnp.float32
BF16 = jnp.bfloat16
VMEM_LIMIT = 16 * 1024 * 1024
PAIR_PIECES = 1
UNROLL_PROJECT = 4
UNROLL_ATTEND = 8


def dot(a, b):
    return jnp.dot(a, b, preferred_element_type=F32)


def contract(a, b, a_axis, b_axis):
    return lax.dot_general(
        a, b, (((a_axis,), (b_axis,)), ((), ())), preferred_element_type=F32
    )


def standardize(rows):
    rows = rows.astype(F32)
    centered = rows - jnp.mean(rows, -1, keepdims=True)
    inv_std = lax.rsqrt(jnp.mean(centered * centered, -1, keepdims=True) + EPS)
    return centered * inv_std, inv_std


def head_masks(shape, axis, heads):
    size = shape[axis] // heads
    position = lax.broadcasted_iota(jnp.int32, shape, axis)
    return [(position >= h * size) & (position < (h + 1) * size) for h in range(heads)]


def stack_heads(block, masks):
    return jnp.concatenate([jnp.where(m, block, jnp.zeros_like(block)) for m in masks], 0)


def pick_heads(stacked, masks):
    size = stacked.shape[0] // len(masks)
    picked = stacked[:size]
    for h in range(1, len(masks)):
        picked = jnp.where(masks[h], stacked[h * size : (h + 1) * size], picked)
    return picked


def begin_all(sources, targets, sems):
    copies = [
        pltpu.make_async_copy(source, target, sems.at[n])
        for n, (source, target) in enumerate(zip(sources, targets, strict=True))
    ]
    for copy in copies:
        copy.start()
    return copies


def norm_kernel(
    pair_hbm,
    gain_hbm,
    bias_weight_hbm,
    proj_weight_hbm,
    gate_shift_hbm,
    normed_ref,
    bias_ref,
    proj_weight_ref,
    gate_shift_ref,
    pair,
    gain,
    bias_weight,
    held,
    sems,
):
    row_count = pair.shape[0]
    heads = bias_weight.shape[0]
    pieces = sems.shape[0] - 4
    step = row_count // pieces
    spans = [slice(n * step, (n + 1) * step) for n in range(pieces)]
    copies = begin_all(
        (gain_hbm, bias_weight_hbm, *(pair_hbm.at[span] for span in spans))
        + (proj_weight_hbm, gate_shift_hbm),
        (gain, bias_weight, *(pair.at[span] for span in spans))
        + (proj_weight_ref, gate_shift_ref),
        sems,
    )
    for copy in copies[:2]:
        copy.wait()
    for row in range(row_count):
        if row % step == 0:
            copies[2 + row // step].wait()
        x_hat, _ = standardize(pair[row])
        normed = (x_hat * gain[...]).astype(BF16)
        normed_ref[row] = normed
        held[pl.ds(row, heads, stride=row_count), :] = contract(bias_weight[...], normed, 1, 1)
    block = held[...].astype(BF16)
    for peer in range(bias_ref.shape[0]):
        bias_ref[peer] = block
    for copy in copies[2 + pieces :]:
        copy.wait()


def project_kernel(
    heads,
    place_ref,
    normed_ref,
    proj_weight_ref,
    gate_shift_ref,
    cot_hbm,
    out_weight_hbm,
    narrow_ref,
    wide_ref,
    cot,
    out_weight,
    sems,
):
    row_count, width, channels = cot.shape
    scaling = (channels // heads) ** (-0.5)
    copies = begin_all((cot_hbm, out_weight_hbm), (cot, out_weight), sems)
    length, first_row = place_ref[0], place_ref[1]
    weight_t = proj_weight_ref[...].T
    share = weight_t.shape[0] // row_count
    for row in range(row_count):
        narrow_ref[row, 5 * width + 2 * channels :] = weight_t[row * share : (row + 1) * share]
    weight_t = weight_t[channels : 3 * channels]
    token = lax.broadcasted_iota(jnp.int32, (width, channels), 0)

    def place(row, n, block):
        narrow_ref[row, n * width : (n + 1) * width] = block.astype(BF16)

    def forward(row, carry):
        normed = normed_ref[row]
        projected = dot(normed, proj_weight_ref[...])
        place(row, 0, projected[:, :channels] * scaling)
        place(row, 3, projected[:, channels : 2 * channels])
        place(row, 4, projected[:, 2 * channels : 3 * channels])
        wide_ref[row, :width] = jax.nn.sigmoid(projected[:, 3 * channels :] + gate_shift_ref[...])
        narrow_ref[row, 5 * width : 5 * width + 2 * channels] = contract(
            weight_t, normed, 1, 1
        ).astype(BF16)
        return carry

    def backward(row, carry):
        live = token < jnp.where(first_row + row < length, length, 0)
        d_output = jnp.where(live, cot[row].astype(F32), 0.0).astype(BF16)
        d_mixed = contract(d_output, out_weight[...], 1, 1)
        place(row, 1, d_mixed * wide_ref[row, :width])
        place(row, 2, d_output)
        wide_ref[row, width:] = d_mixed
        return carry

    lax.fori_loop(0, row_count, forward, 0, unroll=UNROLL_PROJECT)
    for copy in copies:
        copy.wait()
    lax.fori_loop(0, row_count, backward, 0, unroll=UNROLL_PROJECT)


def attend_kernel(
    place_ref,
    bias_ref,
    normed_ref,
    narrow_ref,
    wide_ref,
    parts_ref,
    mixed_ref,
    normed_proj_ref,
    shift_ref,
    bias_t,
    bias_sum,
    parts,
    d_proj,
    weight_t,
):
    row_count, width, channels = normed_ref.shape
    heads = bias_t.shape[0] // width
    head_size = channels // heads
    scaling = head_size ** (-0.5)
    length = place_ref[0]
    devices = bias_ref.shape[0]
    key_live = lax.broadcasted_iota(jnp.int32, (width, width), 0) < length
    for h in range(heads):
        rows = [
            bias_ref[d].astype(F32)[h * row_count : (h + 1) * row_count]
            for d in range(devices)
        ]
        turned = jnp.concatenate(rows, 0).T
        bias_t[h * width : (h + 1) * width] = jnp.where(key_live, turned, DEAD)
    bias_sum[...] = jnp.zeros_like(bias_sum)
    lane_masks = head_masks((width, channels), 1, heads)
    share = weight_t.shape[0] // row_count
    for row in range(row_count):
        weight_t[row * share : (row + 1) * share] = narrow_ref[row, 5 * width + 2 * channels :]

    def one_row(row, shift_sum):
        weights, lows, attended_t, d_query_t = [], [], [], []
        queries, d_attend, _, keys, values = (
            narrow_ref[row, n * width : (n + 1) * width] for n in range(5)
        )
        turned = narrow_ref.at[row, 5 * width :]
        scores = contract(stack_heads(keys, lane_masks), queries, 1, 1)
        grads = contract(stack_heads(values, lane_masks), d_attend, 1, 1)
        for h in range(heads):
            part = slice(h * width, (h + 1) * width)
            own = slice(h * head_size, (h + 1) * head_size)
            expo = jnp.exp(scores[part] + bias_t[part])
            probs = expo * (1.0 / jnp.sum(expo, 0, keepdims=True))
            weight = probs.astype(BF16)
            g = grads[part]
            d_scores = probs * (g - jnp.sum(probs * g, 0, keepdims=True))
            bias_sum[part] += d_scores
            low = d_scores.astype(BF16)
            weights.append(weight)
            lows.append(low)
            attended_t.append(dot(turned[channels + own.start : channels + own.stop], weight))
            d_query_t.append(dot(turned[own], low))
        attended = jnp.concatenate(attended_t, 0).T.astype(BF16).astype(F32)
        d_query = jnp.concatenate(d_query_t, 0).T
        d_value = pick_heads(dot(jnp.concatenate(weights, 0), d_attend), lane_masks)
        d_key = pick_heads(dot(jnp.concatenate(lows, 0), queries), lane_masks)
        gating = wide_ref[row, :width]
        mixed = gating * attended
        mixed_ref[row] = mixed.astype(BF16)
        d_gating = (wide_ref[row, width:] * mixed * (1.0 - gating)).astype(BF16)
        d_row = jnp.concatenate(
            [
                (d_query * scaling).astype(BF16),
                d_key.astype(BF16),
                d_value.astype(BF16),
                d_gating,
            ],
            1,
        )
        d_proj[row] = d_row
        normed_proj_ref[row] = dot(d_row, weight_t[...])
        return shift_sum + jnp.sum(d_gating.astype(F32), 0, keepdims=True)

    zero = jnp.zeros((1, channels), F32)
    shift_ref[...] = lax.fori_loop(0, row_count, one_row, zero, unroll=UNROLL_ATTEND)
    shared = heads * row_count
    for h in range(heads):
        turned = bias_sum[h * width : (h + 1) * width].T
        for d in range(devices):
            parts[d, h * row_count : (h + 1) * row_count] = turned[
                d * row_count : (d + 1) * row_count
            ]
    tokens = row_count * width
    normed = normed_ref[...].reshape(tokens, channels)
    grad_proj = contract(normed, d_proj[...].reshape(tokens, 4 * channels), 0, 0)
    grad_out = contract(
        mixed_ref[...].reshape(tokens, channels),
        narrow_ref[:, 2 * width : 3 * width].reshape(tokens, channels),
        0,
        0,
    )
    pieces = [grad_proj[:, i * channels : (i + 1) * channels] for i in range(4)] + [grad_out]
    for d in range(devices):
        for i, piece in enumerate(pieces):
            start = shared + i * row_count
            parts[d, start : start + row_count] = piece[d * row_count : (d + 1) * row_count]
    unused = shared + len(pieces) * row_count
    parts[:, unused:] = jnp.zeros((devices, parts.shape[1] - unused, width), F32)
    parts_ref[...] = parts[...].astype(BF16)


def bias_kernel(
    parts_ref, normed_ref, shift_ref, mixed_ref, normed_proj_ref, bias_grad_ref, held
):
    del mixed_ref, normed_proj_ref
    row_count, width, channels = normed_ref.shape
    shared = bias_grad_ref.shape[0]
    heads = shared // row_count
    total = parts_ref[0].astype(F32)
    for d in range(1, parts_ref.shape[0]):
        total = total + parts_ref[d].astype(F32)
    bias_grad = total[:shared].astype(BF16)
    bias_grad_ref[...] = bias_grad
    bias_grad = bias_grad.astype(F32)
    of_row = lax.broadcasted_iota(jnp.int32, bias_grad.shape, 0) % row_count
    grad_bias = jnp.zeros((shared, channels), F32)
    for row in range(row_count):
        own = jnp.where(of_row == row, bias_grad, 0.0).astype(BF16)
        grad_bias = grad_bias + dot(own, normed_ref[row])
    grads = 5 * row_count
    held[:grads] = total[shared : shared + grads]
    held[grads:] = jnp.zeros((held.shape[0] - grads, channels), F32)
    for h in range(heads):
        held[grads + h : grads + h + 1] = jnp.sum(
            grad_bias[h * row_count : (h + 1) * row_count], 0, keepdims=True
        )
    held[grads + heads : grads + heads + 1] = shift_ref[...]


def pair_kernel(own_ref, other_ref, sums_ref):
    block = (own_ref[...] + other_ref[...]).astype(BF16)
    for peer in range(sums_ref.shape[0]):
        sums_ref[peer] = block


def finish_kernel(
    place_ref,
    bias_grad_ref,
    mixed_hbm,
    normed_proj_hbm,
    pair_hbm,
    cot_hbm,
    gain_hbm,
    bias_weight_hbm,
    out_weight_hbm,
    updated_ref,
    pair_grad_ref,
    pair_ref,
    cot_ref,
    gain_ref,
    bias_weight_ref,
    out_weight_ref,
    mixed_ref,
    normed_proj_ref,
    sems,
):
    copies = begin_all(
        (
            pair_hbm,
            cot_hbm,
            gain_hbm,
            bias_weight_hbm,
            out_weight_hbm,
            mixed_hbm,
            normed_proj_hbm,
        ),
        (
            pair_ref,
            cot_ref,
            gain_ref,
            bias_weight_ref,
            out_weight_ref,
            mixed_ref,
            normed_proj_ref,
        ),
        sems,
    )
    row_count, width, channels = pair_ref.shape
    heads = bias_weight_ref.shape[0]
    length, first_row = place_ref[0], place_ref[1]
    token = lax.broadcasted_iota(jnp.int32, (width, channels), 0)
    bias_grad = bias_grad_ref[...].astype(F32)
    of_row = lax.broadcasted_iota(jnp.int32, bias_grad.shape, 0) % row_count
    for copy in copies:
        copy.wait()
    weight = bias_weight_ref[...].astype(F32)
    spread = jnp.concatenate(
        [jnp.broadcast_to(weight[h : h + 1], (row_count, channels)) for h in range(heads)], 0
    ).astype(BF16)
    for row in range(row_count):
        live = token < jnp.where(first_row + row < length, length, 0)
        output = dot(mixed_ref[row], out_weight_ref[...])
        updated_ref[row] = (
            pair_ref[row].astype(F32) + jnp.where(live, output, 0.0)
        ).astype(BF16)
        own = jnp.where(of_row == row, bias_grad, 0.0)
        added = dot(own.T.astype(BF16), spread)
        x_hat, inv_std = standardize(pair_ref[row])
        d_x_hat = (normed_proj_ref[row] + added) * gain_ref[...]
        d_pair = inv_std * (
            d_x_hat
            - jnp.mean(d_x_hat, -1, keepdims=True)
            - x_hat * jnp.mean(d_x_hat * x_hat, -1, keepdims=True)
        )
        pair_grad_ref[row] = (cot_ref[row].astype(F32) + d_pair).astype(BF16)


def sum_kernel(sums_ref, out_ref):
    total = sums_ref[0].astype(F32)
    for d in range(1, sums_ref.shape[0]):
        total = total + sums_ref[d].astype(F32)
    block = total.astype(BF16)
    for peer in range(out_ref.shape[0]):
        out_ref[peer] = block


def assemble_kernel(
    scale,
    blocks_ref,
    proj_weight_ref,
    bias_weight_ref,
    gain_ref,
    grad_proj_ref,
    grad_shift_ref,
    grad_out_ref,
    grad_bias_ref,
    grad_gain_ref,
):
    devices = blocks_ref.shape[0]
    channels = grad_out_ref.shape[0]
    heads = grad_bias_ref.shape[0]
    row_count = channels // devices
    grads = 5 * row_count
    small = None
    by_channel = []
    for d in range(devices):
        block = blocks_ref[d].astype(F32) * scale
        own = slice(d * row_count, (d + 1) * row_count)
        by_lane = None
        for i in range(4):
            columns = slice(i * channels, (i + 1) * channels)
            piece = block[i * row_count : (i + 1) * row_count]
            grad_proj_ref[own, columns] = piece
            term = piece * proj_weight_ref[own, columns].astype(F32)
            by_lane = term if by_lane is None else by_lane + term
        by_channel.append(by_lane)
        grad_out_ref[own] = block[4 * row_count : grads]
        small = block[grads:] if small is None else small + block[grads:]
    grad_bias_ref[...] = small[:heads]
    grad_shift_ref[...] = small[heads : heads + 1]
    gain_sum = jnp.sum(jnp.concatenate(by_channel, 0).T, 0, keepdims=True)
    gain_sum = gain_sum + jnp.sum(
        small[:heads] * bias_weight_ref[...].astype(F32), 0, keepdims=True
    )
    grad_gain_ref[...] = gain_sum / gain_ref[...]


def per_device(
    pair_act, lengths, cotangent, proj_weight, gate_shift, out_weight, bias_weight, norm_gain
):
    pair, cot = pair_act[0], cotangent[0]
    row_count, width, channels = pair.shape
    heads = bias_weight.shape[1]
    gain, bias_weight_t = norm_gain[None], bias_weight.T
    devices, samples = lax.axis_size("dap"), lax.axis_size("dp")
    shared = heads * row_count
    chunk = -(-(5 * row_count + heads + 1) // 16) * 16
    vmem = pl.BlockSpec(memory_space=pltpu.VMEM)
    smem = pl.BlockSpec(memory_space=pltpu.SMEM)
    hbm = pl.BlockSpec(memory_space=pltpu.MemorySpace.HBM)
    rows_shape = (row_count, width, channels)
    line = ((1, channels), F32)

    def away(array):
        return pltpu.with_memory_space_constraint(array, pltpu.MemorySpace.HBM)

    def call(kernel, name, args, outs, scratch=(), placed=False, near=0, sems=0, flops=0, moved=0):
        return pl.pallas_call(
            kernel,
            out_shape=tuple(jax.ShapeDtypeStruct(shape, dtype) for shape, dtype in outs),
            in_specs=[smem] * placed + [vmem] * near + [hbm] * (len(args) - placed - near),
            out_specs=(vmem,) * len(outs),
            scratch_shapes=[pltpu.VMEM(shape, dtype) for shape, dtype in scratch]
            + [pltpu.SemaphoreType.DMA((sems,))] * bool(sems),
            compiler_params=pltpu.CompilerParams(vmem_limit_bytes=VMEM_LIMIT),
            cost_estimate=pl.CostEstimate(flops=flops, bytes_accessed=moved, transcendentals=0),
            name=name,
        )(*args[: placed + near], *(away(a) for a in args[placed + near :]))

    def exchange(blocks, axis, groups=None):
        return lax.all_to_all(blocks, axis, 0, 0, axis_index_groups=groups, tiled=True)

    inputs = (pair, gain, bias_weight_t, proj_weight, gate_shift[None])
    normed, bias_copies, near_proj, near_shift = call(
        norm_kernel,
        "norm",
        inputs,
        [
            (rows_shape, BF16),
            ((devices, shared, width), BF16),
            *((a.shape, a.dtype) for a in inputs[3:]),
        ],
        [
            (rows_shape, BF16),
            line,
            (bias_weight_t.shape, BF16),
            ((shared, width), F32),
        ],
        sems=len(inputs) - 1 + PAIR_PIECES,
    )
    bias_all = exchange(bias_copies, "dap")
    place = jnp.stack([lengths[0], lax.axis_index("dap") * row_count]).astype(jnp.int32)
    narrow, wide = call(
        functools.partial(project_kernel, heads),
        "project",
        (place, normed, near_proj, near_shift, cot, out_weight),
        [
            ((row_count, 5 * width + 2 * channels + 4 * channels // row_count, width), BF16),
            ((row_count, 2 * width, channels), F32),
        ],
        [(rows_shape, BF16), (out_weight.shape, BF16)],
        placed=True,
        near=3,
        sems=2,
        flops=3 * 10**9,
        moved=10**7,
    )
    parts, mixed, normed_proj, shift = call(
        attend_kernel,
        "attend",
        (place, bias_all, normed, narrow, wide),
        [
            ((devices, shared + chunk, width), BF16),
            (rows_shape, BF16),
            (rows_shape, F32),
            line,
        ],
        [
            ((heads * width, width), F32),
            ((heads * width, width), F32),
            ((devices, shared + chunk, width), F32),
            ((row_count, width, 4 * channels), BF16),
            ((4 * channels, channels), BF16),
        ],
        placed=True,
        near=4,
    )
    parts = exchange(parts, "dap")
    bias_grad, own = call(
        bias_kernel,
        "bias_grad",
        (parts, normed, shift, mixed, normed_proj),
        [((shared, width), BF16), ((chunk, channels), F32)],
        near=5,
    )
    other = lax.ppermute(own, "dp", [(n, n ^ 1) for n in range(samples)])
    bias_grad, other = lax.optimization_barrier((bias_grad, other))
    (sums,) = call(
        pair_kernel,
        "pair",
        (own, other),
        [((samples // 2, chunk, channels), BF16)],
        near=2,
    )
    same_core = [list(range(core, samples, 2)) for core in range(2)]
    sums = exchange(sums, "dp", same_core)
    updated, pair_grad = call(
        finish_kernel,
        "finish",
        (place, bias_grad, mixed, normed_proj, pair, cot, gain, bias_weight_t, out_weight),
        [(rows_shape, BF16), (rows_shape, BF16)],
        [
            (rows_shape, BF16),
            (rows_shape, BF16),
            line,
            (bias_weight_t.shape, BF16),
            (out_weight.shape, BF16),
            (rows_shape, BF16),
            (rows_shape, F32),
        ],
        placed=True,
        near=1,
        sems=7,
        flops=2 * 10**9,
        moved=6 * 10**6,
    )
    sums, pair_grad, updated = lax.optimization_barrier((sums, pair_grad, updated))
    (blocks,) = call(
        sum_kernel, "sum", (sums,), [((devices, chunk, channels), BF16)], near=1
    )
    blocks = exchange(blocks, "dap")
    grad_proj, grad_shift, grad_out, grad_bias, grad_gain = call(
        functools.partial(assemble_kernel, 1.0 / width),
        "assemble",
        (blocks, proj_weight, bias_weight_t, gain),
        [
            ((channels, 4 * channels), F32),
            line,
            ((channels, channels), F32),
            ((heads, channels), F32),
            line,
        ],
        near=4,
    )
    return (
        updated[None],
        pair_grad[None],
        grad_proj,
        grad_shift[0],
        grad_out,
        grad_bias.T,
        grad_gain[0],
    )


def solution(mesh):
    rows = P("dp", "dap", None, None)
    return jax.shard_map(
        per_device,
        mesh=mesh,
        in_specs=(rows, P("dp"), rows, P(), P(), P(), P(), P()),
        out_specs=(rows, rows, P(), P(), P(), P(), P()),
        check_vma=False,
    )
```

```python
import functools

import jax
import jax.numpy as jnp
from jax import lax
from jax.experimental import pallas as pl
from jax.experimental.pallas import tpu as pltpu
from jax.sharding import PartitionSpec as P

EPS = 1e-05
DEAD = -1e30
F32 = jnp.float32
BF16 = jnp.bfloat16
VMEM_LIMIT = 16 * 1024 * 1024
UNROLL_PROJECT = 4
UNROLL_ATTEND = 8


def dot(a, b):
    return jnp.dot(a, b, preferred_element_type=F32)


def contract(a, b, a_axis, b_axis):
    return lax.dot_general(
        a, b, (((a_axis,), (b_axis,)), ((), ())), preferred_element_type=F32
    )


def standardize(rows):
    rows = rows.astype(F32)
    centered = rows - jnp.mean(rows, -1, keepdims=True)
    inv_std = lax.rsqrt(jnp.mean(centered * centered, -1, keepdims=True) + EPS)
    return centered * inv_std, inv_std


def head_masks(shape, axis, heads):
    size = shape[axis] // heads
    position = lax.broadcasted_iota(jnp.int32, shape, axis)
    return [(position >= h * size) & (position < (h + 1) * size) for h in range(heads)]


def stack_heads(block, masks):
    return jnp.concatenate([jnp.where(m, block, jnp.zeros_like(block)) for m in masks], 0)


def pick_heads(stacked, masks):
    size = stacked.shape[0] // len(masks)
    picked = stacked[:size]
    for h in range(1, len(masks)):
        picked = jnp.where(masks[h], stacked[h * size : (h + 1) * size], picked)
    return picked


def begin_all(sources, targets, sems):
    copies = [
        pltpu.make_async_copy(source, target, sems.at[n])
        for n, (source, target) in enumerate(zip(sources, targets, strict=True))
    ]
    for copy in copies:
        copy.start()
    return copies


def norm_kernel(
    pair_hbm,
    gain_hbm,
    bias_weight_hbm,
    proj_weight_hbm,
    gate_shift_hbm,
    normed_ref,
    bias_ref,
    proj_weight_ref,
    gate_shift_ref,
    pair,
    gain,
    bias_weight,
    held,
    sems,
):
    row_count = pair.shape[0]
    heads = bias_weight.shape[0]
    copies = begin_all(
        (gain_hbm, bias_weight_hbm, pair_hbm, proj_weight_hbm, gate_shift_hbm),
        (gain, bias_weight, pair, proj_weight_ref, gate_shift_ref),
        sems,
    )
    for copy in copies[:3]:
        copy.wait()
    for row in range(row_count):
        x_hat, _ = standardize(pair[row])
        normed = (x_hat * gain[...]).astype(BF16)
        normed_ref[row] = normed
        held[pl.ds(row, heads, stride=row_count), :] = contract(bias_weight[...], normed, 1, 1)
    block = held[...].astype(BF16)
    for peer in range(bias_ref.shape[0]):
        bias_ref[peer] = block
    for copy in copies[3:]:
        copy.wait()


def project_kernel(
    heads,
    place_ref,
    normed_ref,
    proj_weight_ref,
    gate_shift_ref,
    cot_hbm,
    out_weight_hbm,
    narrow_ref,
    wide_ref,
    cot,
    out_weight,
    sems,
):
    row_count, width, channels = cot.shape
    scaling = (channels // heads) ** (-0.5)
    copies = begin_all((cot_hbm, out_weight_hbm), (cot, out_weight), sems)
    length, first_row = place_ref[0], place_ref[1]
    weight_t = proj_weight_ref[...].T
    share = weight_t.shape[0] // row_count
    for row in range(row_count):
        narrow_ref[row, 5 * width + 2 * channels :] = weight_t[row * share : (row + 1) * share]
    weight_t = weight_t[channels : 3 * channels]
    token = lax.broadcasted_iota(jnp.int32, (width, channels), 0)

    def place(row, n, block):
        narrow_ref[row, n * width : (n + 1) * width] = block.astype(BF16)

    def forward(row, carry):
        normed = normed_ref[row]
        projected = dot(normed, proj_weight_ref[...])
        place(row, 0, projected[:, :channels] * scaling)
        place(row, 3, projected[:, channels : 2 * channels])
        place(row, 4, projected[:, 2 * channels : 3 * channels])
        wide_ref[row, :width] = jax.nn.sigmoid(projected[:, 3 * channels :] + gate_shift_ref[...])
        narrow_ref[row, 5 * width : 5 * width + 2 * channels] = contract(
            weight_t, normed, 1, 1
        ).astype(BF16)
        return carry

    def backward(row, carry):
        live = token < jnp.where(first_row + row < length, length, 0)
        d_output = jnp.where(live, cot[row].astype(F32), 0.0).astype(BF16)
        d_mixed = contract(d_output, out_weight[...], 1, 1)
        place(row, 1, d_mixed * wide_ref[row, :width])
        place(row, 2, d_output)
        wide_ref[row, width:] = d_mixed
        return carry

    lax.fori_loop(0, row_count, forward, 0, unroll=UNROLL_PROJECT)
    for copy in copies:
        copy.wait()
    lax.fori_loop(0, row_count, backward, 0, unroll=UNROLL_PROJECT)


def attend_kernel(
    place_ref,
    bias_ref,
    normed_ref,
    narrow_ref,
    wide_ref,
    parts_ref,
    mixed_ref,
    normed_proj_ref,
    shift_ref,
    bias_t,
    bias_sum,
    parts,
    d_proj,
    weight_t,
):
    row_count, width, channels = normed_ref.shape
    heads = bias_t.shape[0] // width
    head_size = channels // heads
    scaling = head_size ** (-0.5)
    length = place_ref[0]
    devices = bias_ref.shape[0]
    key_live = lax.broadcasted_iota(jnp.int32, (width, width), 0) < length
    for h in range(heads):
        rows = [
            bias_ref[d].astype(F32)[h * row_count : (h + 1) * row_count]
            for d in range(devices)
        ]
        turned = jnp.concatenate(rows, 0).T
        bias_t[h * width : (h + 1) * width] = jnp.where(key_live, turned, DEAD)
    bias_sum[...] = jnp.zeros_like(bias_sum)
    lane_masks = head_masks((width, channels), 1, heads)
    share = weight_t.shape[0] // row_count
    for row in range(row_count):
        weight_t[row * share : (row + 1) * share] = narrow_ref[row, 5 * width + 2 * channels :]

    def one_row(row, shift_sum):
        weights, lows, attended_t, d_query_t = [], [], [], []
        queries, d_attend, _, keys, values = (
            narrow_ref[row, n * width : (n + 1) * width] for n in range(5)
        )
        turned = narrow_ref.at[row, 5 * width :]
        scores = contract(stack_heads(keys, lane_masks), queries, 1, 1)
        grads = contract(stack_heads(values, lane_masks), d_attend, 1, 1)
        for h in range(heads):
            part = slice(h * width, (h + 1) * width)
            own = slice(h * head_size, (h + 1) * head_size)
            expo = jnp.exp(scores[part] + bias_t[part])
            probs = expo * (1.0 / jnp.sum(expo, 0, keepdims=True))
            weight = probs.astype(BF16)
            g = grads[part]
            d_scores = probs * (g - jnp.sum(probs * g, 0, keepdims=True))
            bias_sum[part] += d_scores
            low = d_scores.astype(BF16)
            weights.append(weight)
            lows.append(low)
            attended_t.append(dot(turned[channels + own.start : channels + own.stop], weight))
            d_query_t.append(dot(turned[own], low))
        attended = jnp.concatenate(attended_t, 0).T.astype(BF16).astype(F32)
        d_query = jnp.concatenate(d_query_t, 0).T
        d_value = pick_heads(dot(jnp.concatenate(weights, 0), d_attend), lane_masks)
        d_key = pick_heads(dot(jnp.concatenate(lows, 0), queries), lane_masks)
        gating = wide_ref[row, :width]
        mixed = gating * attended
        mixed_ref[row] = mixed.astype(BF16)
        d_gating = (wide_ref[row, width:] * mixed * (1.0 - gating)).astype(BF16)
        d_row = jnp.concatenate(
            [
                (d_query * scaling).astype(BF16),
                d_key.astype(BF16),
                d_value.astype(BF16),
                d_gating,
            ],
            1,
        )
        d_proj[row] = d_row
        return shift_sum + jnp.sum(d_gating.astype(F32), 0, keepdims=True)

    zero = jnp.zeros((1, channels), F32)
    shift_ref[...] = lax.fori_loop(0, row_count, one_row, zero, unroll=UNROLL_ATTEND)
    flat = d_proj[...].reshape(row_count * width, 4 * channels)
    normed_proj_ref[...] = dot(flat, weight_t[...]).reshape(normed_proj_ref.shape)
    shared = heads * row_count
    for h in range(heads):
        turned = bias_sum[h * width : (h + 1) * width].T
        for d in range(devices):
            parts[d, h * row_count : (h + 1) * row_count] = turned[
                d * row_count : (d + 1) * row_count
            ]
    tokens = row_count * width
    normed = normed_ref[...].reshape(tokens, channels)
    grad_proj = contract(normed, flat, 0, 0)
    grad_out = contract(
        mixed_ref[...].reshape(tokens, channels),
        narrow_ref[:, 2 * width : 3 * width].reshape(tokens, channels),
        0,
        0,
    )
    pieces = [grad_proj[:, i * channels : (i + 1) * channels] for i in range(4)] + [grad_out]
    for d in range(devices):
        for i, piece in enumerate(pieces):
            start = shared + i * row_count
            parts[d, start : start + row_count] = piece[d * row_count : (d + 1) * row_count]
    parts_ref[...] = parts[...].astype(BF16)


def bias_kernel(
    parts_ref, normed_ref, shift_ref, mixed_ref, normed_proj_ref, bias_grad_ref, held
):
    del mixed_ref, normed_proj_ref
    row_count, width, channels = normed_ref.shape
    shared = bias_grad_ref.shape[0]
    heads = shared // row_count
    total = parts_ref[0].astype(F32)
    for d in range(1, parts_ref.shape[0]):
        total = total + parts_ref[d].astype(F32)
    bias_grad = total[:shared].astype(BF16)
    bias_grad_ref[...] = bias_grad
    bias_grad = bias_grad.astype(F32)
    of_row = lax.broadcasted_iota(jnp.int32, bias_grad.shape, 0) % row_count
    grad_bias = jnp.zeros((shared, channels), F32)
    for row in range(row_count):
        own = jnp.where(of_row == row, bias_grad, 0.0).astype(BF16)
        grad_bias = grad_bias + dot(own, normed_ref[row])
    grads = 5 * row_count
    held[:grads] = total[shared : shared + grads]
    held[grads:] = jnp.zeros((held.shape[0] - grads, channels), F32)
    for h in range(heads):
        held[grads + h : grads + h + 1] = jnp.sum(
            grad_bias[h * row_count : (h + 1) * row_count], 0, keepdims=True
        )
    held[grads + heads : grads + heads + 1] = shift_ref[...]


def pair_kernel(own_ref, other_ref, sums_ref):
    block = (own_ref[...] + other_ref[...]).astype(BF16)
    for peer in range(sums_ref.shape[0]):
        sums_ref[peer] = block


def finish_kernel(
    place_ref,
    bias_grad_ref,
    mixed_hbm,
    normed_proj_hbm,
    pair_hbm,
    cot_hbm,
    gain_hbm,
    bias_weight_hbm,
    out_weight_hbm,
    updated_ref,
    pair_grad_ref,
    pair_ref,
    cot_ref,
    gain_ref,
    bias_weight_ref,
    out_weight_ref,
    mixed_ref,
    normed_proj_ref,
    sems,
):
    copies = begin_all(
        (
            pair_hbm,
            cot_hbm,
            gain_hbm,
            bias_weight_hbm,
            out_weight_hbm,
            mixed_hbm,
            normed_proj_hbm,
        ),
        (
            pair_ref,
            cot_ref,
            gain_ref,
            bias_weight_ref,
            out_weight_ref,
            mixed_ref,
            normed_proj_ref,
        ),
        sems,
    )
    row_count, width, channels = pair_ref.shape
    heads = bias_weight_ref.shape[0]
    length, first_row = place_ref[0], place_ref[1]
    token = lax.broadcasted_iota(jnp.int32, (width, channels), 0)
    bias_grad = bias_grad_ref[...].astype(F32)
    of_row = lax.broadcasted_iota(jnp.int32, bias_grad.shape, 0) % row_count
    for copy in copies:
        copy.wait()
    weight = bias_weight_ref[...].astype(F32)
    spread = jnp.concatenate(
        [jnp.broadcast_to(weight[h : h + 1], (row_count, channels)) for h in range(heads)], 0
    ).astype(BF16)
    for row in range(row_count):
        live = token < jnp.where(first_row + row < length, length, 0)
        output = dot(mixed_ref[row], out_weight_ref[...])
        updated_ref[row] = (
            pair_ref[row].astype(F32) + jnp.where(live, output, 0.0)
        ).astype(BF16)
        own = jnp.where(of_row == row, bias_grad, 0.0)
        added = dot(own.T.astype(BF16), spread)
        x_hat, inv_std = standardize(pair_ref[row])
        d_x_hat = (normed_proj_ref[row] + added) * gain_ref[...]
        d_pair = inv_std * (
            d_x_hat
            - jnp.mean(d_x_hat, -1, keepdims=True)
            - x_hat * jnp.mean(d_x_hat * x_hat, -1, keepdims=True)
        )
        pair_grad_ref[row] = (cot_ref[row].astype(F32) + d_pair).astype(BF16)


def sum_kernel(sums_ref, out_ref):
    total = sums_ref[0].astype(F32)
    for d in range(1, sums_ref.shape[0]):
        total = total + sums_ref[d].astype(F32)
    block = total.astype(BF16)
    for peer in range(out_ref.shape[0]):
        out_ref[peer] = block


def assemble_kernel(
    scale,
    blocks_ref,
    proj_weight_ref,
    bias_weight_ref,
    gain_ref,
    grad_proj_ref,
    grad_shift_ref,
    grad_out_ref,
    grad_bias_ref,
    grad_gain_ref,
):
    devices = blocks_ref.shape[0]
    channels = grad_out_ref.shape[0]
    heads = grad_bias_ref.shape[0]
    row_count = channels // devices
    grads = 5 * row_count
    small = None
    by_channel = []
    for d in range(devices):
        block = blocks_ref[d].astype(F32) * scale
        own = slice(d * row_count, (d + 1) * row_count)
        by_lane = None
        for i in range(4):
            columns = slice(i * channels, (i + 1) * channels)
            piece = block[i * row_count : (i + 1) * row_count]
            grad_proj_ref[own, columns] = piece
            term = piece * proj_weight_ref[own, columns].astype(F32)
            by_lane = term if by_lane is None else by_lane + term
        by_channel.append(by_lane)
        grad_out_ref[own] = block[4 * row_count : grads]
        small = block[grads:] if small is None else small + block[grads:]
    grad_bias_ref[...] = small[:heads]
    grad_shift_ref[...] = small[heads : heads + 1]
    gain_sum = jnp.sum(jnp.concatenate(by_channel, 0).T, 0, keepdims=True)
    gain_sum = gain_sum + jnp.sum(
        small[:heads] * bias_weight_ref[...].astype(F32), 0, keepdims=True
    )
    grad_gain_ref[...] = gain_sum / gain_ref[...]


def per_device(
    pair_act, lengths, cotangent, proj_weight, gate_shift, out_weight, bias_weight, norm_gain
):
    pair, cot = pair_act[0], cotangent[0]
    row_count, width, channels = pair.shape
    heads = bias_weight.shape[1]
    gain, bias_weight_t = norm_gain[None], bias_weight.T
    devices, samples = lax.axis_size("dap"), lax.axis_size("dp")
    shared = heads * row_count
    chunk = -(-(5 * row_count + heads + 1) // 16) * 16
    vmem = pl.BlockSpec(memory_space=pltpu.VMEM)
    smem = pl.BlockSpec(memory_space=pltpu.SMEM)
    hbm = pl.BlockSpec(memory_space=pltpu.MemorySpace.HBM)
    rows_shape = (row_count, width, channels)
    line = ((1, channels), F32)

    def away(array):
        return pltpu.with_memory_space_constraint(array, pltpu.MemorySpace.HBM)

    def call(kernel, name, args, outs, scratch=(), placed=False, near=0, sems=0, flops=0, moved=0):
        return pl.pallas_call(
            kernel,
            out_shape=tuple(jax.ShapeDtypeStruct(shape, dtype) for shape, dtype in outs),
            in_specs=[smem] * placed + [vmem] * near + [hbm] * (len(args) - placed - near),
            out_specs=(vmem,) * len(outs),
            scratch_shapes=[pltpu.VMEM(shape, dtype) for shape, dtype in scratch]
            + [pltpu.SemaphoreType.DMA((sems,))] * bool(sems),
            compiler_params=pltpu.CompilerParams(vmem_limit_bytes=VMEM_LIMIT),
            cost_estimate=pl.CostEstimate(flops=flops, bytes_accessed=moved, transcendentals=0),
            name=name,
        )(*args[: placed + near], *(away(a) for a in args[placed + near :]))

    def exchange(blocks, axis, groups=None):
        return lax.all_to_all(blocks, axis, 0, 0, axis_index_groups=groups, tiled=True)

    inputs = (pair, gain, bias_weight_t, proj_weight, gate_shift[None])
    normed, bias_copies, near_proj, near_shift = call(
        norm_kernel,
        "norm",
        inputs,
        [
            (rows_shape, BF16),
            ((devices, shared, width), BF16),
            *((a.shape, a.dtype) for a in inputs[3:]),
        ],
        [
            (rows_shape, BF16),
            line,
            (bias_weight_t.shape, BF16),
            ((shared, width), F32),
        ],
        sems=len(inputs),
    )
    bias_all = exchange(bias_copies, "dap")
    place = jnp.stack([lengths[0], lax.axis_index("dap") * row_count]).astype(jnp.int32)
    narrow, wide = call(
        functools.partial(project_kernel, heads),
        "project",
        (place, normed, near_proj, near_shift, cot, out_weight),
        [
            ((row_count, 5 * width + 2 * channels + 4 * channels // row_count, width), BF16),
            ((row_count, 2 * width, channels), F32),
        ],
        [(rows_shape, BF16), (out_weight.shape, BF16)],
        placed=True,
        near=3,
        sems=2,
        flops=3 * 10**9,
        moved=10**7,
    )
    parts, mixed, normed_proj, shift = call(
        attend_kernel,
        "attend",
        (place, bias_all, normed, narrow, wide),
        [
            ((devices, shared + 5 * row_count, width), BF16),
            (rows_shape, BF16),
            (rows_shape, F32),
            line,
        ],
        [
            ((heads * width, width), F32),
            ((heads * width, width), F32),
            ((devices, shared + 5 * row_count, width), F32),
            ((row_count, width, 4 * channels), BF16),
            ((4 * channels, channels), BF16),
        ],
        placed=True,
        near=4,
    )
    parts = exchange(parts, "dap")
    bias_grad, own = call(
        bias_kernel,
        "bias_grad",
        (parts, normed, shift, mixed, normed_proj),
        [((shared, width), BF16), ((chunk, channels), F32)],
        near=5,
    )
    other = lax.ppermute(own, "dp", [(n, n ^ 1) for n in range(samples)])
    bias_grad, other = lax.optimization_barrier((bias_grad, other))
    (sums,) = call(
        pair_kernel,
        "pair",
        (own, other),
        [((samples // 2, chunk, channels), BF16)],
        near=2,
    )
    same_core = [list(range(core, samples, 2)) for core in range(2)]
    sums = exchange(sums, "dp", same_core)
    updated, pair_grad = call(
        finish_kernel,
        "finish",
        (place, bias_grad, mixed, normed_proj, pair, cot, gain, bias_weight_t, out_weight),
        [(rows_shape, BF16), (rows_shape, BF16)],
        [
            (rows_shape, BF16),
            (rows_shape, BF16),
            line,
            (bias_weight_t.shape, BF16),
            (out_weight.shape, BF16),
            (rows_shape, BF16),
            (rows_shape, F32),
        ],
        placed=True,
        near=1,
        sems=7,
        flops=2 * 10**9,
        moved=6 * 10**6,
    )
    sums, pair_grad, updated = lax.optimization_barrier((sums, pair_grad, updated))
    (blocks,) = call(
        sum_kernel, "sum", (sums,), [((devices, chunk, channels), BF16)], near=1
    )
    blocks = exchange(blocks, "dap")
    grad_proj, grad_shift, grad_out, grad_bias, grad_gain = call(
        functools.partial(assemble_kernel, 1.0 / width),
        "assemble",
        (blocks, proj_weight, bias_weight_t, gain),
        [
            ((channels, 4 * channels), F32),
            line,
            ((channels, channels), F32),
            ((heads, channels), F32),
            line,
        ],
        near=4,
    )
    return (
        updated[None],
        pair_grad[None],
        grad_proj,
        grad_shift[0],
        grad_out,
        grad_bias.T,
        grad_gain[0],
    )


def solution(mesh):
    rows = P("dp", "dap", None, None)
    return jax.shard_map(
        per_device,
        mesh=mesh,
        in_specs=(rows, P("dp"), rows, P(), P(), P(), P(), P()),
        out_specs=(rows, rows, P(), P(), P(), P(), P()),
        check_vma=False,
    )
```

```python
import functools

import jax
import jax.numpy as jnp
from jax import lax
from jax.experimental import pallas as pl
from jax.experimental.pallas import tpu as pltpu
from jax.sharding import PartitionSpec as P

EPS = 1e-05
DEAD = -1e30
F32 = jnp.float32
BF16 = jnp.bfloat16
VMEM_LIMIT = 16 * 1024 * 1024
UNROLL_PROJECT = 4
UNROLL_ATTEND = 8


def dot(a, b):
    return jnp.dot(a, b, preferred_element_type=F32)


def contract(a, b, a_axis, b_axis):
    return lax.dot_general(
        a, b, (((a_axis,), (b_axis,)), ((), ())), preferred_element_type=F32
    )


def standardize(rows):
    rows = rows.astype(F32)
    centered = rows - jnp.mean(rows, -1, keepdims=True)
    inv_std = lax.rsqrt(jnp.mean(centered * centered, -1, keepdims=True) + EPS)
    return centered * inv_std, inv_std


def head_masks(shape, axis, heads):
    size = shape[axis] // heads
    position = lax.broadcasted_iota(jnp.int32, shape, axis)
    return [(position >= h * size) & (position < (h + 1) * size) for h in range(heads)]


def stack_heads(block, masks):
    return jnp.concatenate([jnp.where(m, block, jnp.zeros_like(block)) for m in masks], 0)


def pick_heads(stacked, masks):
    size = stacked.shape[0] // len(masks)
    picked = stacked[:size]
    for h in range(1, len(masks)):
        picked = jnp.where(masks[h], stacked[h * size : (h + 1) * size], picked)
    return picked


def begin_all(sources, targets, sems):
    copies = [
        pltpu.make_async_copy(source, target, sems.at[n])
        for n, (source, target) in enumerate(zip(sources, targets, strict=True))
    ]
    for copy in copies:
        copy.start()
    return copies


def norm_kernel(
    pair_hbm,
    gain_hbm,
    bias_weight_hbm,
    proj_weight_hbm,
    gate_shift_hbm,
    normed_ref,
    bias_ref,
    proj_weight_ref,
    gate_shift_ref,
    pair,
    gain,
    bias_weight,
    held,
    sems,
):
    row_count = pair.shape[0]
    heads = bias_weight.shape[0]
    copies = begin_all(
        (gain_hbm, bias_weight_hbm, pair_hbm, proj_weight_hbm, gate_shift_hbm),
        (gain, bias_weight, pair, proj_weight_ref, gate_shift_ref),
        sems,
    )
    for copy in copies[:3]:
        copy.wait()
    for row in range(row_count):
        x_hat, _ = standardize(pair[row])
        normed = (x_hat * gain[...]).astype(BF16)
        normed_ref[row] = normed
        held[pl.ds(row, heads, stride=row_count), :] = contract(bias_weight[...], normed, 1, 1)
    block = held[...].astype(BF16)
    for peer in range(bias_ref.shape[0]):
        bias_ref[peer] = block
    for copy in copies[3:]:
        copy.wait()


def project_kernel(
    heads,
    place_ref,
    normed_ref,
    proj_weight_ref,
    gate_shift_ref,
    cot_hbm,
    out_weight_hbm,
    narrow_ref,
    wide_ref,
    cot,
    out_weight,
    sems,
):
    row_count, width, channels = cot.shape
    scaling = (channels // heads) ** (-0.5)
    copies = begin_all((cot_hbm, out_weight_hbm), (cot, out_weight), sems)
    length, first_row = place_ref[0], place_ref[1]
    weight_t = proj_weight_ref[...].T
    share = weight_t.shape[0] // row_count
    for row in range(row_count):
        narrow_ref[row, 5 * width + 2 * channels :] = weight_t[row * share : (row + 1) * share]
    weight_t = weight_t[channels : 3 * channels]
    token = lax.broadcasted_iota(jnp.int32, (width, channels), 0)

    def place(row, n, block):
        narrow_ref[row, n * width : (n + 1) * width] = block.astype(BF16)

    def forward(row, carry):
        normed = normed_ref[row]
        projected = dot(normed, proj_weight_ref[...])
        place(row, 0, projected[:, :channels] * scaling)
        place(row, 3, projected[:, channels : 2 * channels])
        place(row, 4, projected[:, 2 * channels : 3 * channels])
        wide_ref[row, :width] = jax.nn.sigmoid(projected[:, 3 * channels :] + gate_shift_ref[...])
        narrow_ref[row, 5 * width : 5 * width + 2 * channels] = contract(
            weight_t, normed, 1, 1
        ).astype(BF16)
        return carry

    def backward(row, carry):
        live = token < jnp.where(first_row + row < length, length, 0)
        d_output = jnp.where(live, cot[row].astype(F32), 0.0).astype(BF16)
        d_mixed = contract(d_output, out_weight[...], 1, 1)
        place(row, 1, d_mixed * wide_ref[row, :width])
        place(row, 2, d_output)
        wide_ref[row, width:] = d_mixed
        return carry

    lax.fori_loop(0, row_count, forward, 0, unroll=UNROLL_PROJECT)
    for copy in copies:
        copy.wait()
    lax.fori_loop(0, row_count, backward, 0, unroll=UNROLL_PROJECT)


def attend_kernel(
    place_ref,
    bias_ref,
    normed_ref,
    narrow_ref,
    wide_ref,
    parts_ref,
    mixed_ref,
    normed_proj_ref,
    shift_ref,
    bias_t,
    bias_sum,
    parts,
    d_proj,
    weight_t,
):
    row_count, width, channels = normed_ref.shape
    heads = bias_t.shape[0] // width
    head_size = channels // heads
    scaling = head_size ** (-0.5)
    length = place_ref[0]
    devices = bias_ref.shape[0]
    key_live = lax.broadcasted_iota(jnp.int32, (width, width), 0) < length
    for h in range(heads):
        rows = [
            bias_ref[d].astype(F32)[h * row_count : (h + 1) * row_count]
            for d in range(devices)
        ]
        turned = jnp.concatenate(rows, 0).T
        bias_t[h * width : (h + 1) * width] = jnp.where(key_live, turned, DEAD)
    bias_sum[...] = jnp.zeros_like(bias_sum)
    lane_masks = head_masks((width, channels), 1, heads)
    share = weight_t.shape[0] // row_count
    for row in range(row_count):
        weight_t[row * share : (row + 1) * share] = narrow_ref[row, 5 * width + 2 * channels :]

    def one_row(row, shift_sum):
        weights, lows, attended_t, d_query_t = [], [], [], []
        queries, d_attend, _, keys, values = (
            narrow_ref[row, n * width : (n + 1) * width] for n in range(5)
        )
        turned = narrow_ref.at[row, 5 * width :]
        scores = contract(stack_heads(keys, lane_masks), queries, 1, 1)
        grads = contract(stack_heads(values, lane_masks), d_attend, 1, 1)
        for h in range(heads):
            part = slice(h * width, (h + 1) * width)
            own = slice(h * head_size, (h + 1) * head_size)
            expo = jnp.exp(scores[part] + bias_t[part])
            probs = expo * (1.0 / jnp.sum(expo, 0, keepdims=True))
            weight = probs.astype(BF16)
            g = grads[part]
            d_scores = probs * (g - jnp.sum(probs * g, 0, keepdims=True))
            bias_sum[part] += d_scores
            low = d_scores.astype(BF16)
            weights.append(weight)
            lows.append(low)
            attended_t.append(dot(turned[channels + own.start : channels + own.stop], weight))
            d_query_t.append(dot(turned[own], low))
        attended = jnp.concatenate(attended_t, 0).T.astype(BF16).astype(F32)
        d_query = jnp.concatenate(d_query_t, 0).T
        d_value = pick_heads(dot(jnp.concatenate(weights, 0), d_attend), lane_masks)
        d_key = pick_heads(dot(jnp.concatenate(lows, 0), queries), lane_masks)
        gating = wide_ref[row, :width]
        mixed = gating * attended
        mixed_ref[row] = mixed.astype(BF16)
        d_gating = (wide_ref[row, width:] * mixed * (1.0 - gating)).astype(BF16)
        d_row = jnp.concatenate(
            [
                (d_query * scaling).astype(BF16),
                d_key.astype(BF16),
                d_value.astype(BF16),
                d_gating,
            ],
            1,
        )
        d_proj[row] = d_row
        return shift_sum + jnp.sum(d_gating.astype(F32), 0, keepdims=True)

    zero = jnp.zeros((1, channels), F32)
    shift_ref[...] = lax.fori_loop(0, row_count, one_row, zero, unroll=UNROLL_ATTEND)
    flat = d_proj[...].reshape(row_count * width, 4 * channels)
    normed_proj_ref[...] = dot(flat, weight_t[...]).reshape(normed_proj_ref.shape)
    shared = heads * row_count
    for h in range(heads):
        turned = bias_sum[h * width : (h + 1) * width].T
        for d in range(devices):
            parts[d, h * row_count : (h + 1) * row_count] = turned[
                d * row_count : (d + 1) * row_count
            ]
    tokens = row_count * width
    normed = normed_ref[...].reshape(tokens, channels)
    grad_proj = contract(normed, flat, 0, 0)
    grad_out = contract(
        mixed_ref[...].reshape(tokens, channels),
        narrow_ref[:, 2 * width : 3 * width].reshape(tokens, channels),
        0,
        0,
    )
    pieces = [grad_proj[:, i * channels : (i + 1) * channels] for i in range(4)] + [grad_out]
    for d in range(devices):
        for i, piece in enumerate(pieces):
            start = shared + i * row_count
            parts[d, start : start + row_count] = piece[d * row_count : (d + 1) * row_count]
    parts_ref[...] = parts[...].astype(BF16)


def bias_kernel(
    parts_ref, normed_ref, shift_ref, mixed_ref, normed_proj_ref, bias_grad_ref, own_ref, held
):
    del mixed_ref, normed_proj_ref
    row_count, width, channels = normed_ref.shape
    shared = bias_grad_ref.shape[0]
    heads = shared // row_count
    total = parts_ref[0].astype(F32)
    for d in range(1, parts_ref.shape[0]):
        total = total + parts_ref[d].astype(F32)
    bias_grad = total[:shared].astype(BF16)
    bias_grad_ref[...] = bias_grad
    bias_grad = bias_grad.astype(F32)
    of_row = lax.broadcasted_iota(jnp.int32, bias_grad.shape, 0) % row_count
    grad_bias = jnp.zeros((shared, channels), F32)
    for row in range(row_count):
        own = jnp.where(of_row == row, bias_grad, 0.0).astype(BF16)
        grad_bias = grad_bias + dot(own, normed_ref[row])
    grads = 5 * row_count
    held[:grads] = total[shared : shared + grads]
    held[grads:] = jnp.zeros((held.shape[0] - grads, channels), F32)
    for h in range(heads):
        held[grads + h : grads + h + 1] = jnp.sum(
            grad_bias[h * row_count : (h + 1) * row_count], 0, keepdims=True
        )
    held[grads + heads : grads + heads + 1] = shift_ref[...]
    own_ref[...] = held[...].astype(BF16)


def pair_kernel(near_ref, sums_ref):
    block = near_ref[0].astype(F32)
    for n in range(1, near_ref.shape[0]):
        block = block + near_ref[n].astype(F32)
    block = block.astype(BF16)
    for peer in range(sums_ref.shape[0]):
        sums_ref[peer] = block


def finish_kernel(
    place_ref,
    bias_grad_ref,
    mixed_hbm,
    normed_proj_hbm,
    pair_hbm,
    cot_hbm,
    gain_hbm,
    bias_weight_hbm,
    out_weight_hbm,
    updated_ref,
    pair_grad_ref,
    pair_ref,
    cot_ref,
    gain_ref,
    bias_weight_ref,
    out_weight_ref,
    mixed_ref,
    normed_proj_ref,
    sems,
):
    copies = begin_all(
        (
            pair_hbm,
            cot_hbm,
            gain_hbm,
            bias_weight_hbm,
            out_weight_hbm,
            mixed_hbm,
            normed_proj_hbm,
        ),
        (
            pair_ref,
            cot_ref,
            gain_ref,
            bias_weight_ref,
            out_weight_ref,
            mixed_ref,
            normed_proj_ref,
        ),
        sems,
    )
    row_count, width, channels = pair_ref.shape
    heads = bias_weight_ref.shape[0]
    length, first_row = place_ref[0], place_ref[1]
    token = lax.broadcasted_iota(jnp.int32, (width, channels), 0)
    bias_grad = bias_grad_ref[...].astype(F32)
    of_row = lax.broadcasted_iota(jnp.int32, bias_grad.shape, 0) % row_count
    for copy in copies:
        copy.wait()
    weight = bias_weight_ref[...].astype(F32)
    spread = jnp.concatenate(
        [jnp.broadcast_to(weight[h : h + 1], (row_count, channels)) for h in range(heads)], 0
    ).astype(BF16)
    for row in range(row_count):
        live = token < jnp.where(first_row + row < length, length, 0)
        output = dot(mixed_ref[row], out_weight_ref[...])
        updated_ref[row] = (
            pair_ref[row].astype(F32) + jnp.where(live, output, 0.0)
        ).astype(BF16)
        own = jnp.where(of_row == row, bias_grad, 0.0)
        added = dot(own.T.astype(BF16), spread)
        x_hat, inv_std = standardize(pair_ref[row])
        d_x_hat = (normed_proj_ref[row] + added) * gain_ref[...]
        d_pair = inv_std * (
            d_x_hat
            - jnp.mean(d_x_hat, -1, keepdims=True)
            - x_hat * jnp.mean(d_x_hat * x_hat, -1, keepdims=True)
        )
        pair_grad_ref[row] = (cot_ref[row].astype(F32) + d_pair).astype(BF16)


def sum_kernel(sums_ref, out_ref):
    total = sums_ref[0].astype(F32)
    for d in range(1, sums_ref.shape[0]):
        total = total + sums_ref[d].astype(F32)
    block = total.astype(BF16)
    for peer in range(out_ref.shape[0]):
        out_ref[peer] = block


def assemble_kernel(
    scale,
    blocks_ref,
    proj_weight_ref,
    bias_weight_ref,
    gain_ref,
    grad_proj_ref,
    grad_shift_ref,
    grad_out_ref,
    grad_bias_ref,
    grad_gain_ref,
):
    devices = blocks_ref.shape[0]
    channels = grad_out_ref.shape[0]
    heads = grad_bias_ref.shape[0]
    row_count = channels // devices
    grads = 5 * row_count
    small = None
    by_channel = []
    for d in range(devices):
        block = blocks_ref[d].astype(F32) * scale
        own = slice(d * row_count, (d + 1) * row_count)
        by_lane = None
        for i in range(4):
            columns = slice(i * channels, (i + 1) * channels)
            piece = block[i * row_count : (i + 1) * row_count]
            grad_proj_ref[own, columns] = piece
            term = piece * proj_weight_ref[own, columns].astype(F32)
            by_lane = term if by_lane is None else by_lane + term
        by_channel.append(by_lane)
        grad_out_ref[own] = block[4 * row_count : grads]
        small = block[grads:] if small is None else small + block[grads:]
    grad_bias_ref[...] = small[:heads]
    grad_shift_ref[...] = small[heads : heads + 1]
    gain_sum = jnp.sum(jnp.concatenate(by_channel, 0).T, 0, keepdims=True)
    gain_sum = gain_sum + jnp.sum(
        small[:heads] * bias_weight_ref[...].astype(F32), 0, keepdims=True
    )
    grad_gain_ref[...] = gain_sum / gain_ref[...]


def per_device(
    pair_act, lengths, cotangent, proj_weight, gate_shift, out_weight, bias_weight, norm_gain
):
    pair, cot = pair_act[0], cotangent[0]
    row_count, width, channels = pair.shape
    heads = bias_weight.shape[1]
    gain, bias_weight_t = norm_gain[None], bias_weight.T
    devices, samples = lax.axis_size("dap"), lax.axis_size("dp")
    shared = heads * row_count
    chunk = -(-(5 * row_count + heads + 1) // 16) * 16
    vmem = pl.BlockSpec(memory_space=pltpu.VMEM)
    smem = pl.BlockSpec(memory_space=pltpu.SMEM)
    hbm = pl.BlockSpec(memory_space=pltpu.MemorySpace.HBM)
    rows_shape = (row_count, width, channels)
    line = ((1, channels), F32)

    def away(array):
        return pltpu.with_memory_space_constraint(array, pltpu.MemorySpace.HBM)

    def call(kernel, name, args, outs, scratch=(), placed=False, near=0, sems=0, flops=0, moved=0):
        return pl.pallas_call(
            kernel,
            out_shape=tuple(jax.ShapeDtypeStruct(shape, dtype) for shape, dtype in outs),
            in_specs=[smem] * placed + [vmem] * near + [hbm] * (len(args) - placed - near),
            out_specs=(vmem,) * len(outs),
            scratch_shapes=[pltpu.VMEM(shape, dtype) for shape, dtype in scratch]
            + [pltpu.SemaphoreType.DMA((sems,))] * bool(sems),
            compiler_params=pltpu.CompilerParams(vmem_limit_bytes=VMEM_LIMIT),
            cost_estimate=pl.CostEstimate(flops=flops, bytes_accessed=moved, transcendentals=0),
            name=name,
        )(*args[: placed + near], *(away(a) for a in args[placed + near :]))

    def exchange(blocks, axis, groups=None):
        return lax.all_to_all(blocks, axis, 0, 0, axis_index_groups=groups, tiled=True)

    inputs = (pair, gain, bias_weight_t, proj_weight, gate_shift[None])
    normed, bias_copies, near_proj, near_shift = call(
        norm_kernel,
        "norm",
        inputs,
        [
            (rows_shape, BF16),
            ((devices, shared, width), BF16),
            *((a.shape, a.dtype) for a in inputs[3:]),
        ],
        [
            (rows_shape, BF16),
            line,
            (bias_weight_t.shape, BF16),
            ((shared, width), F32),
        ],
        sems=len(inputs),
    )
    bias_all = exchange(bias_copies, "dap")
    place = jnp.stack([lengths[0], lax.axis_index("dap") * row_count]).astype(jnp.int32)
    narrow, wide = call(
        functools.partial(project_kernel, heads),
        "project",
        (place, normed, near_proj, near_shift, cot, out_weight),
        [
            ((row_count, 5 * width + 2 * channels + 4 * channels // row_count, width), BF16),
            ((row_count, 2 * width, channels), F32),
        ],
        [(rows_shape, BF16), (out_weight.shape, BF16)],
        placed=True,
        near=3,
        sems=2,
        flops=3 * 10**9,
        moved=10**7,
    )
    parts, mixed, normed_proj, shift = call(
        attend_kernel,
        "attend",
        (place, bias_all, normed, narrow, wide),
        [
            ((devices, shared + 5 * row_count, width), BF16),
            (rows_shape, BF16),
            (rows_shape, F32),
            line,
        ],
        [
            ((heads * width, width), F32),
            ((heads * width, width), F32),
            ((devices, shared + 5 * row_count, width), F32),
            ((row_count, width, 4 * channels), BF16),
            ((4 * channels, channels), BF16),
        ],
        placed=True,
        near=4,
    )
    parts = exchange(parts, "dap")
    bias_grad, own = call(
        bias_kernel,
        "bias_grad",
        (parts, normed, shift, mixed, normed_proj),
        [((shared, width), BF16), ((chunk, channels), BF16)],
        [((chunk, channels), F32)],
        near=5,
    )
    near = 4
    runs = [list(range(n, n + near)) for n in range(0, samples, near)]
    across = [list(range(n, samples, near)) for n in range(near)]
    gathered = lax.all_gather(own, "dp", axis=0, axis_index_groups=runs)
    bias_grad, gathered = lax.optimization_barrier((bias_grad, gathered))
    (sums,) = call(
        pair_kernel,
        "pair",
        (gathered,),
        [((samples // near, chunk, channels), BF16)],
        near=1,
    )
    sums = exchange(sums, "dp", across)
    updated, pair_grad = call(
        finish_kernel,
        "finish",
        (place, bias_grad, mixed, normed_proj, pair, cot, gain, bias_weight_t, out_weight),
        [(rows_shape, BF16), (rows_shape, BF16)],
        [
            (rows_shape, BF16),
            (rows_shape, BF16),
            line,
            (bias_weight_t.shape, BF16),
            (out_weight.shape, BF16),
            (rows_shape, BF16),
            (rows_shape, F32),
        ],
        placed=True,
        near=1,
        sems=7,
        flops=2 * 10**9,
        moved=6 * 10**6,
    )
    (blocks,) = call(
        sum_kernel, "sum", (sums,), [((devices, chunk, channels), BF16)], near=1
    )
    blocks = exchange(blocks, "dap")
    grad_proj, grad_shift, grad_out, grad_bias, grad_gain = call(
        functools.partial(assemble_kernel, 1.0 / width),
        "assemble",
        (blocks, proj_weight, bias_weight_t, gain),
        [
            ((channels, 4 * channels), F32),
            line,
            ((channels, channels), F32),
            ((heads, channels), F32),
            line,
        ],
        near=4,
    )
    return (
        updated[None],
        pair_grad[None],
        grad_proj,
        grad_shift[0],
        grad_out,
        grad_bias.T,
        grad_gain[0],
    )


def solution(mesh):
    rows = P("dp", "dap", None, None)
    return jax.shard_map(
        per_device,
        mesh=mesh,
        in_specs=(rows, P("dp"), rows, P(), P(), P(), P(), P()),
        out_specs=(rows, rows, P(), P(), P(), P(), P()),
        check_vma=False,
    )
```

```python
import functools

import jax
import jax.numpy as jnp
from jax import lax
from jax.experimental import pallas as pl
from jax.experimental.pallas import tpu as pltpu
from jax.sharding import PartitionSpec as P

EPS = 1e-05
DEAD = -1e30
F32 = jnp.float32
BF16 = jnp.bfloat16
VMEM_LIMIT = 16 * 1024 * 1024
UNROLL_PROJECT = 4
UNROLL_ATTEND = 8


def dot(a, b):
    return jnp.dot(a, b, preferred_element_type=F32)


def contract(a, b, a_axis, b_axis):
    return lax.dot_general(
        a, b, (((a_axis,), (b_axis,)), ((), ())), preferred_element_type=F32
    )


def standardize(rows):
    rows = rows.astype(F32)
    centered = rows - jnp.mean(rows, -1, keepdims=True)
    inv_std = lax.rsqrt(jnp.mean(centered * centered, -1, keepdims=True) + EPS)
    return centered * inv_std, inv_std


def head_masks(shape, axis, heads):
    size = shape[axis] // heads
    position = lax.broadcasted_iota(jnp.int32, shape, axis)
    return [(position >= h * size) & (position < (h + 1) * size) for h in range(heads)]


def stack_heads(block, masks):
    return jnp.concatenate([jnp.where(m, block, jnp.zeros_like(block)) for m in masks], 0)


def pick_heads(stacked, masks):
    size = stacked.shape[0] // len(masks)
    picked = stacked[:size]
    for h in range(1, len(masks)):
        picked = jnp.where(masks[h], stacked[h * size : (h + 1) * size], picked)
    return picked


def begin_all(sources, targets, sems):
    copies = [
        pltpu.make_async_copy(source, target, sems.at[n])
        for n, (source, target) in enumerate(zip(sources, targets, strict=True))
    ]
    for copy in copies:
        copy.start()
    return copies


def norm_kernel(
    pair_hbm,
    gain_hbm,
    bias_weight_hbm,
    proj_weight_hbm,
    gate_shift_hbm,
    normed_ref,
    bias_ref,
    proj_weight_ref,
    gate_shift_ref,
    pair,
    gain,
    bias_weight,
    held,
    sems,
):
    row_count = pair.shape[0]
    heads = bias_weight.shape[0]
    copies = begin_all(
        (gain_hbm, bias_weight_hbm, pair_hbm, proj_weight_hbm, gate_shift_hbm),
        (gain, bias_weight, pair, proj_weight_ref, gate_shift_ref),
        sems,
    )
    for copy in copies[:3]:
        copy.wait()
    for row in range(row_count):
        x_hat, _ = standardize(pair[row])
        normed = (x_hat * gain[...]).astype(BF16)
        normed_ref[row] = normed
        held[pl.ds(row, heads, stride=row_count), :] = contract(bias_weight[...], normed, 1, 1)
    block = held[: heads * row_count].astype(BF16)
    for peer in range(bias_ref.shape[0]):
        bias_ref[peer] = block
    for copy in copies[3:]:
        copy.wait()


def project_kernel(
    heads,
    place_ref,
    normed_ref,
    proj_weight_ref,
    gate_shift_ref,
    cot_hbm,
    out_weight_hbm,
    narrow_ref,
    wide_ref,
    cot,
    out_weight,
    sems,
):
    row_count, width, channels = cot.shape
    scaling = (channels // heads) ** (-0.5)
    copies = begin_all((cot_hbm, out_weight_hbm), (cot, out_weight), sems)
    length, first_row = place_ref[0], place_ref[1]
    weight_t = proj_weight_ref[...].T
    share = weight_t.shape[0] // row_count
    for row in range(row_count):
        narrow_ref[row, 5 * width + 2 * channels :] = weight_t[row * share : (row + 1) * share]
    weight_t = weight_t[channels : 3 * channels]
    token = lax.broadcasted_iota(jnp.int32, (width, channels), 0)

    def place(row, n, block):
        narrow_ref[row, n * width : (n + 1) * width] = block.astype(BF16)

    def forward(row, carry):
        normed = normed_ref[row]
        projected = dot(normed, proj_weight_ref[...])
        place(row, 0, projected[:, :channels] * scaling)
        place(row, 3, projected[:, channels : 2 * channels])
        place(row, 4, projected[:, 2 * channels : 3 * channels])
        wide_ref[row, :width] = jax.nn.sigmoid(projected[:, 3 * channels :] + gate_shift_ref[...])
        narrow_ref[row, 5 * width : 5 * width + 2 * channels] = contract(
            weight_t, normed, 1, 1
        ).astype(BF16)
        return carry

    def backward(row, carry):
        live = token < jnp.where(first_row + row < length, length, 0)
        d_output = jnp.where(live, cot[row].astype(F32), 0.0).astype(BF16)
        d_mixed = contract(d_output, out_weight[...], 1, 1)
        place(row, 1, d_mixed * wide_ref[row, :width])
        place(row, 2, d_output)
        wide_ref[row, width:] = d_mixed
        return carry

    lax.fori_loop(0, row_count, forward, 0, unroll=UNROLL_PROJECT)
    for copy in copies:
        copy.wait()
    lax.fori_loop(0, row_count, backward, 0, unroll=UNROLL_PROJECT)


def attend_kernel(
    place_ref,
    bias_ref,
    normed_ref,
    narrow_ref,
    wide_ref,
    parts_ref,
    mixed_ref,
    normed_proj_ref,
    shift_ref,
    bias_t,
    bias_sum,
    parts,
    d_proj,
    weight_t,
):
    row_count, width, channels = normed_ref.shape
    heads = bias_t.shape[0] // width
    head_size = channels // heads
    scaling = head_size ** (-0.5)
    length = place_ref[0]
    devices = bias_ref.shape[0]
    key_live = lax.broadcasted_iota(jnp.int32, (width, width), 0) < length
    for h in range(heads):
        rows = [
            bias_ref[d].astype(F32)[h * row_count : (h + 1) * row_count]
            for d in range(devices)
        ]
        turned = jnp.concatenate(rows, 0).T
        bias_t[h * width : (h + 1) * width] = jnp.where(key_live, turned, DEAD)
    bias_sum[...] = jnp.zeros_like(bias_sum)
    lane_masks = head_masks((width, channels), 1, heads)
    share = weight_t.shape[0] // row_count
    for row in range(row_count):
        weight_t[row * share : (row + 1) * share] = narrow_ref[row, 5 * width + 2 * channels :]

    def one_row(row, shift_sum):
        weights, lows, attended_t, d_query_t = [], [], [], []
        queries, d_attend, _, keys, values = (
            narrow_ref[row, n * width : (n + 1) * width] for n in range(5)
        )
        turned = narrow_ref.at[row, 5 * width :]
        scores = contract(stack_heads(keys, lane_masks), queries, 1, 1)
        grads = contract(stack_heads(values, lane_masks), d_attend, 1, 1)
        for h in range(heads):
            part = slice(h * width, (h + 1) * width)
            own = slice(h * head_size, (h + 1) * head_size)
            expo = jnp.exp(scores[part] + bias_t[part])
            probs = expo * (1.0 / jnp.sum(expo, 0, keepdims=True))
            weight = probs.astype(BF16)
            g = grads[part]
            d_scores = probs * (g - jnp.sum(probs * g, 0, keepdims=True))
            bias_sum[part] += d_scores
            low = d_scores.astype(BF16)
            weights.append(weight)
            lows.append(low)
            attended_t.append(dot(turned[channels + own.start : channels + own.stop], weight))
            d_query_t.append(dot(turned[own], low))
        attended = jnp.concatenate(attended_t, 0).T.astype(BF16).astype(F32)
        d_query = jnp.concatenate(d_query_t, 0).T
        d_value = pick_heads(dot(jnp.concatenate(weights, 0), d_attend), lane_masks)
        d_key = pick_heads(dot(jnp.concatenate(lows, 0), queries), lane_masks)
        gating = wide_ref[row, :width]
        mixed = gating * attended
        mixed_ref[row] = mixed.astype(BF16)
        d_gating = (wide_ref[row, width:] * mixed * (1.0 - gating)).astype(BF16)
        d_row = jnp.concatenate(
            [
                (d_query * scaling).astype(BF16),
                d_key.astype(BF16),
                d_value.astype(BF16),
                d_gating,
            ],
            1,
        )
        d_proj[row] = d_row
        return shift_sum + jnp.sum(d_gating.astype(F32), 0, keepdims=True)

    zero = jnp.zeros((1, channels), F32)
    shift_ref[...] = lax.fori_loop(0, row_count, one_row, zero, unroll=UNROLL_ATTEND)
    flat = d_proj[...].reshape(row_count * width, 4 * channels)
    normed_proj_ref[...] = dot(flat, weight_t[...]).reshape(normed_proj_ref.shape)
    shared = heads * row_count
    for h in range(heads):
        turned = bias_sum[h * width : (h + 1) * width].T
        for d in range(devices):
            parts[d, h * row_count : (h + 1) * row_count] = turned[
                d * row_count : (d + 1) * row_count
            ]
    tokens = row_count * width
    normed = normed_ref[...].reshape(tokens, channels)
    grad_proj = contract(normed, flat, 0, 0)
    grad_out = contract(
        mixed_ref[...].reshape(tokens, channels),
        narrow_ref[:, 2 * width : 3 * width].reshape(tokens, channels),
        0,
        0,
    )
    pieces = [grad_proj[:, i * channels : (i + 1) * channels] for i in range(4)] + [grad_out]
    for d in range(devices):
        for i, piece in enumerate(pieces):
            start = shared + i * row_count
            parts[d, start : start + row_count] = piece[d * row_count : (d + 1) * row_count]
    parts_ref[...] = parts[...].astype(BF16)


def bias_kernel(
    parts_ref, normed_ref, shift_ref, mixed_ref, normed_proj_ref, bias_grad_ref, own_ref, held
):
    del mixed_ref, normed_proj_ref
    row_count, width, channels = normed_ref.shape
    shared = bias_grad_ref.shape[0]
    heads = shared // row_count
    total = parts_ref[0].astype(F32)
    for d in range(1, parts_ref.shape[0]):
        total = total + parts_ref[d].astype(F32)
    bias_grad = total[:shared].astype(BF16)
    bias_grad_ref[...] = bias_grad
    bias_grad = bias_grad.astype(F32)
    of_row = lax.broadcasted_iota(jnp.int32, bias_grad.shape, 0) % row_count
    grad_bias = jnp.zeros((shared, channels), F32)
    for row in range(row_count):
        own = jnp.where(of_row == row, bias_grad, 0.0).astype(BF16)
        grad_bias = grad_bias + dot(own, normed_ref[row])
    grads = 5 * row_count
    held[:grads] = total[shared : shared + grads]
    held[grads:] = jnp.zeros((held.shape[0] - grads, channels), F32)
    for h in range(heads):
        held[grads + h : grads + h + 1] = jnp.sum(
            grad_bias[h * row_count : (h + 1) * row_count], 0, keepdims=True
        )
    held[grads + heads : grads + heads + 1] = shift_ref[...]
    own_ref[...] = held[: own_ref.shape[0]].astype(BF16)


def pair_kernel(near_ref, sums_ref):
    block = near_ref[0].astype(F32)
    for n in range(1, near_ref.shape[0]):
        block = block + near_ref[n].astype(F32)
    block = block.astype(BF16)
    for peer in range(sums_ref.shape[0]):
        sums_ref[peer] = block


def finish_kernel(
    place_ref,
    bias_grad_ref,
    mixed_hbm,
    normed_proj_hbm,
    pair_hbm,
    cot_hbm,
    gain_hbm,
    bias_weight_hbm,
    out_weight_hbm,
    updated_ref,
    pair_grad_ref,
    pair_ref,
    cot_ref,
    gain_ref,
    bias_weight_ref,
    out_weight_ref,
    mixed_ref,
    normed_proj_ref,
    sems,
):
    copies = begin_all(
        (
            pair_hbm,
            cot_hbm,
            gain_hbm,
            bias_weight_hbm,
            out_weight_hbm,
            mixed_hbm,
            normed_proj_hbm,
        ),
        (
            pair_ref,
            cot_ref,
            gain_ref,
            bias_weight_ref,
            out_weight_ref,
            mixed_ref,
            normed_proj_ref,
        ),
        sems,
    )
    row_count, width, channels = pair_ref.shape
    heads = bias_weight_ref.shape[0]
    length, first_row = place_ref[0], place_ref[1]
    token = lax.broadcasted_iota(jnp.int32, (width, channels), 0)
    bias_grad = bias_grad_ref[...].astype(F32)
    of_row = lax.broadcasted_iota(jnp.int32, bias_grad.shape, 0) % row_count
    for copy in copies:
        copy.wait()
    weight = bias_weight_ref[...].astype(F32)
    spread = jnp.concatenate(
        [jnp.broadcast_to(weight[h : h + 1], (row_count, channels)) for h in range(heads)], 0
    ).astype(BF16)
    for row in range(row_count):
        live = token < jnp.where(first_row + row < length, length, 0)
        output = dot(mixed_ref[row], out_weight_ref[...])
        updated_ref[row] = (
            pair_ref[row].astype(F32) + jnp.where(live, output, 0.0)
        ).astype(BF16)
        own = jnp.where(of_row == row, bias_grad, 0.0)
        added = dot(own.T.astype(BF16), spread)
        x_hat, inv_std = standardize(pair_ref[row])
        d_x_hat = (normed_proj_ref[row] + added) * gain_ref[...]
        d_pair = inv_std * (
            d_x_hat
            - jnp.mean(d_x_hat, -1, keepdims=True)
            - x_hat * jnp.mean(d_x_hat * x_hat, -1, keepdims=True)
        )
        pair_grad_ref[row] = (cot_ref[row].astype(F32) + d_pair).astype(BF16)


def sum_kernel(sums_ref, out_ref):
    total = sums_ref[0].astype(F32)
    for d in range(1, sums_ref.shape[0]):
        total = total + sums_ref[d].astype(F32)
    block = total.astype(BF16)
    for peer in range(out_ref.shape[0]):
        out_ref[peer] = block


def assemble_kernel(
    scale,
    blocks_ref,
    proj_weight_ref,
    bias_weight_ref,
    gain_ref,
    grad_proj_ref,
    grad_shift_ref,
    grad_out_ref,
    grad_bias_ref,
    grad_gain_ref,
):
    devices = blocks_ref.shape[0]
    channels = grad_out_ref.shape[0]
    heads = grad_bias_ref.shape[0]
    row_count = channels // devices
    grads = 5 * row_count
    small = None
    by_channel = []
    for d in range(devices):
        block = blocks_ref[d].astype(F32) * scale
        own = slice(d * row_count, (d + 1) * row_count)
        by_lane = None
        for i in range(4):
            columns = slice(i * channels, (i + 1) * channels)
            piece = block[i * row_count : (i + 1) * row_count]
            grad_proj_ref[own, columns] = piece
            term = piece * proj_weight_ref[own, columns].astype(F32)
            by_lane = term if by_lane is None else by_lane + term
        by_channel.append(by_lane)
        grad_out_ref[own] = block[4 * row_count : grads]
        small = block[grads:] if small is None else small + block[grads:]
    grad_bias_ref[...] = small[:heads]
    grad_shift_ref[...] = small[heads : heads + 1]
    gain_sum = jnp.sum(jnp.concatenate(by_channel, 0).T, 0, keepdims=True)
    gain_sum = gain_sum + jnp.sum(
        small[:heads] * bias_weight_ref[...].astype(F32), 0, keepdims=True
    )
    grad_gain_ref[...] = gain_sum / gain_ref[...]


def per_device(
    pair_act, lengths, cotangent, proj_weight, gate_shift, out_weight, bias_weight, norm_gain
):
    pair, cot = pair_act[0], cotangent[0]
    row_count, width, channels = pair.shape
    heads = bias_weight.shape[1]
    gain, bias_weight_t = norm_gain[None], bias_weight.T
    devices, samples = lax.axis_size("dap"), lax.axis_size("dp")
    shared = heads * row_count
    chunk = -(-(5 * row_count + heads + 1) // 16) * 16
    vmem = pl.BlockSpec(memory_space=pltpu.VMEM)
    smem = pl.BlockSpec(memory_space=pltpu.SMEM)
    hbm = pl.BlockSpec(memory_space=pltpu.MemorySpace.HBM)
    rows_shape = (row_count, width, channels)
    line = ((1, channels), F32)

    def away(array):
        return pltpu.with_memory_space_constraint(array, pltpu.MemorySpace.HBM)

    def call(kernel, name, args, outs, scratch=(), placed=False, near=0, sems=0, flops=0, moved=0):
        return pl.pallas_call(
            kernel,
            out_shape=tuple(jax.ShapeDtypeStruct(shape, dtype) for shape, dtype in outs),
            in_specs=[smem] * placed + [vmem] * near + [hbm] * (len(args) - placed - near),
            out_specs=(vmem,) * len(outs),
            scratch_shapes=[pltpu.VMEM(shape, dtype) for shape, dtype in scratch]
            + [pltpu.SemaphoreType.DMA((sems,))] * bool(sems),
            compiler_params=pltpu.CompilerParams(vmem_limit_bytes=VMEM_LIMIT),
            cost_estimate=pl.CostEstimate(flops=flops, bytes_accessed=moved, transcendentals=0),
            name=name,
        )(*args[: placed + near], *(away(a) for a in args[placed + near :]))

    def exchange(blocks, axis, groups=None):
        return lax.all_to_all(blocks, axis, 0, 0, axis_index_groups=groups, tiled=True)

    inputs = (pair, gain, bias_weight_t, proj_weight, gate_shift[None])
    normed, bias_copies, near_proj, near_shift = call(
        norm_kernel,
        "norm",
        inputs,
        [
            (rows_shape, BF16),
            ((devices, shared, width), BF16),
            *((a.shape, a.dtype) for a in inputs[3:]),
        ],
        [
            (rows_shape, BF16),
            line,
            (bias_weight_t.shape, BF16),
            ((row_count * row_count, width), F32),
        ],
        sems=len(inputs),
    )
    bias_all = exchange(bias_copies, "dap")
    place = jnp.stack([lengths[0], lax.axis_index("dap") * row_count]).astype(jnp.int32)
    narrow, wide = call(
        functools.partial(project_kernel, heads),
        "project",
        (place, normed, near_proj, near_shift, cot, out_weight),
        [
            ((row_count, 5 * width + 2 * channels + 4 * channels // row_count, width), BF16),
            ((row_count, 2 * width, channels), F32),
        ],
        [(rows_shape, BF16), (out_weight.shape, BF16)],
        placed=True,
        near=3,
        sems=2,
        flops=3 * 10**9,
        moved=10**7,
    )
    parts, mixed, normed_proj, shift = call(
        attend_kernel,
        "attend",
        (place, bias_all, normed, narrow, wide),
        [
            ((devices, shared + 5 * row_count, width), BF16),
            (rows_shape, BF16),
            (rows_shape, F32),
            line,
        ],
        [
            ((heads * width, width), F32),
            ((heads * width, width), F32),
            ((devices, shared + 5 * row_count, width), F32),
            ((row_count, width, 4 * channels), BF16),
            ((4 * channels, channels), BF16),
        ],
        placed=True,
        near=4,
    )
    parts = exchange(parts, "dap")
    bias_grad, own = call(
        bias_kernel,
        "bias_grad",
        (parts, normed, shift, mixed, normed_proj),
        [((shared, width), BF16), ((chunk, channels), BF16)],
        [((chunk + 8, channels), F32)],
        near=5,
    )
    near = 4
    runs = [list(range(n, n + near)) for n in range(0, samples, near)]
    across = [list(range(n, samples, near)) for n in range(near)]
    gathered = lax.all_gather(own, "dp", axis=0, axis_index_groups=runs)
    bias_grad, gathered = lax.optimization_barrier((bias_grad, gathered))
    (sums,) = call(
        pair_kernel,
        "pair",
        (gathered,),
        [((samples // near, chunk, channels), BF16)],
        near=1,
    )
    sums = exchange(sums, "dp", across)
    updated, pair_grad = call(
        finish_kernel,
        "finish",
        (place, bias_grad, mixed, normed_proj, pair, cot, gain, bias_weight_t, out_weight),
        [(rows_shape, BF16), (rows_shape, BF16)],
        [
            (rows_shape, BF16),
            (rows_shape, BF16),
            line,
            (bias_weight_t.shape, BF16),
            (out_weight.shape, BF16),
            (rows_shape, BF16),
            (rows_shape, F32),
        ],
        placed=True,
        near=1,
        sems=7,
        flops=2 * 10**9,
        moved=6 * 10**6,
    )
    (blocks,) = call(
        sum_kernel, "sum", (sums,), [((devices, chunk, channels), BF16)], near=1
    )
    blocks = exchange(blocks, "dap")
    grad_proj, grad_shift, grad_out, grad_bias, grad_gain = call(
        functools.partial(assemble_kernel, 1.0 / width),
        "assemble",
        (blocks, proj_weight, bias_weight_t, gain),
        [
            ((channels, 4 * channels), F32),
            line,
            ((channels, channels), F32),
            ((heads, channels), F32),
            line,
        ],
        near=4,
    )
    return (
        updated[None],
        pair_grad[None],
        grad_proj,
        grad_shift[0],
        grad_out,
        grad_bias.T,
        grad_gain[0],
    )


def solution(mesh):
    rows = P("dp", "dap", None, None)
    return jax.shard_map(
        per_device,
        mesh=mesh,
        in_specs=(rows, P("dp"), rows, P(), P(), P(), P(), P()),
        out_specs=(rows, rows, P(), P(), P(), P(), P()),
        check_vma=False,
    )
```

```python
import functools

import jax
import jax.numpy as jnp
from jax import lax
from jax.experimental import pallas as pl
from jax.experimental.pallas import tpu as pltpu
from jax.sharding import PartitionSpec as P

EPS = 1e-05
DEAD = -1e30
F32 = jnp.float32
BF16 = jnp.bfloat16
VMEM_LIMIT = 16 * 1024 * 1024
UNROLL_PROJECT = 4
UNROLL_ATTEND = 8


def dot(a, b):
    return jnp.dot(a, b, preferred_element_type=F32)


def contract(a, b, a_axis, b_axis):
    return lax.dot_general(
        a, b, (((a_axis,), (b_axis,)), ((), ())), preferred_element_type=F32
    )


def standardize(rows):
    rows = rows.astype(F32)
    centered = rows - jnp.mean(rows, -1, keepdims=True)
    inv_std = lax.rsqrt(jnp.mean(centered * centered, -1, keepdims=True) + EPS)
    return centered * inv_std, inv_std


def head_masks(shape, axis, heads):
    size = shape[axis] // heads
    position = lax.broadcasted_iota(jnp.int32, shape, axis)
    return [(position >= h * size) & (position < (h + 1) * size) for h in range(heads)]


def stack_heads(block, masks):
    return jnp.concatenate([jnp.where(m, block, jnp.zeros_like(block)) for m in masks], 0)


def pick_heads(stacked, masks):
    size = stacked.shape[0] // len(masks)
    picked = stacked[:size]
    for h in range(1, len(masks)):
        picked = jnp.where(masks[h], stacked[h * size : (h + 1) * size], picked)
    return picked


def begin_all(sources, targets, sems):
    copies = [
        pltpu.make_async_copy(source, target, sems.at[n])
        for n, (source, target) in enumerate(zip(sources, targets, strict=True))
    ]
    for copy in copies:
        copy.start()
    return copies


def norm_kernel(
    pair_hbm,
    gain_hbm,
    bias_weight_hbm,
    proj_weight_hbm,
    gate_shift_hbm,
    normed_ref,
    bias_ref,
    proj_weight_ref,
    gate_shift_ref,
    pair,
    gain,
    bias_weight,
    held,
    sems,
):
    row_count = pair.shape[0]
    heads = bias_weight.shape[0]
    copies = begin_all(
        (gain_hbm, bias_weight_hbm, pair_hbm, proj_weight_hbm, gate_shift_hbm),
        (gain, bias_weight, pair, proj_weight_ref, gate_shift_ref),
        sems,
    )
    for copy in copies[:3]:
        copy.wait()
    for row in range(row_count):
        x_hat, _ = standardize(pair[row])
        normed = (x_hat * gain[...]).astype(BF16)
        normed_ref[row] = normed
        held[pl.ds(row, heads, stride=row_count), :] = contract(bias_weight[...], normed, 1, 1)
    block = held[: heads * row_count].astype(BF16)
    for peer in range(bias_ref.shape[0]):
        bias_ref[peer] = block
    for copy in copies[3:]:
        copy.wait()


def project_kernel(
    heads,
    place_ref,
    normed_ref,
    proj_weight_ref,
    gate_shift_ref,
    cot_hbm,
    out_weight_hbm,
    narrow_ref,
    cot,
    out_weight,
    gating,
    sems,
):
    row_count, width, channels = cot.shape
    scaling = (channels // heads) ** (-0.5)
    copies = begin_all((cot_hbm, out_weight_hbm), (cot, out_weight), sems)
    length, first_row = place_ref[0], place_ref[1]
    weight_t = proj_weight_ref[...].T
    weight_t = weight_t[channels : 3 * channels]
    token = lax.broadcasted_iota(jnp.int32, (width, channels), 0)

    def place(row, n, block):
        narrow_ref[row, n * width : (n + 1) * width] = block.astype(BF16)

    def forward(row, carry):
        normed = normed_ref[row]
        projected = dot(normed, proj_weight_ref[...])
        place(row, 0, projected[:, :channels] * scaling)
        place(row, 3, projected[:, channels : 2 * channels])
        place(row, 4, projected[:, 2 * channels : 3 * channels])
        gate = jax.nn.sigmoid(projected[:, 3 * channels :] + gate_shift_ref[...])
        gating[row] = gate
        place(row, 6, gate)
        place(row, 7, normed)
        narrow_ref[row, 8 * width :] = contract(
            weight_t, normed, 1, 1
        ).astype(BF16)
        return carry

    def backward(row, carry):
        live = token < jnp.where(first_row + row < length, length, 0)
        d_output = jnp.where(live, cot[row].astype(F32), 0.0).astype(BF16)
        d_mixed = contract(d_output, out_weight[...], 1, 1)
        place(row, 1, d_mixed * gating[row])
        place(row, 2, d_output)
        place(row, 5, d_mixed)
        return carry

    lax.fori_loop(0, row_count, forward, 0, unroll=UNROLL_PROJECT)
    for copy in copies:
        copy.wait()
    lax.fori_loop(0, row_count, backward, 0, unroll=UNROLL_PROJECT)


def attend_kernel(
    place_ref,
    bias_ref,
    narrow_ref,
    parts_ref,
    mixed_ref,
    d_proj_ref,
    shift_ref,
    bias_t,
    bias_sum,
    parts,
):
    row_count, width, channels = mixed_ref.shape
    heads = bias_t.shape[0] // width
    head_size = channels // heads
    scaling = head_size ** (-0.5)
    length = place_ref[0]
    devices = bias_ref.shape[0]
    key_live = lax.broadcasted_iota(jnp.int32, (width, width), 0) < length
    for h in range(heads):
        rows = [
            bias_ref[d].astype(F32)[h * row_count : (h + 1) * row_count]
            for d in range(devices)
        ]
        turned = jnp.concatenate(rows, 0).T
        bias_t[h * width : (h + 1) * width] = jnp.where(key_live, turned, DEAD)
    bias_sum[...] = jnp.zeros_like(bias_sum)
    lane_masks = head_masks((width, channels), 1, heads)

    def one_row(row, shift_sum):
        weights, lows, attended_t, d_query_t = [], [], [], []
        queries, d_attend, _, keys, values = (
            narrow_ref[row, n * width : (n + 1) * width] for n in range(5)
        )
        turned = narrow_ref.at[row, 8 * width :]
        scores = contract(stack_heads(keys, lane_masks), queries, 1, 1)
        grads = contract(stack_heads(values, lane_masks), d_attend, 1, 1)
        for h in range(heads):
            part = slice(h * width, (h + 1) * width)
            own = slice(h * head_size, (h + 1) * head_size)
            expo = jnp.exp(scores[part] + bias_t[part])
            probs = expo * (1.0 / jnp.sum(expo, 0, keepdims=True))
            weight = probs.astype(BF16)
            g = grads[part]
            d_scores = probs * (g - jnp.sum(probs * g, 0, keepdims=True))
            bias_sum[part] += d_scores
            low = d_scores.astype(BF16)
            weights.append(weight)
            lows.append(low)
            attended_t.append(dot(turned[channels + own.start : channels + own.stop], weight))
            d_query_t.append(dot(turned[own], low))
        attended = jnp.concatenate(attended_t, 0).T.astype(BF16).astype(F32)
        d_query = jnp.concatenate(d_query_t, 0).T
        d_value = pick_heads(dot(jnp.concatenate(weights, 0), d_attend), lane_masks)
        d_key = pick_heads(dot(jnp.concatenate(lows, 0), queries), lane_masks)
        gating = narrow_ref[row, 6 * width : 7 * width].astype(F32)
        mixed = gating * attended
        mixed_ref[row] = mixed.astype(BF16)
        d_gating = (narrow_ref[row, 5 * width : 6 * width].astype(F32) * mixed * (1.0 - gating)).astype(BF16)
        d_row = jnp.concatenate(
            [
                (d_query * scaling).astype(BF16),
                d_key.astype(BF16),
                d_value.astype(BF16),
                d_gating,
            ],
            1,
        )
        d_proj_ref[row] = d_row
        return shift_sum + jnp.sum(d_gating.astype(F32), 0, keepdims=True)

    zero = jnp.zeros((1, channels), F32)
    shift_ref[...] = lax.fori_loop(0, row_count, one_row, zero, unroll=UNROLL_ATTEND)
    flat = d_proj_ref[...].reshape(row_count * width, 4 * channels)
    shared = heads * row_count
    for h in range(heads):
        turned = bias_sum[h * width : (h + 1) * width].T
        for d in range(devices):
            parts[d, h * row_count : (h + 1) * row_count] = turned[
                d * row_count : (d + 1) * row_count
            ]
    tokens = row_count * width
    normed = narrow_ref[:, 7 * width : 8 * width].reshape(tokens, channels)
    grad_proj = contract(normed, flat, 0, 0)
    grad_out = contract(
        mixed_ref[...].reshape(tokens, channels),
        narrow_ref[:, 2 * width : 3 * width].reshape(tokens, channels),
        0,
        0,
    )
    pieces = [grad_proj[:, i * channels : (i + 1) * channels] for i in range(4)] + [grad_out]
    for d in range(devices):
        for i, piece in enumerate(pieces):
            start = shared + i * row_count
            parts[d, start : start + row_count] = piece[d * row_count : (d + 1) * row_count]
    parts_ref[...] = parts[...].astype(BF16)


def bias_kernel(
    parts_ref, normed_ref, shift_ref, mixed_ref, d_proj_ref, bias_grad_ref, own_ref, held
):
    del mixed_ref, d_proj_ref
    row_count, width, channels = normed_ref.shape
    shared = bias_grad_ref.shape[0]
    heads = shared // row_count
    total = parts_ref[0].astype(F32)
    for d in range(1, parts_ref.shape[0]):
        total = total + parts_ref[d].astype(F32)
    bias_grad = total[:shared].astype(BF16)
    bias_grad_ref[...] = bias_grad
    bias_grad = bias_grad.astype(F32)
    of_row = lax.broadcasted_iota(jnp.int32, bias_grad.shape, 0) % row_count
    grad_bias = jnp.zeros((shared, channels), F32)
    for row in range(row_count):
        own = jnp.where(of_row == row, bias_grad, 0.0).astype(BF16)
        grad_bias = grad_bias + dot(own, normed_ref[row])
    grads = 5 * row_count
    held[:grads] = total[shared : shared + grads]
    held[grads:] = jnp.zeros((held.shape[0] - grads, channels), F32)
    for h in range(heads):
        held[grads + h : grads + h + 1] = jnp.sum(
            grad_bias[h * row_count : (h + 1) * row_count], 0, keepdims=True
        )
    held[grads + heads : grads + heads + 1] = shift_ref[...]
    own_ref[...] = held[: own_ref.shape[0]].astype(BF16)


def pair_kernel(near_ref, sums_ref):
    block = near_ref[0].astype(F32)
    for n in range(1, near_ref.shape[0]):
        block = block + near_ref[n].astype(F32)
    block = block.astype(BF16)
    for peer in range(sums_ref.shape[0]):
        sums_ref[peer] = block


def finish_kernel(
    place_ref,
    bias_grad_ref,
    mixed_hbm,
    d_proj_hbm,
    proj_weight_hbm,
    pair_hbm,
    cot_hbm,
    gain_hbm,
    bias_weight_hbm,
    out_weight_hbm,
    updated_ref,
    pair_grad_ref,
    pair_ref,
    cot_ref,
    gain_ref,
    bias_weight_ref,
    out_weight_ref,
    mixed_ref,
    d_proj_ref,
    proj_weight_ref,
    normed_proj_ref,
    sems,
):
    copies = begin_all(
        (
            pair_hbm,
            cot_hbm,
            gain_hbm,
            bias_weight_hbm,
            out_weight_hbm,
            mixed_hbm,
            d_proj_hbm,
            proj_weight_hbm,
        ),
        (
            pair_ref,
            cot_ref,
            gain_ref,
            bias_weight_ref,
            out_weight_ref,
            mixed_ref,
            d_proj_ref,
            proj_weight_ref,
        ),
        sems,
    )
    row_count, width, channels = pair_ref.shape
    heads = bias_weight_ref.shape[0]
    length, first_row = place_ref[0], place_ref[1]
    token = lax.broadcasted_iota(jnp.int32, (width, channels), 0)
    bias_grad = bias_grad_ref[...].astype(F32)
    of_row = lax.broadcasted_iota(jnp.int32, bias_grad.shape, 0) % row_count
    for copy in copies:
        copy.wait()
    flat = d_proj_ref[...].reshape(row_count * width, 4 * channels)
    normed_proj_ref[...] = contract(flat, proj_weight_ref[...], 1, 1).reshape(
        normed_proj_ref.shape
    )
    weight = bias_weight_ref[...].astype(F32)
    spread = jnp.concatenate(
        [jnp.broadcast_to(weight[h : h + 1], (row_count, channels)) for h in range(heads)], 0
    ).astype(BF16)
    for row in range(row_count):
        live = token < jnp.where(first_row + row < length, length, 0)
        output = dot(mixed_ref[row], out_weight_ref[...])
        updated_ref[row] = (
            pair_ref[row].astype(F32) + jnp.where(live, output, 0.0)
        ).astype(BF16)
        own = jnp.where(of_row == row, bias_grad, 0.0)
        added = dot(own.T.astype(BF16), spread)
        x_hat, inv_std = standardize(pair_ref[row])
        d_x_hat = (normed_proj_ref[row] + added) * gain_ref[...]
        d_pair = inv_std * (
            d_x_hat
            - jnp.mean(d_x_hat, -1, keepdims=True)
            - x_hat * jnp.mean(d_x_hat * x_hat, -1, keepdims=True)
        )
        pair_grad_ref[row] = (cot_ref[row].astype(F32) + d_pair).astype(BF16)


def sum_kernel(sums_ref, out_ref):
    total = sums_ref[0].astype(F32)
    for d in range(1, sums_ref.shape[0]):
        total = total + sums_ref[d].astype(F32)
    block = total.astype(BF16)
    for peer in range(out_ref.shape[0]):
        out_ref[peer] = block


def assemble_kernel(
    scale,
    blocks_ref,
    proj_weight_ref,
    bias_weight_ref,
    gain_ref,
    grad_proj_ref,
    grad_shift_ref,
    grad_out_ref,
    grad_bias_ref,
    grad_gain_ref,
):
    devices = blocks_ref.shape[0]
    channels = grad_out_ref.shape[0]
    heads = grad_bias_ref.shape[0]
    row_count = channels // devices
    grads = 5 * row_count
    small = None
    by_channel = []
    for d in range(devices):
        block = blocks_ref[d].astype(F32) * scale
        own = slice(d * row_count, (d + 1) * row_count)
        by_lane = None
        for i in range(4):
            columns = slice(i * channels, (i + 1) * channels)
            piece = block[i * row_count : (i + 1) * row_count]
            grad_proj_ref[own, columns] = piece
            term = piece * proj_weight_ref[own, columns].astype(F32)
            by_lane = term if by_lane is None else by_lane + term
        by_channel.append(by_lane)
        grad_out_ref[own] = block[4 * row_count : grads]
        small = block[grads:] if small is None else small + block[grads:]
    grad_bias_ref[...] = small[:heads]
    grad_shift_ref[...] = small[heads : heads + 1]
    gain_sum = jnp.sum(jnp.concatenate(by_channel, 0).T, 0, keepdims=True)
    gain_sum = gain_sum + jnp.sum(
        small[:heads] * bias_weight_ref[...].astype(F32), 0, keepdims=True
    )
    grad_gain_ref[...] = gain_sum / gain_ref[...]


def per_device(
    pair_act, lengths, cotangent, proj_weight, gate_shift, out_weight, bias_weight, norm_gain
):
    pair, cot = pair_act[0], cotangent[0]
    row_count, width, channels = pair.shape
    heads = bias_weight.shape[1]
    gain, bias_weight_t = norm_gain[None], bias_weight.T
    devices, samples = lax.axis_size("dap"), lax.axis_size("dp")
    shared = heads * row_count
    chunk = -(-(5 * row_count + heads + 1) // 16) * 16
    vmem = pl.BlockSpec(memory_space=pltpu.VMEM)
    smem = pl.BlockSpec(memory_space=pltpu.SMEM)
    hbm = pl.BlockSpec(memory_space=pltpu.MemorySpace.HBM)
    rows_shape = (row_count, width, channels)
    line = ((1, channels), F32)

    def away(array):
        return pltpu.with_memory_space_constraint(array, pltpu.MemorySpace.HBM)

    def call(kernel, name, args, outs, scratch=(), placed=False, near=0, sems=0, flops=0, moved=0):
        return pl.pallas_call(
            kernel,
            out_shape=tuple(jax.ShapeDtypeStruct(shape, dtype) for shape, dtype in outs),
            in_specs=[smem] * placed + [vmem] * near + [hbm] * (len(args) - placed - near),
            out_specs=(vmem,) * len(outs),
            scratch_shapes=[pltpu.VMEM(shape, dtype) for shape, dtype in scratch]
            + [pltpu.SemaphoreType.DMA((sems,))] * bool(sems),
            compiler_params=pltpu.CompilerParams(vmem_limit_bytes=VMEM_LIMIT),
            cost_estimate=pl.CostEstimate(flops=flops, bytes_accessed=moved, transcendentals=0),
            name=name,
        )(*args[: placed + near], *(away(a) for a in args[placed + near :]))

    def exchange(blocks, axis, groups=None):
        return lax.all_to_all(blocks, axis, 0, 0, axis_index_groups=groups, tiled=True)

    inputs = (pair, gain, bias_weight_t, proj_weight, gate_shift[None])
    normed, bias_copies, near_proj, near_shift = call(
        norm_kernel,
        "norm",
        inputs,
        [
            (rows_shape, BF16),
            ((devices, shared, width), BF16),
            *((a.shape, a.dtype) for a in inputs[3:]),
        ],
        [
            (rows_shape, BF16),
            line,
            (bias_weight_t.shape, BF16),
            ((row_count * row_count, width), F32),
        ],
        sems=len(inputs),
    )
    bias_all = exchange(bias_copies, "dap")
    place = jnp.stack([lengths[0], lax.axis_index("dap") * row_count]).astype(jnp.int32)
    (narrow,) = call(
        functools.partial(project_kernel, heads),
        "project",
        (place, normed, near_proj, near_shift, cot, out_weight),
        [
            ((row_count, 8 * width + 2 * channels, width), BF16),
        ],
        [(rows_shape, BF16), (out_weight.shape, BF16), (rows_shape, F32)],
        placed=True,
        near=3,
        sems=2,
        flops=3 * 10**9,
        moved=10**7,
    )
    parts, mixed, d_proj, shift = call(
        attend_kernel,
        "attend",
        (place, bias_all, narrow),
        [
            ((devices, shared + 5 * row_count, width), BF16),
            (rows_shape, BF16),
            ((row_count, width, 4 * channels), BF16),
            line,
        ],
        [
            ((heads * width, width), F32),
            ((heads * width, width), F32),
            ((devices, shared + 5 * row_count, width), F32),
        ],
        placed=True,
        near=2,
    )
    parts = exchange(parts, "dap")
    bias_grad, own = call(
        bias_kernel,
        "bias_grad",
        (parts, normed, shift, mixed, d_proj),
        [((shared, width), BF16), ((chunk, channels), BF16)],
        [((chunk + 8, channels), F32)],
        near=5,
    )
    near = 4
    runs = [list(range(n, n + near)) for n in range(0, samples, near)]
    across = [list(range(n, samples, near)) for n in range(near)]
    gathered = lax.all_gather(own, "dp", axis=0, axis_index_groups=runs)
    bias_grad, gathered = lax.optimization_barrier((bias_grad, gathered))
    (sums,) = call(
        pair_kernel,
        "pair",
        (gathered,),
        [((samples // near, chunk, channels), BF16)],
        near=1,
    )
    sums = exchange(sums, "dp", across)
    updated, pair_grad = call(
        finish_kernel,
        "finish",
        (
            place,
            bias_grad,
            mixed,
            d_proj,
            proj_weight,
            pair,
            cot,
            gain,
            bias_weight_t,
            out_weight,
        ),
        [(rows_shape, BF16), (rows_shape, BF16)],
        [
            (rows_shape, BF16),
            (rows_shape, BF16),
            line,
            (bias_weight_t.shape, BF16),
            (out_weight.shape, BF16),
            (rows_shape, BF16),
            ((row_count, width, 4 * channels), BF16),
            (proj_weight.shape, BF16),
            (rows_shape, F32),
        ],
        placed=True,
        near=1,
        sems=8,
        flops=2 * 10**9,
        moved=6 * 10**6,
    )
    (blocks,) = call(
        sum_kernel, "sum", (sums,), [((devices, chunk, channels), BF16)], near=1
    )
    blocks = exchange(blocks, "dap")
    grad_proj, grad_shift, grad_out, grad_bias, grad_gain = call(
        functools.partial(assemble_kernel, 1.0 / width),
        "assemble",
        (blocks, proj_weight, bias_weight_t, gain),
        [
            ((channels, 4 * channels), F32),
            line,
            ((channels, channels), F32),
            ((heads, channels), F32),
            line,
        ],
        near=4,
    )
    return (
        updated[None],
        pair_grad[None],
        grad_proj,
        grad_shift[0],
        grad_out,
        grad_bias.T,
        grad_gain[0],
    )


def solution(mesh):
    rows = P("dp", "dap", None, None)
    return jax.shard_map(
        per_device,
        mesh=mesh,
        in_specs=(rows, P("dp"), rows, P(), P(), P(), P(), P()),
        out_specs=(rows, rows, P(), P(), P(), P(), P()),
        check_vma=False,
    )
```
